512 devices in a mesh: patch: 128 (over z, x, y_lo), slab: 4 (over y_hi, core).
Axes of the slice: x: 4, y: 8 (y_hi: 2, y_lo: 4; y = y_hi * 4 + y_lo), z: 8, core: 2. Of those that a mesh axis runs over, the one named last changes fastest.
Arguments:
- load_vector: float32 [128, 64, 16384], P('patch', 'slab'), may hold values from -6 to 6
- reaction: float32 [128, 64, 16384], P('patch', 'slab'), may hold values from 0.1 to 1
- geometry: float32 [128, 3], P('patch'), may hold values from 0.25 to 64, as said below
- stiff_plane: float32 [128, 128], replicated, as said below
- mass_plane: float32 [128, 128], replicated, as said below
- stiff_vertical: float32 [64, 64], replicated, as said below
- mass_vertical: float32 [64, 64], replicated, as said below
- basis_plane: float32 [128, 128], replicated, as said below
- eigen_plane: float32 [128], replicated, as said below
- basis_vertical: float32 [64, 64], replicated, as said below
- eigen_vertical: float32 [64], replicated, as said below
- restrict_plane: float32 [126, 128], replicated, as said below
- restrict_vertical: float32 [62, 64], replicated, as said below
- patch_links: int32 [128, 3], P('patch'), may hold values from 0 to 3, as said below
Outputs:
- iterate: float32 [128, 64, 16384], P('patch', 'slab')
- coarse_residual: float32 [128, 62, 15876], P('patch', None, 'slab')
The draws below stay inside these ranges and needn't reach their ends.
Inputs may be any that keep to these rules, and one draw needn't show every extreme that they name: `geometry`: positive scale factors. `patch_links`: column 0 holds a face of 0 to 3, column 1 the opposite face (0 with 1, 2 with 3), column 2 is 0 or 1. `stiff_plane`: Symmetric, zero beyond 4 places from the diagonal, positive definite. `mass_plane`: Symmetric, zero beyond 4 places from the diagonal, positive definite. `stiff_vertical`: Symmetric, zero beyond 4 places from the diagonal, positive definite. `mass_vertical`: Symmetric, zero beyond 4 places from the diagonal, positive definite. `basis_plane`: columns are eigenvectors of stiff_plane against mass_plane with unit mass norm. `eigen_plane`: positive eigenvalues matching basis_plane. `basis_vertical`: columns are eigenvectors of stiff_vertical against mass_vertical with unit mass norm. `eigen_vertical`: positive eigenvalues matching basis_vertical. `restrict_plane`: row c is nonzero at most for fine indices c - 1 to c + 3; fine index 0 feeds only row 0 and the last fine index only the last row. `restrict_vertical`: row m is nonzero at most for fine indices m - 1 to m + 3; fine index 0 feeds only row 0 and the last fine index only the last row.
All inputs are finite; a program needn't handle non-finite values.
Results may differ from the reference program's by a relative error of at most 0.0003.
Values sent between devices are 32-bit elements; how exact they have to be, the bound alone decides.
No kernel may reach another device: no remote copies, remote signals or barrier semaphores. Data moves between devices by JAX's collectives and lax.ppermute only.
A program may use at most 64 MiB of HBM per device.

```python
import math
import jax
import jax.numpy as jnp
from jax import lax

NP = 128
NZ = 64
SWEEPS = 3
PATCHES = 128


HIGHEST = lax.Precision.HIGHEST


def family_coefficients(key):
    key_m0, key_m1, key_m2, key_s1, key_s2, key_s4 = jax.random.split(key, 6)
    mass_zero = jax.random.uniform(key_m0, (), jnp.float32, 2.0, 3.0)
    mass_one = jax.random.uniform(key_m1, (), jnp.float32, 0.2, 0.4)
    mass_two = jax.random.uniform(key_m2, (), jnp.float32, 0.02, 0.05)
    stiff_one = jax.random.uniform(key_s1, (), jnp.float32, 1.0, 2.0)
    stiff_two = jax.random.uniform(key_s2, (), jnp.float32, 0.05, 0.2)
    stiff_four = jax.random.uniform(key_s4, (), jnp.float32, 0.001, 0.004)
    return (mass_zero, mass_one, mass_two, stiff_one, stiff_two, stiff_four)


def band_pair(key, matrix_order):
    mass_zero, mass_one, mass_two, stiff_one, stiff_two, stiff_four = family_coefficients(key)
    row_ids = jnp.arange(matrix_order)[:, None]
    col_ids = jnp.arange(matrix_order)[None, :]
    identity = (row_ids == col_ids).astype(jnp.float32)
    second_diff = 2.0 * identity - (jnp.abs(row_ids - col_ids) == 1).astype(jnp.float32)
    diff_two = jnp.dot(second_diff, second_diff, precision=HIGHEST)
    diff_four = jnp.dot(diff_two, diff_two, precision=HIGHEST)
    mass_matrix = mass_zero * identity - mass_one * second_diff + mass_two * diff_two
    stiffness = stiff_one * second_diff + stiff_two * diff_two + stiff_four * diff_four
    return (stiffness, mass_matrix)


def eigen_pair(key, matrix_order):
    mass_zero, mass_one, mass_two, stiff_one, stiff_two, stiff_four = family_coefficients(key)
    modes = jnp.arange(1, matrix_order + 1).astype(jnp.float32)
    points = jnp.arange(1, matrix_order + 1).astype(jnp.float32)
    theta = 2.0 - 2.0 * jnp.cos(jnp.pi * modes / (matrix_order + 1))
    mass_values = mass_zero - mass_one * theta + mass_two * theta * theta
    stiff_values = stiff_one * theta + stiff_two * theta * theta + stiff_four * theta ** 4
    sine_table = jnp.sqrt(2.0 / (matrix_order + 1)) * jnp.sin(jnp.pi * points[:, None] * modes[None, :] / (matrix_order + 1))
    basis_matrix = sine_table / jnp.sqrt(mass_values)[None, :]
    return (stiff_values / mass_values, basis_matrix)


def band_restriction(key, coarse_count, fine_count):
    row_ids = jnp.arange(coarse_count)[:, None]
    col_ids = jnp.arange(fine_count)[None, :]
    inside = (col_ids >= row_ids - 1) & (col_ids <= row_ids + 3)
    inside = inside & jnp.logical_not((col_ids == 0) & (row_ids > 0))
    inside = inside & jnp.logical_not((col_ids == fine_count - 1) & (row_ids < coarse_count - 1))
    weights = jax.random.uniform(key, (coarse_count, fine_count), jnp.float32, 0.05, 0.35)
    return jnp.where(inside, weights, 0.0)


def draw_geometry(key, part):
    key = jax.random.fold_in(key, 41)
    exponent = jax.random.uniform(key, (PATCHES, 3), jnp.float32, math.log(0.5), math.log(2.0))
    return jnp.exp(exponent)


def draw_stiff_plane(key, part):
    return band_pair(jax.random.fold_in(key, 101), NP)[0]


def draw_mass_plane(key, part):
    return band_pair(jax.random.fold_in(key, 101), NP)[1]


def draw_stiff_vertical(key, part):
    return band_pair(jax.random.fold_in(key, 202), NZ)[0]


def draw_mass_vertical(key, part):
    return band_pair(jax.random.fold_in(key, 202), NZ)[1]


def draw_basis_plane(key, part):
    return eigen_pair(jax.random.fold_in(key, 101), NP)[1]


def draw_eigen_plane(key, part):
    return eigen_pair(jax.random.fold_in(key, 101), NP)[0]


def draw_basis_vertical(key, part):
    return eigen_pair(jax.random.fold_in(key, 202), NZ)[1]


def draw_eigen_vertical(key, part):
    return eigen_pair(jax.random.fold_in(key, 202), NZ)[0]


def draw_restrict_plane(key, part):
    key = jax.random.fold_in(key, 21)
    return band_restriction(key, NP - 2, NP)


def draw_restrict_vertical(key, part):
    key = jax.random.fold_in(key, 22)
    return band_restriction(key, NZ - 2, NZ)


def draw_patch_links(key, part):
    key = jax.random.fold_in(key, 31)
    key_west, key_flip = jax.random.split(key)
    west_faces = jax.random.randint(key_west, (PATCHES,), 0, 4)
    east_faces = west_faces + 1 - 2 * (west_faces % 2)
    flip_bits = jax.random.randint(key_flip, (PATCHES,), 0, 2)
    return jnp.stack([west_faces, east_faces, flip_bits], axis=1).astype(jnp.int32)


def shard_levels(own_key, dims, cuts, least, largest):
    def one(dim, shards_of):
        draws = jax.random.uniform(jax.random.fold_in(jax.random.fold_in(own_key, 6), dim), (shards_of,), jnp.float32, least / len(cuts), largest / len(cuts))
        return jnp.repeat(jnp.exp(draws), dims[dim] // shards_of).reshape((-1,) + (1,) * (len(dims) - dim - 1))

    loudness = one(*cuts[0])
    for cut in cuts[1:]:
        loudness = loudness * one(*cut)
    return loudness


def bell_draw(stream_key, shape, width, limit, cuts=(), kind=jnp.bfloat16):
    entries = width * jax.random.normal(stream_key, shape, jnp.float32)
    if cuts:
        entries = entries * shard_levels(stream_key, shape, cuts, -0.22, 0.18)
    return jnp.clip(entries, -limit, limit).astype(kind)


def setup_inputs(seed: int = 0) -> dict:
    arg_keys = jax.random.split(jax.random.key(seed), 15)
    load_vector = bell_draw(arg_keys[0], (PATCHES, NZ, NP * NP), 1.0, 6.0, ((0, 128), (1, 4)), jnp.float32)
    reaction = jnp.clip(jnp.exp(math.log(1.0) - 2.3025851 * jax.random.uniform(arg_keys[1], (PATCHES, NZ, NP * NP), jnp.float32) ** shard_levels(arg_keys[1], (PATCHES, NZ, NP * NP), ((0, 128), (1, 4)), -0.2, 0.2)), 0.1, 1.0)
    geometry = draw_geometry(jax.random.fold_in(arg_keys[14], 71), 0)
    stiff_plane = draw_stiff_plane(jax.random.fold_in(arg_keys[14], 71), 0)
    mass_plane = draw_mass_plane(jax.random.fold_in(arg_keys[14], 71), 0)
    stiff_vertical = draw_stiff_vertical(jax.random.fold_in(arg_keys[14], 71), 0)
    mass_vertical = draw_mass_vertical(jax.random.fold_in(arg_keys[14], 71), 0)
    basis_plane = draw_basis_plane(jax.random.fold_in(arg_keys[14], 71), 0)
    eigen_plane = draw_eigen_plane(jax.random.fold_in(arg_keys[14], 71), 0)
    basis_vertical = draw_basis_vertical(jax.random.fold_in(arg_keys[14], 71), 0)
    eigen_vertical = draw_eigen_vertical(jax.random.fold_in(arg_keys[14], 71), 0)
    restrict_plane = draw_restrict_plane(jax.random.fold_in(arg_keys[14], 71), 0)
    restrict_vertical = draw_restrict_vertical(jax.random.fold_in(arg_keys[14], 71), 0)
    patch_links = draw_patch_links(jax.random.fold_in(arg_keys[14], 71), 0)
    return dict(load_vector=load_vector, reaction=reaction, geometry=geometry, stiff_plane=stiff_plane, mass_plane=mass_plane, stiff_vertical=stiff_vertical, mass_vertical=mass_vertical, basis_plane=basis_plane, eigen_plane=eigen_plane, basis_vertical=basis_vertical, eigen_vertical=eigen_vertical, restrict_plane=restrict_plane, restrict_vertical=restrict_vertical, patch_links=patch_links)


DAMPING = 0.25
HIGHEST = lax.Precision.HIGHEST


def face_values(volume, face_id, flip_bit):
    length = volume.shape[1]
    position = jnp.where(face_id % 2 == 0, 0, length - 1).astype(jnp.int32)
    on_rows = lax.dynamic_index_in_dim(volume, position, axis=1, keepdims=False)
    on_cols = lax.dynamic_index_in_dim(volume, position, axis=2, keepdims=False)
    values = jnp.where(face_id < 2, on_rows, on_cols)
    return jnp.where(flip_bit == 1, values[:, ::-1], values)


def add_face(volume, face_id, flip_bit, values):
    length = volume.shape[1]
    oriented = jnp.where(flip_bit == 1, values[:, ::-1], values)
    position = jnp.where(face_id % 2 == 0, 0, length - 1).astype(jnp.int32)
    marker = (jnp.arange(length, dtype=jnp.int32) == position).astype(volume.dtype)
    row_update = marker[None, :, None] * oriented[:, None, :]
    col_update = marker[None, None, :] * oriented[:, :, None]
    return volume + jnp.where(face_id < 2, row_update, col_update)


def assemble(fields, links):
    west_face = jax.vmap(face_values)(fields, links[:, 0], links[:, 2])
    east_face = jax.vmap(face_values)(fields, links[:, 1], links[:, 2])
    from_left = jnp.roll(east_face, 1, axis=0)
    from_right = jnp.roll(west_face, -1, axis=0)

    def update(inputs):
        volume, west_id, east_id, flip_bit, left_vals, right_vals = inputs
        volume = add_face(volume, west_id, flip_bit, left_vals)
        return add_face(volume, east_id, flip_bit, right_vals)

    return lax.map(update, (fields, links[:, 0], links[:, 1], links[:, 2], from_left, from_right))


def apply_operator(volume, react_field, scales, stiff_plane, mass_plane, stiff_vertical, mass_vertical):
    along_mass = jnp.einsum('kl,lij->kij', mass_vertical, volume, precision=HIGHEST)
    along_stiff = jnp.einsum('kl,lij->kij', stiff_vertical, volume, precision=HIGHEST)
    mass_mass = jnp.einsum('kij,bj->kib', along_mass, mass_plane, precision=HIGHEST)
    mass_stiff = jnp.einsum('kij,bj->kib', along_mass, stiff_plane, precision=HIGHEST)
    stiff_mass = jnp.einsum('kij,bj->kib', along_stiff, mass_plane, precision=HIGHEST)
    inner_sum = scales[1] * mass_stiff + scales[2] * stiff_mass
    result = scales[0] * jnp.einsum('ai,kib->kab', stiff_plane, mass_mass, precision=HIGHEST)
    result = result + jnp.einsum('ai,kib->kab', mass_plane, inner_sum, precision=HIGHEST)
    return result + react_field * volume


def smooth(residual, scales, basis_plane, eigen_plane, basis_vertical, eigen_vertical):
    first_pass = jnp.einsum('kij,jb->kib', residual, basis_plane, precision=HIGHEST)
    second = jnp.einsum('ia,kib->kab', basis_plane, first_pass, precision=HIGHEST)
    mixed_rows = jnp.einsum('kc,kab->cab', basis_vertical, second, precision=HIGHEST)
    denominator = (scales[0] * eigen_plane[None, :, None] + scales[1] * eigen_plane[None, None, :]
                   + scales[2] * eigen_vertical[:, None, None])
    scaled = mixed_rows / denominator
    back_rows = jnp.einsum('kc,cab->kab', basis_vertical, scaled, precision=HIGHEST)
    across = jnp.einsum('kab,jb->kaj', back_rows, basis_plane, precision=HIGHEST)
    return jnp.einsum('ia,kaj->kij', basis_plane, across, precision=HIGHEST)


def reference(load_vector, reaction, geometry, stiff_plane, mass_plane, stiff_vertical, mass_vertical,
              basis_plane, eigen_plane, basis_vertical, eigen_vertical, restrict_plane, restrict_vertical,
              patch_links):
    fine_load = load_vector.reshape(PATCHES, NZ, NP, NP)
    react_all = reaction.reshape(PATCHES, NZ, NP, NP)

    def operate(fields):
        return lax.map(lambda inputs: apply_operator(inputs[0], inputs[1], inputs[2], stiff_plane, mass_plane,
                                                     stiff_vertical, mass_vertical), (fields, react_all, geometry))

    def precondition(fields):
        return lax.map(lambda inputs: smooth(inputs[0], inputs[1], basis_plane, eigen_plane, basis_vertical,
                                             eigen_vertical), (fields, geometry))

    iterate = jnp.zeros((PATCHES, NZ, NP, NP), jnp.float32)
    for sweep_index in range(SWEEPS):
        residual = assemble(fine_load - operate(iterate), patch_links)
        iterate = iterate + DAMPING * assemble(precondition(residual), patch_links)
    final_local = fine_load - operate(iterate)

    def restrict(volume):
        halfway = jnp.einsum('ci,kij->kcj', restrict_plane, volume, precision=HIGHEST)
        return jnp.einsum('kcj,dj->kcd', halfway, restrict_plane, precision=HIGHEST)

    plane_coarse = assemble(lax.map(restrict, final_local), patch_links)
    coarse = lax.map(lambda volume: jnp.einsum('mk,kcd->mcd', restrict_vertical, volume, precision=HIGHEST),
                     plane_coarse)
    return iterate.reshape(PATCHES, NZ, NP * NP), coarse.reshape(PATCHES, NZ - 2, (NP - 2) * (NP - 2))
```

```python
import jax
import jax.numpy as jnp
from jax import lax
from jax.experimental import pallas as pl
from jax.experimental.pallas import tpu as pltpu
from jax.sharding import PartitionSpec as P

BAND = 4
SWEEPS = 3
DAMPING = 0.25
KEEP = 1.0 - DAMPING
HIGHEST = lax.Precision.HIGHEST
F32 = jnp.float32
BF16 = jnp.bfloat16

N = 128
LAYERS = 64
HALF = 32
BLOCK = 16
REACH = HALF + BAND
ROWS = 40
TOP = HALF - BAND
CHUNK = 32
COARSE = N - 2


def split(x):
    high = x.astype(BF16)
    return high, (x - high.astype(F32)).astype(BF16)


def right_mul(x, packed):
    high, low = split(x)
    both = jnp.dot(jnp.concatenate([high, low], axis=-1), packed, preferred_element_type=F32)
    return both[:, :N] + both[:, N:]


def left_mul_planes(packed, planes):
    out = []
    for q in range(0, len(planes), 2):
        high, low = split(jnp.concatenate(planes[q:q + 2], axis=1))
        wide = jnp.dot(packed, jnp.concatenate([high, high], axis=0), preferred_element_type=F32)
        wide = wide + jnp.dot(packed[:, :N], low, preferred_element_type=F32)
        out += [wide[:, :N], wide[:, N:]]
    return out


def dot_full(x, y):
    return jnp.dot(x, y, precision=HIGHEST, preferred_element_type=F32)


def pack_right(a):
    high, low = split(a)
    top = jnp.concatenate([high, low], axis=1)
    bottom = jnp.concatenate([high, jnp.zeros_like(low)], axis=1)
    return jnp.concatenate([top, bottom], axis=0)


def pack_left(a):
    return jnp.concatenate(split(a), axis=1)


def call(kernel, outs, ints, *args, flops=0, scratch=(), floats=None):
    smem = [ints] if floats is None else [ints, floats]
    specs = [pl.BlockSpec(memory_space=pltpu.SMEM)] * len(smem)
    specs += [pl.BlockSpec(memory_space=pltpu.VMEM)] * len(args)
    shapes = [s if isinstance(s, jax.ShapeDtypeStruct) else jax.ShapeDtypeStruct(s, F32) for s in outs]
    moved = sum(a.size * a.dtype.itemsize for a in args) + sum(4 * s.size for s in shapes)
    return pl.pallas_call(
        kernel,
        out_shape=shapes,
        in_specs=specs,
        out_specs=[pl.BlockSpec(memory_space=pltpu.VMEM)] * len(outs),
        scratch_shapes=list(scratch),
        compiler_params=pltpu.CompilerParams(vmem_limit_bytes=20 * 1024 * 1024),
        cost_estimate=pl.CostEstimate(
            flops=flops, bytes_accessed=moved, transcendentals=0
        ),
    )(*smem, *args)


def source_layer(ints, t):
    inside = jnp.where(ints[2] == 1, HALF - 1 - t, t)
    return inside // BLOCK, inside % BLOCK


def load_layer(ints, own_ref, other_ref, out_ref, t):
    block, index = source_layer(ints, t)
    mine = own_ref[index]
    theirs = other_ref[index]
    value = jnp.where(block == ints[3], mine, theirs)
    out_ref[t] = value

    @pl.when(ints[1] == 1)
    def _():
        out_ref[t] = value.T


def slots(ints, west, east, slot_refs):
    odd = ints[0] == 1
    slot_refs[0][...] = jnp.where(odd, east, west)
    slot_refs[1][...] = jnp.where(odd, west, east)


def sides(ints, received0, received1):
    odd = ints[0] == 1
    return jnp.where(odd, received1, received0), jnp.where(odd, received0, received1)


def face_rows(ints, ref, side):
    position = ints[4 + side]
    return jnp.where(position == 0, ref[:, 0, :], ref[:, N - 1, :])


def load_kernel(ints, own, other, scal, f_ref, pay_ref, slot0, slot1):
    def body(t, carry):
        load_layer(ints, own, other, f_ref, t)
        return carry

    lax.fori_loop(0, HALF, body, 0, unroll=4)
    packs = []
    for side in range(2):
        rows = face_rows(ints, f_ref, side)
        packs.append(
            jnp.concatenate([rows, jnp.zeros((ROWS - HALF, N), F32), scal[side]], axis=0)
        )
        pay_ref[side] = packs[side]
    slots(ints, packs[0], packs[1], (slot0, slot1))


def reaction_kernel(ints, own, other, r_ref, face_ref):
    def body(t, carry):
        load_layer(ints, own, other, r_ref, t)
        return carry

    lax.fori_loop(0, HALF, body, 0, unroll=4)
    for side in range(2):
        face_ref[side] = face_rows(ints, r_ref, side)


def forward_planes(x, wb, lbt):
    count = x.shape[0]
    first = right_mul(x.reshape(count * N, N), wb).reshape(count, N, N)
    return left_mul_planes(lbt, [first[q] for q in range(count)])


GROUP = 16


def transform_kernel(ints, f_ref, wb, lbt, out_ref):
    def body(g, carry):
        t = g * GROUP
        planes = forward_planes(f_ref[pl.ds(t, GROUP)], wb[...], lbt[...])
        for q in range(GROUP):
            out_ref[t + q] = planes[q]
        return carry

    lax.fori_loop(0, HALF // GROUP, body, 0)


FACTOR_ROWS = 16


def factor_kernel(
    ints, alpha_ref, bands, modes, l_ref, dinv_ref, lu_ref, lo_ref, do_ref, mend_ref, zs
):
    def coefficient(alpha, which, t, d):
        return alpha * bands[which, 0, d, t:t + 1, :] + bands[which, 1, d, t:t + 1, :]

    def mode(which, t):
        return modes[which, t:t + 1, :]

    def row_weights(a, l, t, least):
        w = {}
        for d in range(min(BAND, t), least - 1, -1):
            v = a[d]
            for m in range(d + 1, min(BAND, t) + 1):
                v = v - w[m] * l[t - d][m - d]
            w[d] = v
        return w

    def eliminate(a, l, dinv, t):
        w = row_weights(a, l, t, 1)
        row = {d: w[d] * dinv[t - d] for d in w}
        pivot = a[0]
        for d in w:
            pivot = pivot - w[d] * row[d]
        return row, 1.0 / pivot

    def body(c, carry):
        part = pl.ds(c * FACTOR_ROWS, FACTOR_ROWS)
        alpha = alpha_ref[part, :]
        l, dinv, sent = {}, {}, {}
        for t in range(HALF):
            a = [coefficient(alpha, 1, t, d) for d in range(min(BAND, t) + 1)]
            l[t], dinv[t] = eliminate(a, l, dinv, t)
            sent[t] = jnp.broadcast_to(mode(2, t), alpha.shape)
            for d in l[t]:
                sent[t] = sent[t] - l[t][d] * sent[t - d]
            if t >= TOP:
                for d in range(1, BAND + 1):
                    lo_ref[t - TOP, d - 1, part, :] = l[t][d]
                do_ref[t - TOP, part, :] = dinv[t]
        outer = {}
        for j in range(BAND):
            t = HALF + j
            a = [coefficient(alpha, 1, t, d) for d in range(BAND + 1)]
            outer[j] = row_weights(a, l, t, j + 1)
            l[t] = {d: outer[j][d] * dinv[t - d] for d in outer[j]}
            for d in range(1, BAND + 1):
                lo_ref[BAND + j, d - 1, part, :] = l[t][d] if d in l[t] else jnp.zeros_like(alpha)
        schur = {}
        for j in range(BAND):
            for i in range(j + 1):
                total = None
                for s in range(TOP + j, HALF):
                    term = outer[j][HALF + j - s] * l[HALF + i][HALF + i - s] if HALF + i - s <= BAND else None
                    if term is not None:
                        total = term if total is None else total + term
                schur[(j, i)] = schur[(i, j)] = total
        shift = {}
        for j in range(BAND):
            for d in range(j + 1, BAND + 1):
                term = l[HALF + j][d] * sent[HALF + j - d]
                shift[j] = term if j not in shift else shift[j] + term
        l, dinv, z = {}, {}, {}
        plain, plain_inv = None, None
        for t in range(HALF):
            a = [coefficient(alpha, 0, t, d) for d in range(min(BAND, t) + 1)]
            if t == TOP:
                plain, plain_inv = dict(l), dict(dinv)
            if t >= TOP:
                plain[t], plain_inv[t] = eliminate(a, plain, plain_inv, t)
                for d in range(1, BAND + 1):
                    lu_ref[t - TOP, d - 1, part, :] = plain[t][d]
                j = HALF - 1 - t
                for d in range(t - TOP + 1):
                    a[d] = a[d] - schur[(j, j + d)]
            l[t], dinv[t] = eliminate(a, l, dinv, t)
            for d in range(1, BAND + 1):
                l_ref[t, d - 1, part, :] = l[t][d] if d in l[t] else jnp.zeros_like(alpha)
            dinv_ref[t, part, :] = dinv[t]
            z[t] = jnp.broadcast_to(mode(1, t), alpha.shape)
            if t >= TOP:
                z[t] = z[t] - shift[HALF - 1 - t]
            for d in l[t]:
                z[t] = z[t] - l[t][d] * z[t - d]
            zs[t] = z[t]
        exact = 1.0 / (alpha + modes[3, 0:1, :])
        y, miss, norm = {}, jnp.zeros_like(alpha), jnp.zeros_like(modes[3, 0:1, :])
        for t in range(HALF - 1, -1, -1):
            y[t] = zs[t] * dinv_ref[t, part, :]
            for d in range(1, min(BAND, HALF - 1 - t) + 1):
                y[t] = y[t] - l_ref[t + d, d - 1, part, :] * y[t + d]
            miss = miss + mode(1, t) * (mode(0, t) * exact - y[t])
            norm = norm + mode(1, t) * mode(0, t)
        mend_ref[part, :] = jnp.where(norm > 0.01, miss / jnp.maximum(norm, 0.01), 0.0)
        return carry

    lax.fori_loop(0, N // FACTOR_ROWS, body, 0)


def four(get):
    return [get(side, who) for side in range(2) for who in range(2)]


def vertical_apply(products, vert, scal_k, scal_m, scal_v):
    mass = [k * p[:, :N] + m * p[:, N:] for p, k, m in zip(products, scal_k, scal_m)]
    stiff = [v * p[:, :N] for p, v in zip(products, scal_v)]
    out = dot_full(vert[0], jnp.concatenate(mass, axis=1))
    out = out + dot_full(vert[1], jnp.concatenate(stiff, axis=1))
    return [out[:, q * N:(q + 1) * N] for q in range(len(products))]


def plane_products(faces, mk):
    stacked = dot_full(jnp.concatenate(faces, axis=0), mk[...])
    return [stacked[q * ROWS:(q + 1) * ROWS] for q in range(len(faces))]


def flip_masks(scal, nscal):
    return [scal[side, 3:4, :] != nscal[side, 3:4, :] for side in range(2)]


def orient_all(arrays, mirror, masks):
    turned = dot_full(jnp.concatenate([a for _, a in arrays], axis=0), mirror[...])
    return [
        jnp.where(masks[side], turned[q * ROWS:(q + 1) * ROWS], a)
        for q, (side, a) in enumerate(arrays)
    ]


def update_faces(c_faces, state, scal, nscal, mirror, mk, vert):
    masks = flip_masks(scal, nscal)
    residual = four(lambda side, who: state[4][2 * side + who])
    arrays = []
    for side in range(2):
        for who in range(2):
            arrays.append((side, c_faces[2 * side + 1 - who]))
    for side in range(2):
        for who in range(2):
            arrays.append((side, residual[2 * side + 1 - who]))
    turned = orient_all(arrays, mirror, masks)
    e, added = turned[:4], turned[4:]
    products = plane_products(e, mk)
    which = four(lambda side, who: (nscal if who else scal)[side])
    applied = vertical_apply(
        products, vert, [w[0:1] for w in which], [w[1:2] for w in which], [w[2:3] for w in which]
    )
    new = [list(state[s]) for s in range(6)]
    for q in range(4):
        new[2][q] = state[2][q] + DAMPING * (c_faces[q] + e[q])
        new[3][q] = state[3][q] + DAMPING * (residual[q] + added[q] + applied[q])
        new[4][q] = state[0][q] - state[1][q] * new[2][q] - new[3][q]
        new[5][q] = KEEP * state[5][q] + DAMPING * e[q]
    return new, e, masks


def read_state(ref):
    return [[ref[s, q] for q in range(4)] for s in range(6)]


def pad_rows(x):
    return jnp.concatenate([x, jnp.zeros((ROWS - x.shape[0], N), F32)], axis=0)


def eliminate_forward(gh_ref, spread, rows_hat, l_ref, lu_ref, modes, z_ref, msg_ref):
    def body(c, carry):
        part = pl.ds(pl.multiple_of(c * CHUNK, CHUNK), CHUNK)
        west, east = spread[0, part, :], spread[1, part, :]
        z = {}
        lowest = jnp.zeros_like(west)
        for t in range(HALF):
            x = gh_ref[t, part, :] + west * rows_hat[0, t:t + 1, :] + east * rows_hat[1, t:t + 1, :]
            lowest = lowest + modes[0, t:t + 1, :] * x
            z_ref[t, part, :] = x
            table, index = (l_ref, t) if t < TOP else (lu_ref, t - TOP)
            for d in range(1, min(BAND, t) + 1):
                x = x - table[index, d - 1, part, :] * z[t - d]
            z[t] = x
            if t < TOP:
                z_ref[t, part, :] = x
            else:
                msg_ref[t - TOP, part, :] = x
        msg_ref[BAND, part, :] = lowest
        return carry

    lax.fori_loop(0, N // CHUNK, body, 0)


def first_kernel(
    ints, gh, own_pay, rec0, rec1, scal, spread, b_full, mirror, l_ref, lu_ref, modes,
    z_ref, msg_ref, state_ref, rows_u, rows_g, nscal_ref, rows_hat,
):
    received = sides(ints, rec0[...], rec1[...])
    for side in range(2):
        nscal_ref[side] = received[side][ROWS:ROWS + 8]
    masks = flip_masks(scal, nscal_ref)
    state_ref[...] = jnp.zeros_like(state_ref)
    for side in range(2):
        for who in range(2):
            values = received[side][:ROWS] if who else own_pay[side, :ROWS]
            state_ref[0, 2 * side + who] = values
            state_ref[4, 2 * side + who] = values
    turned = orient_all([(side, received[side][:ROWS]) for side in range(2)], mirror, masks)
    rows_u[...] = jnp.zeros_like(rows_u)
    for side in range(2):
        rows_g[side] = turned[side]
        rows_hat[side] = dot_full(turned[side], b_full[...])
    eliminate_forward(gh, spread, rows_hat, l_ref, lu_ref, modes, z_ref, msg_ref)


def next_kernel(
    ints, gh, own_pay, rec0, rec1, state_in, scal, nscal, spread, b_full, mirror, mk, vert,
    l_ref, lu_ref, modes, z_ref, msg_ref, state_ref, rows_u, rows_g, rows_hat,
):
    received = sides(ints, rec0[...], rec1[...])
    state = read_state(state_in)
    if own_pay.shape[1] > ROWS:
        for side in range(2):
            state[1][2 * side] = pad_rows(own_pay[side, ROWS:])
            state[1][2 * side + 1] = pad_rows(received[side][ROWS:])
    c_faces = four(lambda side, who: received[side][:ROWS] if who else own_pay[side, :ROWS])
    state, e, masks = update_faces(c_faces, state, scal, nscal, mirror, mk, vert)
    for s in range(6):
        for q in range(4):
            state_ref[s, q] = state[s][q]
    turned = orient_all([(side, state[4][2 * side + 1]) for side in range(2)], mirror, masks)
    for side in range(2):
        step = DAMPING * e[2 * side]
        rows = turned[side] - state[1][2 * side] * step
        rows_u[side] = step
        rows_g[side] = rows
        rows_hat[side] = dot_full(rows, b_full[...])
    eliminate_forward(gh, spread, rows_hat, l_ref, lu_ref, modes, z_ref, msg_ref)


def solve_kernel(
    ints, z_ref, msg_ref, zr_ref, l_ref, dinv_ref, lo_ref, do_ref, mend, modes, spread, bt_full, state, extra,
    y_ref, pay_ref, slot0, slot1, sums,
):
    sums[...] = jnp.zeros_like(sums)

    def body(c, carry):
        part = pl.ds(pl.multiple_of(c * CHUNK, CHUNK), CHUNK)
        sent = [zr_ref[s, part, :] for s in range(BAND)]
        weights = (spread[0, part, :], spread[1, part, :])

        low = mend[part, :] * (msg_ref[BAND, part, :] + zr_ref[BAND, part, :])

        def put(t, value):
            value = value + low * modes[0, t:t + 1, :]
            y_ref[t, part, :] = value
            for side in range(2):
                product = weights[side] * value
                total = product[0:8]
                for s in range(8, CHUNK, 8):
                    total = total + product[s:s + 8]
                sums[side, t] += total

        z = {t: z_ref[t, part, :] for t in range(TOP - BAND, HALF)}
        for j in range(BAND):
            for d in range(j + 1, BAND + 1):
                z[HALF - 1 - j] = z[HALF - 1 - j] - lo_ref[BAND + j, d - 1, part, :] * sent[BAND + j - d]
        for t in range(TOP, HALF):
            for d in range(1, BAND + 1):
                z[t] = z[t] - l_ref[t, d - 1, part, :] * z[t - d]
        y = {}
        for t in range(HALF - 1, TOP - 1, -1):
            value = z[t] * dinv_ref[t, part, :]
            for d in range(1, HALF - t):
                value = value - l_ref[t + d, d - 1, part, :] * y[t + d]
            y[t] = value
            put(t, value)
        far = {HALF + j: y[HALF - 1 - j] for j in range(BAND)}
        for t in range(HALF - 1, TOP - 1, -1):
            value = sent[t - TOP] * do_ref[t - TOP, part, :]
            for d in range(1, BAND + 1):
                value = value - lo_ref[t + d - TOP, d - 1, part, :] * far[t + d]
            far[t] = value
            put(2 * HALF - 1 - t, value)
        for t in range(TOP - 1, -1, -1):
            source = z[t] if t in z else z_ref[t, part, :]
            value = source * dinv_ref[t, part, :]
            for d in range(1, BAND + 1):
                value = value - l_ref[t + d, d - 1, part, :] * y[t + d]
            y[t] = value
            put(t, value)
        return carry

    lax.fori_loop(0, N // CHUNK, body, 0)
    mixed = jnp.sum(sums[...], axis=2)
    faces = dot_full(mixed.reshape(2 * ROWS, N), bt_full[...])
    packs = []
    for side in range(2):
        c = faces[side * ROWS:(side + 1) * ROWS] - state[2, 2 * side]
        pay_ref[side, :ROWS] = c
        if pay_ref.shape[1] > ROWS:
            pay_ref[side, ROWS:] = extra[side]
    slots(ints, pay_ref[0], pay_ref[1], (slot0, slot1))


def back_planes(y, wbt, lb):
    count = y.shape[0]
    across = right_mul(y.reshape(count * N, N), wbt).reshape(count, N, N)
    return left_mul_planes(lb, [across[q] for q in range(count)])


def make_plane_kernel(sweep):
    last = sweep == SWEEPS - 1

    def kernel(*refs):
        refs = list(refs)
        refs.pop(0)
        y_ref, f_ref, r_ref, rows_u, rows_g, mask, wbt, lb = refs[:8]
        refs = refs[8:]
        if sweep > 0:
            up_in, g_in = refs[:2]
            refs = refs[2:]
        if last:
            wrt, lr, cut, pay_in = refs[:4]
            up_out, coarse_out, pay_out, slot0, slot1, sums = refs[4:]
        else:
            wb, lbt = refs[:2]
            up_out, g_out, gh_out = refs[2:]

        def on_faces(rows, t):
            return mask[0] * rows[0, pl.ds(t, 1), :] + mask[1] * rows[1, pl.ds(t, 1), :]

        def body(g, carry):
            t0 = g * GROUP
            corrections = back_planes(y_ref[pl.ds(t0, GROUP)], wbt[...], lb[...])
            fresh = []
            for q in range(GROUP):
                t = t0 + q
                on_u, on_g = on_faces(rows_u, t), on_faces(rows_g, t)
                load, react = f_ref[t], r_ref[t]
                if sweep == 0:
                    u, total = on_u, DAMPING * (load + on_g)
                else:
                    old = up_in[t]
                    u = old + on_u
                    total = KEEP * g_in[t] + DAMPING * (load - react * old + on_g)
                new = KEEP * u + DAMPING * corrections[q]
                up_out[t] = new
                residual = load - react * new
                if last:
                    residual = residual - total
                    for side in range(2):
                        product = cut[side] * residual
                        part = product[0:8]
                        for s in range(8, N, 8):
                            part = part + product[s:s + 8]
                        sums[side, t] = part
                else:
                    g_out[t] = total
                fresh.append(residual)
            stacked = jnp.concatenate(fresh, axis=0).reshape(GROUP, N, N)
            if last:
                planes = forward_planes(stacked, wrt[...], lr[...])
            else:
                planes = forward_planes(stacked, wb[...], lbt[...])
            for q in range(GROUP):
                (coarse_out if last else gh_out)[t0 + q] = planes[q]
            return carry

        lax.fori_loop(0, HALF // GROUP, body, 0)
        if last:
            ints = kernel_ints[0]
            for side in range(2):
                pay_out[side, :ROWS] = pay_in[side, :ROWS]
                pay_out[side, ROWS:] = jnp.sum(sums[side], axis=1)
            slots(ints, pay_out[0], pay_out[1], (slot0, slot1))

    kernel_ints = []

    def outer(ints, *refs):
        kernel_ints.clear()
        kernel_ints.append(ints)
        kernel(ints, *refs)

    return outer


def final_kernel(
    ints, floats, up, coarse_in, own_pay, rec0, rec1, state_in, scal, nscal, mirror, mirror_coarse, mk, vert,
    rt_full, mask, profile, out_u, out_d, parts, plane,
):
    received = sides(ints, rec0[...], rec1[...])
    state = read_state(state_in)
    c_faces = four(lambda side, who: received[side][:ROWS] if who else own_pay[side, :ROWS])
    state, e, masks = update_faces(c_faces, state, scal, nscal, mirror, mk, vert)
    gathered = state[5]
    products = plane_products(gathered, mk)
    far = vertical_apply(
        [products[1], products[3]], vert,
        [nscal[side, 4:5] for side in range(2)],
        [nscal[side, 5:6] for side in range(2)],
        [nscal[side, 6:7] for side in range(2)],
    )
    one = floats[0]
    near_stiff = vertical_apply([products[0], products[2]], vert, [one] * 2, [floats[3]] * 2, [floats[3]] * 2)
    near_mass = vertical_apply([products[0], products[2]], vert, [floats[3]] * 2, [floats[1]] * 2, [floats[2]] * 2)
    stack = []
    for side in range(2):
        nbr = 2 * side + 1
        theirs = pad_rows(received[side][ROWS:])
        theirs = theirs - nscal[side, 7:8] * DAMPING * state[1][nbr] * e[nbr] - far[side]
        mine = scal[side, 7:8] * DAMPING * state[1][2 * side] * e[2 * side]
        stack += [near_stiff[side], near_mass[side], mine, theirs]
    restricted = dot_full(jnp.concatenate(stack, axis=0), rt_full[...])
    pieces = [restricted[q * ROWS:(q + 1) * ROWS] for q in range(8)]
    turned = dot_full(jnp.concatenate([pieces[3], pieces[7]], axis=0), mirror_coarse[...])
    for side in range(2):
        added = jnp.where(masks[side], turned[side * ROWS:(side + 1) * ROWS], pieces[4 * side + 3])
        parts[3 * side] = -pieces[4 * side]
        parts[3 * side + 1] = -pieces[4 * side + 1]
        parts[3 * side + 2] = added - pieces[4 * side + 2]

    def coarse_body(t, carry):
        value = coarse_in[t]
        for s in range(6):
            value = value + profile[s] * parts[s, pl.ds(t, 1), :]
        plane[...] = value

        @pl.when(ints[1] == 1)
        def _():
            plane[...] = value.T

        @pl.when(ints[3] == 0)
        def _():
            out_d[0, t] = plane[0:32]
            out_d[1, t] = plane[63:95]

        @pl.when(ints[3] == 1)
        def _():
            out_d[0, t] = plane[31:63]
            out_d[1, t] = plane[94:126]

        return carry

    lax.fori_loop(0, HALF, coarse_body, 0, unroll=2)

    for side in range(2):
        parts[side] = DAMPING * e[2 * side]

    def u_body(index, carry):
        inside = ints[3] * BLOCK + index
        t = jnp.where(ints[2] == 1, HALF - 1 - inside, inside)
        value = up[t] + mask[0] * parts[0, pl.ds(t, 1), :] + mask[1] * parts[1, pl.ds(t, 1), :]
        out_u[index] = value

        @pl.when(ints[1] == 1)
        def _():
            out_u[index] = value.T

        return carry

    lax.fori_loop(0, BLOCK, u_body, 0, unroll=2)


def prepare_kernel(
    ints, floats, stiff, mass, stiff_v, mass_v, basis, eigen, basis_v, eigen_v, restrict,
    wb, wbt, wrt, lb, lbt, lr, bt_out, rt_out, mk, mirror, mirror_coarse, vert, scal, spread, mask, cut,
    profile, alpha, bands, modes,
):
    a1, a2, a3 = floats[0], floats[1], floats[2]
    rows = lax.broadcasted_iota(jnp.int32, (N, N), 0)
    lanes = lax.broadcasted_iota(jnp.int32, (N, N), 1)
    eye = rows == lanes

    def column(row):
        picked = jnp.sum(jnp.where(eye, row, 0.0), axis=1, keepdims=True)
        return jnp.broadcast_to(picked, (N, N))

    b, k, m = basis[...], stiff[...], mass[...]
    bt = b.T
    r = jnp.concatenate([restrict[...], jnp.zeros((N - COARSE, N), F32)], axis=0)
    rt = r.T
    wb[...], wbt[...], wrt[...] = pack_right(b), pack_right(bt), pack_right(rt)
    lb[...], lbt[...], lr[...] = pack_left(b), pack_left(bt), pack_left(r)
    bt_out[...], rt_out[...] = bt, rt
    mk[:, :N], mk[:, N:] = m, k
    mirror[...] = (rows + lanes == N - 1).astype(F32)
    mirror_coarse[...] = (rows + lanes == COARSE - 1).astype(F32)
    alpha[...] = a1 * column(eigen[...]) + a2 * eigen[...]

    turn = (
        lax.broadcasted_iota(jnp.int32, (LAYERS, LAYERS), 0)
        + lax.broadcasted_iota(jnp.int32, (LAYERS, LAYERS), 1)
        == LAYERS - 1
    ).astype(F32)
    first = ints[2] == 0
    kv, mv = stiff_v[...], mass_v[...]
    ordered = []
    for matrix in (mv, a3 * kv):
        turned = dot_full(dot_full(turn, matrix), turn)
        ordered.append((jnp.where(first, matrix, turned), jnp.where(first, turned, matrix)))
    deep = lax.broadcasted_iota(jnp.int32, (ROWS, LAYERS), 0)
    wide = lax.broadcasted_iota(jnp.int32, (ROWS, LAYERS), 1)
    inside = (deep < HALF) & (wide < REACH)
    own_stiff = jnp.where(first, kv, dot_full(dot_full(turn, kv), turn))
    vert[0] = jnp.where(inside, ordered[0][0][:ROWS], 0.0)[:, :ROWS]
    vert[1] = jnp.where(inside, own_stiff[:ROWS], 0.0)[:, :ROWS]
    for which in range(2):
        for s in range(2):
            for d in range(BAND + 1):
                picked = jnp.where(deep - wide == d, ordered[s][which][:ROWS], 0.0)
                bands[which, s, d] = jnp.broadcast_to(jnp.sum(picked, axis=1, keepdims=True), (ROWS, N))

    mu = eigen_v[...]
    least = jnp.min(mu, axis=1, keepdims=True)
    number = lax.broadcasted_iota(jnp.int32, (1, LAYERS), 1)
    chosen = jnp.min(jnp.where(mu == least, number, LAYERS), axis=1, keepdims=True)
    low = jnp.sum(jnp.where(number == chosen, basis_v[...], 0.0), axis=1, keepdims=True)
    low = jnp.broadcast_to(low, (LAYERS, N))
    low_mass = dot_full(mv, low)
    low_turned, mass_turned = dot_full(turn, low), dot_full(turn, low_mass)
    modes[0] = jnp.where(first, low, low_turned)[:ROWS]
    modes[1] = jnp.where(first, low_mass, mass_turned)[:ROWS]
    modes[2] = jnp.where(first, mass_turned, low_mass)[:ROWS]
    modes[3] = jnp.broadcast_to(a3 * least, (ROWS, N))

    for side in range(2):
        start = ints[4 + side] == 0

        def end_row(matrix, count=N):
            return jnp.where(start, matrix[0:1, :], matrix[count - 1:count, :])

        def corner(matrix):
            value = jnp.where(start, matrix[0:1, 0:1], matrix[N - 1:N, N - 1:N])
            return jnp.broadcast_to(value, (1, N))

        cut_row = end_row(r, COARSE)
        cut_at = jnp.broadcast_to(jnp.where(start, cut_row[:, 0:1], cut_row[:, N - 1:N]), (1, N))
        stiff_profile = jnp.broadcast_to(jnp.sum(r * end_row(k), axis=1, keepdims=True), (N, N))
        mass_profile = jnp.broadcast_to(jnp.sum(r * end_row(m), axis=1, keepdims=True), (N, N))
        at_face = jnp.where(start, 0, COARSE - 1)
        profile[3 * side] = stiff_profile
        profile[3 * side + 1] = mass_profile
        profile[3 * side + 2] = (rows == at_face).astype(F32)
        spread[side] = column(end_row(b))
        mask[side] = (rows == ints[4 + side]).astype(F32)
        cut[side] = column(cut_row)
        scal[side] = jnp.concatenate(
            [
                corner(k) * a1,
                corner(m) * a2,
                corner(m) * a3,
                jnp.broadcast_to(ints[6].astype(F32), (1, N)),
                end_row(stiff_profile, COARSE) * a1,
                end_row(mass_profile, COARSE) * a2,
                end_row(mass_profile, COARSE) * a3,
                cut_at,
            ],
            axis=0,
        )


def per_device(
    load_vector,
    reaction,
    geometry,
    stiff_plane,
    mass_plane,
    stiff_vertical,
    mass_vertical,
    basis_plane,
    eigen_plane,
    basis_vertical,
    eigen_vertical,
    restrict_plane,
    restrict_vertical,
    patch_links,
):
    slab = lax.axis_index("slab")
    half, core = slab // 2, slab % 2
    patch = lax.axis_index("patch")
    patches = lax.axis_size("patch")
    links = patch_links[0]
    geo = geometry[0]
    kind = links[0] // 2
    west_end, east_end = links[0] % 2, links[1] % 2
    ints = jnp.stack(
        [patch % 2, kind, half, core, (N - 1) * west_end, (N - 1) * east_end, links[2], kind]
    ).astype(jnp.int32)
    a1 = jnp.where(kind == 0, geo[0], geo[1])
    a2 = jnp.where(kind == 0, geo[1], geo[0])
    floats = jnp.stack([a1, a2, geo[2], jnp.zeros_like(a1)])
    square, two = (N, N), (2, N, N)
    right = jax.ShapeDtypeStruct((2 * N, 2 * N), BF16)
    left = jax.ShapeDtypeStruct((N, 2 * N), BF16)
    (
        wb, wbt, wrt, lb, lbt, lr, basis_t, restrict_t, mk, mirror, mirror_coarse, vert, scal, spread, mask,
        cut, profile, alpha, bands, modes,
    ) = call(
        prepare_kernel,
        [
            right, right, right, left, left, left, square, square, (N, 2 * N), square, square,
            (2, ROWS, ROWS), (2, 8, N), two, two, two, (6, N, N), square, (2, 2, BAND + 1, ROWS, N), (4, ROWS, N),
        ],
        ints, stiff_plane, mass_plane, stiff_vertical, mass_vertical, basis_plane, eigen_plane.reshape(1, N),
        basis_vertical, eigen_vertical.reshape(1, LAYERS), restrict_plane,
        floats=floats, flops=20_000_000,
    )

    pair = [(0, 1), (1, 0), (2, 3), (3, 2)]
    cross = [(0, 2), (2, 0), (1, 3), (3, 1)]
    even = [(i, i ^ 1) for i in range(patches)]
    odd = [(i, (i + 1) % patches if i % 2 else (i - 1) % patches) for i in range(patches)]

    def swap_faces(slot0, slot1):
        return lax.ppermute(slot0, "patch", odd), lax.ppermute(slot1, "patch", even)

    field = (HALF, N, N)
    own_load = load_vector[0].reshape(BLOCK, N, N)
    own_react = reaction[0].reshape(BLOCK, N, N)
    other_load = lax.ppermute(own_load, "slab", pair)
    other_react = lax.ppermute(own_react, "slab", pair)
    size = ROWS + 8
    f, pay, slot0, slot1 = call(
        load_kernel, [field, (2, size, N), (size, N), (size, N)], ints, own_load, other_load, scal
    )
    rec0, rec1 = swap_faces(slot0, slot1)
    r, react_faces = call(reaction_kernel, [field, (2, HALF, N)], ints, own_react, other_react)
    l, dinv, lu, lo, do, mend = call(
        factor_kernel,
        [(HALF, BAND, N, N), field, (BAND, BAND, N, N), (2 * BAND, BAND, N, N), (BAND, N, N), square],
        ints, alpha, bands, modes, scratch=[pltpu.VMEM((HALF, FACTOR_ROWS, N), F32)], flops=40_000_000,
    )
    (gh,) = call(transform_kernel, [field], ints, f, wb, lbt, flops=1_000_000_000)
    rows_hat = pltpu.VMEM((2, ROWS, N), F32)
    sums = pltpu.VMEM((2, ROWS, 8, N), F32)
    message = (BAND + 1, N, N)
    state_shape = (6, 4, ROWS, N)
    rows_shape = (2, ROWS, N)
    up = total = None
    for sweep in range(SWEEPS):
        if sweep == 0:
            z, msg, state, rows_u, rows_g, nscal = call(
                first_kernel,
                [field, message, state_shape, rows_shape, rows_shape, (2, 8, N)],
                ints, gh, pay, rec0, rec1, scal, spread, basis_plane, mirror, l, lu, modes,
                scratch=[rows_hat], flops=10_000_000,
            )
        else:
            z, msg, state, rows_u, rows_g = call(
                next_kernel,
                [field, message, state_shape, rows_shape, rows_shape],
                ints, gh, pay, rec0, rec1, state, scal, nscal, spread, basis_plane, mirror, mk, vert, l, lu, modes,
                scratch=[rows_hat], flops=10_000_000,
            )
        received = lax.ppermute(msg, "slab", cross)
        last = sweep == SWEEPS - 1
        size = ROWS + HALF if sweep == 0 else ROWS
        y, pay, slot0, slot1 = call(
            solve_kernel,
            [(REACH, N, N), (2, size, N), (size, N), (size, N)],
            ints, z, msg, received, l, dinv, lo, do, mend, modes, spread, basis_t, state, react_faces,
            scratch=[sums], flops=10_000_000,
        )
        args = [y, f, r, rows_u, rows_g, mask, wbt, lb]
        if sweep > 0:
            args += [up, total]
        plane_kernel = make_plane_kernel(sweep)
        if last:
            size = ROWS + HALF
            up, coarse, pay, slot0, slot1 = call(
                plane_kernel,
                [field, field, (2, size, N), (size, N), (size, N)],
                ints, *args, wrt, lr, cut, pay,
                scratch=[pltpu.VMEM((2, HALF, 8, N), F32)], flops=2_000_000_000,
            )
            rec0, rec1 = swap_faces(slot0, slot1)
        else:
            rec0, rec1 = swap_faces(slot0, slot1)
            up, total, gh = call(
                plane_kernel, [field, field, field], ints, *args, wb, lbt, flops=2_000_000_000
            )
    out_u, blocks = call(
        final_kernel,
        [(BLOCK, N, N), (2, HALF, 32, N)],
        ints, up, coarse, pay, rec0, rec1, state, scal, nscal, mirror, mirror_coarse, mk, vert,
        restrict_t, mask, profile, floats=floats,
        scratch=[pltpu.VMEM((6, ROWS, N), F32), pltpu.VMEM((N, N), F32)], flops=10_000_000,
    )
    kept = lax.dynamic_index_in_dim(blocks, half, 0, keepdims=False)
    sent = lax.dynamic_index_in_dim(blocks, 1 - half, 0, keepdims=False)
    arrived = lax.ppermute(sent, "slab", cross)
    turned = restrict_vertical[:, ::-1]
    near = jnp.where(half == 0, restrict_vertical[:, :HALF], turned[:, :HALF])
    far = jnp.where(half == 0, turned[:, :HALF], restrict_vertical[:, :HALF])
    coarse = jnp.einsum("mt,tcd->mcd", near, kept, precision=HIGHEST)
    coarse = coarse + jnp.einsum("mt,tcd->mcd", far, arrived, precision=HIGHEST)
    flat = coarse[:, :, :COARSE].reshape(coarse.shape[0], 32 * COARSE)
    share = COARSE * COARSE // 4
    flat = lax.dynamic_slice_in_dim(flat, core * (COARSE // 2), share, axis=1)
    return out_u.reshape(1, BLOCK, N * N), flat[None]


def solution(mesh):
    in_specs = (
        P("patch", "slab", None),
        P("patch", "slab", None),
        P("patch", None),
        P(), P(), P(), P(), P(), P(), P(), P(), P(), P(),
        P("patch", None),
    )
    out_specs = (P("patch", "slab", None), P("patch", None, "slab"))
    return jax.shard_map(
        per_device, mesh=mesh, in_specs=in_specs, out_specs=out_specs, check_vma=False
    )
```

```python
import jax
import jax.numpy as jnp
from jax import lax
from jax.experimental import pallas as pl
from jax.experimental.pallas import tpu as pltpu
from jax.sharding import PartitionSpec as P

BAND = 4
SWEEPS = 3
DAMPING = 0.25
KEEP = 1.0 - DAMPING
HIGHEST = lax.Precision.HIGHEST
F32 = jnp.float32
BF16 = jnp.bfloat16

N = 128
LAYERS = 64
HALF = 32
BLOCK = 16
REACH = HALF + BAND
ROWS = 40
TOP = HALF - BAND
CHUNK = 64
COARSE = N - 2


def split(x):
    high = x.astype(BF16)
    return high, (x - high.astype(F32)).astype(BF16)


def right_mul(x, packed):
    high, low = split(x)
    both = jnp.dot(jnp.concatenate([high, low], axis=-1), packed, preferred_element_type=F32)
    return both[:, :N] + both[:, N:]


def left_mul_planes(packed, planes):
    out = []
    for q in range(0, len(planes), 2):
        high, low = split(jnp.concatenate(planes[q:q + 2], axis=1))
        wide = jnp.dot(packed, jnp.concatenate([high, high], axis=0), preferred_element_type=F32)
        wide = wide + jnp.dot(packed[:, :N], low, preferred_element_type=F32)
        out += [wide[:, :N], wide[:, N:]]
    return out


def dot_full(x, y):
    return jnp.dot(x, y, precision=HIGHEST, preferred_element_type=F32)


def pack_right(a):
    high, low = split(a)
    top = jnp.concatenate([high, low], axis=1)
    bottom = jnp.concatenate([high, jnp.zeros_like(low)], axis=1)
    return jnp.concatenate([top, bottom], axis=0)


def pack_left(a):
    return jnp.concatenate(split(a), axis=1)


def call(kernel, outs, links, *args, flops=0, scratch=(), geometry=None):
    smem = [links] if geometry is None else [links, geometry]
    specs = [pl.BlockSpec(memory_space=pltpu.SMEM)] * len(smem)
    specs += [pl.BlockSpec(memory_space=pltpu.VMEM)] * len(args)
    shapes = [s if isinstance(s, jax.ShapeDtypeStruct) else jax.ShapeDtypeStruct(s, F32) for s in outs]
    moved = sum(a.size * a.dtype.itemsize for a in args) + sum(4 * s.size for s in shapes)

    def body(links_ref, *refs):
        ints = facts(links_ref)
        if geometry is None:
            kernel(ints, *refs)
        else:
            kernel(ints, scales(ints, refs[0]), *refs[1:])

    return pl.pallas_call(
        body,
        out_shape=shapes,
        in_specs=specs,
        out_specs=[pl.BlockSpec(memory_space=pltpu.VMEM)] * len(outs),
        scratch_shapes=list(scratch),
        compiler_params=pltpu.CompilerParams(vmem_limit_bytes=16 * 1024 * 1024),
        cost_estimate=pl.CostEstimate(
            flops=flops, bytes_accessed=moved, transcendentals=0
        ),
    )(*smem, *args)


def facts(links):
    slab = lax.axis_index("slab")
    west, east = links[0, 0], links[0, 1]
    return (
        links[0, 2], jnp.right_shift(west, 1), jnp.right_shift(slab, 1), jnp.bitwise_and(slab, 1),
        (N - 1) * jnp.bitwise_and(west, 1), (N - 1) * jnp.bitwise_and(east, 1),
    )


def scales(ints, geometry):
    turned = ints[1] == 1
    first, second = geometry[0, 0], geometry[0, 1]
    return (
        jnp.where(turned, second, first), jnp.where(turned, first, second), geometry[0, 2], jnp.float32(0),
    )


def source_layer(ints, t):
    inside = jnp.where(ints[2] == 1, HALF - 1 - t, t)
    return jnp.right_shift(inside, 4), jnp.bitwise_and(inside, BLOCK - 1)


def load_layer(ints, own_ref, other_ref, out_ref, t):
    block, index = source_layer(ints, t)
    mine = own_ref[index]
    theirs = other_ref[index]
    value = jnp.where(block == ints[3], mine, theirs)
    out_ref[t] = value

    @pl.when(ints[1] == 1)
    def _():
        out_ref[t] = value.T


def slot(ints, west, east, slot_ref):
    slot_ref[...] = jnp.where(ints[3] == 0, west, east)


def face_rows(ints, ref, side):
    position = ints[4 + side]
    return jnp.where(position == 0, ref[:, 0, :], ref[:, N - 1, :])


def load_kernel(ints, own, other, f_ref, pay_ref, slot_ref):
    def body(t, carry):
        load_layer(ints, own, other, f_ref, t)
        return carry

    lax.fori_loop(0, HALF, body, 0, unroll=4)
    flag = jnp.broadcast_to(ints[0].astype(F32), (8, N))
    for side in range(2):
        rows = face_rows(ints, f_ref, side)
        pay_ref[side] = jnp.concatenate([rows, jnp.zeros((ROWS - HALF, N), F32), flag], axis=0)
    slot(ints, pay_ref[0], pay_ref[1], slot_ref)


def reaction_kernel(ints, ready, own, other, r_ref, face_ref):
    def body(t, carry):
        load_layer(ints, own, other, r_ref, t)
        return carry

    lax.fori_loop(0, HALF, body, 0, unroll=4)
    for side in range(2):
        face_ref[side] = face_rows(ints, r_ref, side)


def forward_planes(x, wb, lbt):
    count = x.shape[0]
    first = right_mul(x.reshape(count * N, N), wb).reshape(count, N, N)
    return left_mul_planes(lbt, [first[q] for q in range(count)])


GROUP = 32


def transform_kernel(ints, f_ref, wb, lbt, out_ref):
    def body(g, carry):
        t = g * GROUP
        planes = forward_planes(f_ref[pl.ds(t, GROUP)], wb[...], lbt[...])
        for q in range(GROUP):
            out_ref[t + q] = planes[q]
        return carry

    lax.fori_loop(0, HALF // GROUP, body, 0)


FACTOR_ROWS = 16


def coefficient(bands, alpha, which, t, d):
    return alpha * bands[which, 0, d, t:t + 1, :] + bands[which, 1, d, t:t + 1, :]


def row_weights(a, l, t, least):
    w = {}
    for d in range(min(BAND, t), least - 1, -1):
        v = a[d]
        for m in range(d + 1, min(BAND, t) + 1):
            v = v - w[m] * l[t - d][m - d]
        w[d] = v
    return w


def eliminate(a, l, dinv, t):
    w = row_weights(a, l, t, 1)
    row = {d: w[d] * dinv[t - d] for d in w}
    pivot = a[0]
    for d in w:
        pivot = pivot - w[d] * row[d]
    return row, 1.0 / pivot


def factor_kernel(ints, ready, alpha_ref, bands, l_ref, dinv_ref):
    def body(c, carry):
        part = pl.ds(c * FACTOR_ROWS, FACTOR_ROWS)
        alpha = alpha_ref[part, :]
        l, dinv = {}, {}
        for t in range(HALF):
            a = [coefficient(bands, alpha, 0, t, d) for d in range(min(BAND, t) + 1)]
            l[t], dinv[t] = eliminate(a, l, dinv, t)
            for d in l[t]:
                l_ref[t, d - 1, part, :] = l[t][d]
            dinv_ref[t, part, :] = dinv[t]
        return carry

    lax.fori_loop(0, N // FACTOR_ROWS, body, 0)


def meet_kernel(
    ints, alpha_ref, bands, modes, l_ref, dinv_ref, lm_ref, dm_ref, lo_ref, do_ref, mend_ref, zs
):
    def mode(which, t):
        return modes[which, t:t + 1, :]

    def body(c, carry):
        part = pl.ds(c * FACTOR_ROWS, FACTOR_ROWS)
        alpha = alpha_ref[part, :]
        l, dinv, sent = {}, {}, {}
        for t in range(HALF):
            a = [coefficient(bands, alpha, 1, t, d) for d in range(min(BAND, t) + 1)]
            l[t], dinv[t] = eliminate(a, l, dinv, t)
            sent[t] = jnp.broadcast_to(mode(2, t), alpha.shape)
            for d in l[t]:
                sent[t] = sent[t] - l[t][d] * sent[t - d]
            if t >= TOP:
                for d in range(1, BAND + 1):
                    lo_ref[t - TOP, d - 1, part, :] = l[t][d]
                do_ref[t - TOP, part, :] = dinv[t]
        outer = {}
        for j in range(BAND):
            t = HALF + j
            a = [coefficient(bands, alpha, 1, t, d) for d in range(BAND + 1)]
            outer[j] = row_weights(a, l, t, j + 1)
            l[t] = {d: outer[j][d] * dinv[t - d] for d in outer[j]}
            for d in l[t]:
                lo_ref[BAND + j, d - 1, part, :] = l[t][d]
        schur = {}
        for j in range(BAND):
            for i in range(j + 1):
                total = None
                for s in range(TOP + j, HALF):
                    term = outer[j][HALF + j - s] * l[HALF + i][HALF + i - s]
                    total = term if total is None else total + term
                schur[(j, i)] = schur[(i, j)] = total
        shift = {}
        for j in range(BAND):
            for d in range(j + 1, BAND + 1):
                term = l[HALF + j][d] * sent[HALF + j - d]
                shift[j] = term if j not in shift else shift[j] + term
        z = {}
        for t in range(TOP):
            z[t] = jnp.broadcast_to(mode(1, t), alpha.shape)
            for d in range(1, min(BAND, t) + 1):
                z[t] = z[t] - l_ref[t, d - 1, part, :] * z[t - d]
            zs[t] = z[t]
        l = {
            t: {d: l_ref[t, d - 1, part, :] for d in range(1, BAND + 1)} for t in range(TOP - BAND, TOP)
        }
        dinv = {t: dinv_ref[t, part, :] for t in range(TOP - BAND, TOP)}
        for t in range(TOP, HALF):
            a = [coefficient(bands, alpha, 0, t, d) for d in range(BAND + 1)]
            j = HALF - 1 - t
            for d in range(t - TOP + 1):
                a[d] = a[d] - schur[(j, j + d)]
            l[t], dinv[t] = eliminate(a, l, dinv, t)
            for d in range(1, BAND + 1):
                lm_ref[t - TOP, d - 1, part, :] = l[t][d]
            dm_ref[t - TOP, part, :] = dinv[t]
            z[t] = mode(1, t) - shift[j]
            for d in range(1, BAND + 1):
                z[t] = z[t] - l[t][d] * z[t - d]
        exact = 1.0 / (alpha + modes[3, 0:1, :])
        y, miss, norm = {}, jnp.zeros_like(alpha), jnp.zeros_like(modes[3, 0:1, :])
        for t in range(HALF - 1, -1, -1):
            y[t] = z[t] * dinv[t] if t >= TOP else zs[t] * dinv_ref[t, part, :]
            for d in range(1, min(BAND, HALF - 1 - t) + 1):
                factor = l[t + d][d] if t + d >= TOP else l_ref[t + d, d - 1, part, :]
                y[t] = y[t] - factor * y[t + d]
            miss = miss + mode(1, t) * (mode(0, t) * exact - y[t])
            norm = norm + mode(1, t) * mode(0, t)
        mend_ref[part, :] = jnp.where(norm > 0.01, miss / jnp.maximum(norm, 0.01), 0.0)
        return carry

    lax.fori_loop(0, N // FACTOR_ROWS, body, 0)


def four(get):
    return [get(side, who) for side in range(2) for who in range(2)]


def vertical_apply(products, vert, scal_k, scal_m, scal_v):
    mass = [k * p[:, :N] + m * p[:, N:] for p, k, m in zip(products, scal_k, scal_m)]
    stiff = [v * p[:, :N] for p, v in zip(products, scal_v)]
    out = dot_full(vert[0], jnp.concatenate(mass, axis=1))
    out = out + dot_full(vert[1], jnp.concatenate(stiff, axis=1))
    return [out[:, q * N:(q + 1) * N] for q in range(len(products))]


def plane_products(faces, mk):
    stacked = dot_full(jnp.concatenate(faces, axis=0), mk[...])
    return [stacked[q * ROWS:(q + 1) * ROWS] for q in range(len(faces))]


def flip_masks(scal, nscal):
    return [scal[side, 3:4, :] != nscal[side, 3:4, :] for side in range(2)]


def orient_all(arrays, mirror, masks):
    turned = dot_full(jnp.concatenate([a for _, a in arrays], axis=0), mirror[...])
    return [
        jnp.where(masks[side], turned[q * ROWS:(q + 1) * ROWS], a)
        for q, (side, a) in enumerate(arrays)
    ]


def update_faces(c_faces, state, scal, nscal, mirror, mk, vert):
    masks = flip_masks(scal, nscal)
    residual = four(lambda side, who: state[4][2 * side + who])
    arrays = []
    for side in range(2):
        for who in range(2):
            arrays.append((side, c_faces[2 * side + 1 - who]))
    for side in range(2):
        for who in range(2):
            arrays.append((side, residual[2 * side + 1 - who]))
    turned = orient_all(arrays, mirror, masks)
    e, added = turned[:4], turned[4:]
    products = plane_products(e, mk)
    which = four(lambda side, who: (nscal if who else scal)[side])
    applied = vertical_apply(
        products, vert, [w[0:1] for w in which], [w[1:2] for w in which], [w[2:3] for w in which]
    )
    new = [list(state[s]) for s in range(6)]
    for q in range(4):
        new[2][q] = state[2][q] + DAMPING * (c_faces[q] + e[q])
        new[3][q] = state[3][q] + DAMPING * (residual[q] + added[q] + applied[q])
        new[4][q] = state[0][q] - state[1][q] * new[2][q] - new[3][q]
        new[5][q] = KEEP * state[5][q] + DAMPING * e[q]
    return new, e, masks


def read_state(ref):
    return [[ref[s, q] for q in range(4)] for s in range(6)]


def pad_rows(x):
    return jnp.concatenate([x, jnp.zeros((ROWS - x.shape[0], N), F32)], axis=0)


def eliminate_forward(gh_ref, spread, rows_hat, l_ref, modes, z_ref, msg_ref, low_ref, core):
    def body(c, carry):
        part = pl.ds(pl.multiple_of(c * CHUNK, CHUNK), CHUNK)
        west, east = spread[0, part, :], spread[1, part, :]
        z = {}
        lowest = jnp.zeros_like(west)
        for t in range(HALF):
            x = gh_ref[t, part, :] + west * rows_hat[0, t:t + 1, :] + east * rows_hat[1, t:t + 1, :]
            lowest = lowest + modes[0, t:t + 1, :] * x
            z_ref[t, part, :] = x
            for d in range(min(BAND, t), 0, -1):
                x = x - l_ref[t, d - 1, part, :] * z[t - d]
            z[t] = x
            if t < TOP:
                z_ref[t, part, :] = x
        low_ref[part, :] = lowest

        @pl.when(c == core)
        def _():
            there = pl.ds(0, CHUNK)
            for s in range(BAND):
                msg_ref[s, there, :] = z[TOP + s]
            msg_ref[BAND, there, :] = lowest

        return carry

    lax.fori_loop(0, N // CHUNK, body, 0)


def first_kernel(
    ints, gh, own_pay, rec, scal, spread, b_full, mirror, l_ref, modes,
    z_ref, msg_ref, low_ref, state_ref, rows_u, rows_g, rows_hat,
):
    received = (rec[0], rec[1])
    masks = [received[side][ROWS:ROWS + 1] != scal[side, 3:4, :] for side in range(2)]
    state_ref[...] = jnp.zeros_like(state_ref)
    for side in range(2):
        for who in range(2):
            values = received[side][:ROWS] if who else own_pay[side, :ROWS]
            state_ref[0, 2 * side + who] = values
            state_ref[4, 2 * side + who] = values
    turned = orient_all([(side, received[side][:ROWS]) for side in range(2)], mirror, masks)
    rows_u[...] = jnp.zeros_like(rows_u)
    for side in range(2):
        rows_g[side] = turned[side]
        rows_hat[side] = dot_full(turned[side], b_full[...])
    eliminate_forward(gh, spread, rows_hat, l_ref, modes, z_ref, msg_ref, low_ref, ints[3])


def next_kernel(
    ints, gh, own_pay, rec, state_in, scal, nscal, spread, b_full, mirror, mk, vert,
    l_ref, modes, z_ref, msg_ref, low_ref, state_ref, rows_u, rows_g, rows_hat,
):
    received = (rec[0], rec[1])
    state = read_state(state_in)
    if own_pay.shape[1] > ROWS:
        for side in range(2):
            state[1][2 * side] = pad_rows(own_pay[side, ROWS:ROWS + HALF])
            state[1][2 * side + 1] = pad_rows(received[side][ROWS:ROWS + HALF])
    c_faces = four(lambda side, who: received[side][:ROWS] if who else own_pay[side, :ROWS])
    state, e, masks = update_faces(c_faces, state, scal, nscal, mirror, mk, vert)
    for s in range(6):
        for q in range(4):
            state_ref[s, q] = state[s][q]
    turned = orient_all([(side, state[4][2 * side + 1]) for side in range(2)], mirror, masks)
    for side in range(2):
        step = DAMPING * e[2 * side]
        rows = turned[side] - state[1][2 * side] * step
        rows_u[side] = step
        rows_g[side] = rows
        rows_hat[side] = dot_full(rows, b_full[...])
    eliminate_forward(gh, spread, rows_hat, l_ref, modes, z_ref, msg_ref, low_ref, ints[3])


def solve_kernel(
    ints, z_ref, low_ref, zr_ref, l_ref, dinv_ref, lm_ref, dm_ref, lo_ref, do_ref, mend, modes, spread, bt_full, state, *refs,
):
    extra, (y_ref, pay_ref, slot_ref, sums) = refs[:-4], refs[-4:]
    sums[...] = jnp.zeros_like(sums)

    def body(c, carry):
        part = pl.ds(pl.multiple_of(c * CHUNK, CHUNK), CHUNK)
        source = c
        if zr_ref.shape[0] > 2:
            source = source + 2 * (1 - ints[2])
        there = pl.ds(0, CHUNK)
        sent = [zr_ref[source, s, there, :] for s in range(BAND)]
        weights = (spread[0, part, :], spread[1, part, :])

        low = mend[part, :] * (low_ref[part, :] + zr_ref[source, BAND, there, :])

        def put(t, value):
            value = value + low * modes[0, t:t + 1, :]
            y_ref[t, part, :] = value
            for side in range(2):
                product = weights[side] * value
                total = product[0:8]
                for s in range(8, CHUNK, 8):
                    total = total + product[s:s + 8]
                sums[side, t] += total

        z = {t: z_ref[t, part, :] for t in range(TOP - BAND, HALF)}
        for j in range(BAND):
            for d in range(j + 1, BAND + 1):
                z[HALF - 1 - j] = z[HALF - 1 - j] - lo_ref[BAND + j, d - 1, part, :] * sent[BAND + j - d]
        for t in range(TOP, HALF):
            for d in range(BAND, 0, -1):
                z[t] = z[t] - lm_ref[t - TOP, d - 1, part, :] * z[t - d]

        def factor(t, d):
            return lm_ref[t - TOP, d - 1, part, :] if t >= TOP else l_ref[t, d - 1, part, :]

        y = {}
        for t in range(HALF - 1, TOP - 1, -1):
            value = z[t] * dm_ref[t - TOP, part, :]
            for d in range(HALF - 1 - t, 0, -1):
                value = value - factor(t + d, d) * y[t + d]
            y[t] = value
            put(t, value)
        far = {HALF + j: y[HALF - 1 - j] for j in range(BAND)}
        for t in range(HALF - 1, TOP - 1, -1):
            value = sent[t - TOP] * do_ref[t - TOP, part, :]
            for d in range(BAND, 0, -1):
                value = value - lo_ref[t + d - TOP, d - 1, part, :] * far[t + d]
            far[t] = value
            put(2 * HALF - 1 - t, value)
        for t in range(TOP - 1, -1, -1):
            known = z[t] if t in z else z_ref[t, part, :]
            value = known * dinv_ref[t, part, :]
            for d in range(BAND, 0, -1):
                value = value - factor(t + d, d) * y[t + d]
            y[t] = value
            put(t, value)
        return carry

    lax.fori_loop(0, N // CHUNK, body, 0)
    mixed = jnp.sum(sums[...], axis=2)
    faces = dot_full(mixed.reshape(2 * ROWS, N), bt_full[...])
    packs = []
    for side in range(2):
        c = faces[side * ROWS:(side + 1) * ROWS] - state[2, 2 * side]
        pay_ref[side, :ROWS] = c
        if extra:
            pay_ref[side, ROWS:ROWS + HALF] = extra[0][side]
            pay_ref[side, ROWS + HALF:] = extra[1][side]
    slot(ints, pay_ref[0], pay_ref[1], slot_ref)


def back_planes(y, wbt, lb):
    count = y.shape[0]
    across = right_mul(y.reshape(count * N, N), wbt).reshape(count, N, N)
    return left_mul_planes(lb, [across[q] for q in range(count)])


def make_plane_kernel(sweep):
    last = sweep == SWEEPS - 1

    def kernel(ints, *refs):
        refs = list(refs)
        y_ref, f_ref, r_ref, rows_u, rows_g, mask, wbt, lb = refs[:8]
        refs = refs[8:]
        if sweep > 0:
            up_in, g_in = refs[:2]
            refs = refs[2:]
        if last:
            cut, pay_in = refs[:2]
            up_out, final_out, pay_out, slot_ref, sums = refs[2:]
        else:
            wb, lbt = refs[:2]
            up_out, g_out, gh_out = refs[2:]

        def on_faces(rows, t):
            return mask[0] * rows[0, pl.ds(t, 1), :] + mask[1] * rows[1, pl.ds(t, 1), :]

        def body(g, carry):
            t0 = g * GROUP
            corrections = back_planes(y_ref[pl.ds(t0, GROUP)], wbt[...], lb[...])
            fresh = []
            for q in range(GROUP):
                t = t0 + q
                on_u, on_g = on_faces(rows_u, t), on_faces(rows_g, t)
                load, react = f_ref[t], r_ref[t]
                if sweep == 0:
                    u, total = on_u, DAMPING * (load + on_g)
                else:
                    old = up_in[t]
                    u = old + on_u
                    total = KEEP * g_in[t] + DAMPING * (load - react * old + on_g)
                new = KEEP * u + DAMPING * corrections[q]
                if last:
                    block, index = source_layer(ints, t)

                    @pl.when(block == ints[3])
                    def _():
                        up_out[index] = new
                else:
                    up_out[t] = new
                residual = load - react * new
                if last:
                    residual = residual - total
                    for side in range(2):
                        product = cut[side] * residual
                        part = product[0:8]
                        for s in range(8, N, 8):
                            part = part + product[s:s + 8]
                        sums[side, t] = part
                else:
                    g_out[t] = total
                if last:
                    final_out[t] = residual
                fresh.append(residual)
            if not last:
                stacked = jnp.concatenate(fresh, axis=0).reshape(GROUP, N, N)
                planes = forward_planes(stacked, wb[...], lbt[...])
                for q in range(GROUP):
                    gh_out[t0 + q] = planes[q]
            return carry

        lax.fori_loop(0, HALF // GROUP, body, 0)
        if last:
            for side in range(2):
                pay_out[side, :ROWS] = pay_in[side, :ROWS]
                pay_out[side, ROWS:] = jnp.sum(sums[side], axis=1)
            slot(ints, pay_out[0], pay_out[1], slot_ref)

    return kernel


def restrict_kernel(ints, final, wrt, lr, kept, sent, plane):
    def body(g, carry):
        t0 = g * GROUP
        planes = forward_planes(final[pl.ds(t0, GROUP)], wrt[...], lr[...])
        for q in range(GROUP):
            plane[q] = planes[q]

        @pl.when(ints[1] == 1)
        def _():
            for q in range(GROUP):
                plane[q] = planes[q].T

        for half in range(2):
            for core in range(2):
                first = half * (COARSE // 2) + core * 31

                @pl.when((ints[2] == half) & (ints[3] == core))
                def _():
                    kept[pl.ds(t0, GROUP)] = plane[:, first:first + 32]

                @pl.when((ints[2] != half) & (ints[3] == core))
                def _():
                    sent[pl.ds(t0, GROUP)] = plane[:, first:first + 32]

        return carry

    lax.fori_loop(0, HALF // GROUP, body, 0)


def final_kernel(
    ints, floats, own_pay, rec, state_in, scal, nscal, mirror, mirror_coarse, mk, vert, rt_full, parts, rows_u,
):
    received = (rec[0], rec[1])
    state = read_state(state_in)
    c_faces = four(lambda side, who: received[side][:ROWS] if who else own_pay[side, :ROWS])
    state, e, masks = update_faces(c_faces, state, scal, nscal, mirror, mk, vert)
    gathered = state[5]
    products = plane_products(gathered, mk)
    far = vertical_apply(
        [products[1], products[3]], vert,
        [nscal[side, 4:5] for side in range(2)],
        [nscal[side, 5:6] for side in range(2)],
        [nscal[side, 6:7] for side in range(2)],
    )
    one = floats[0]
    near_stiff = vertical_apply([products[0], products[2]], vert, [one] * 2, [floats[3]] * 2, [floats[3]] * 2)
    near_mass = vertical_apply([products[0], products[2]], vert, [floats[3]] * 2, [floats[1]] * 2, [floats[2]] * 2)
    stack = []
    for side in range(2):
        nbr = 2 * side + 1
        theirs = pad_rows(received[side][ROWS:])
        theirs = theirs - nscal[side, 7:8] * DAMPING * state[1][nbr] * e[nbr] - far[side]
        mine = scal[side, 7:8] * DAMPING * state[1][2 * side] * e[2 * side]
        stack += [near_stiff[side], near_mass[side], mine, theirs]
    restricted = dot_full(jnp.concatenate(stack, axis=0), rt_full[...])
    pieces = [restricted[q * ROWS:(q + 1) * ROWS] for q in range(8)]
    turned = dot_full(jnp.concatenate([pieces[3], pieces[7]], axis=0), mirror_coarse[...])
    for side in range(2):
        added = jnp.where(masks[side], turned[side * ROWS:(side + 1) * ROWS], pieces[4 * side + 3])
        parts[3 * side] = -pieces[4 * side][:HALF]
        parts[3 * side + 1] = -pieces[4 * side + 1][:HALF]
        parts[3 * side + 2] = (added - pieces[4 * side + 2])[:HALF]
        rows_u[side] = DAMPING * e[2 * side]

def iterate_kernel(ints, up, rows_u, mask, out_u):
    def body(index, carry):
        inside = ints[3] * BLOCK + index
        t = jnp.where(ints[2] == 1, HALF - 1 - inside, inside)
        value = up[index] + mask[0] * rows_u[0, pl.ds(t, 1), :] + mask[1] * rows_u[1, pl.ds(t, 1), :]
        out_u[index] = value

        @pl.when(ints[1] == 1)
        def _():
            out_u[index] = value.T

        return carry

    lax.fori_loop(0, BLOCK, body, 0, unroll=2)


def coarse_kernel(
    ints, kept, arrived, parts, far_parts, profile, profile_rows, vertical, out, blocks, columns,
):
    deep = vertical.shape[0]
    spots = [0, 31, COARSE // 2, COARSE // 2 + 31]
    weights = vertical[...]
    stacked = [jnp.concatenate([parts[s], far_parts[s]], axis=0) for s in range(6)]
    mixed = dot_full(weights, jnp.concatenate(stacked, axis=1))
    mixed = [mixed[:, s * N:(s + 1) * N] for s in range(6)]
    for c in range(32):
        rows = pl.ds(c, HALF, stride=32)
        both = jnp.concatenate([kept[rows, :], arrived[rows, :]], axis=0)
        blocks[c] = dot_full(weights, both)

    @pl.when(ints[1] == 0)
    def _():
        first = ints[2] * (COARSE // 2) + ints[3] * 31

        def body(c, carry):
            value = blocks[c]
            for s in range(6):
                value = value + profile[s, pl.ds(first + c, 1), :] * mixed[s]
            blocks[c] = value
            return carry

        lax.fori_loop(0, 32, body, 0)

    @pl.when(ints[1] == 1)
    def _():
        for half in range(2):
            for core in range(2):
                shift = (N - spots[2 * half + core]) % N

                @pl.when((ints[2] == half) & (ints[3] == core))
                def _():
                    for s in range(6):
                        columns[s] = pltpu.roll(mixed[s], shift, 1) if shift else mixed[s]

        for c in range(32):
            value = blocks[c]
            for s in range(6):
                value = value + columns[s, :, c:c + 1] * profile_rows[s:s + 1, :]
            blocks[c] = value

    share = out.shape[1]
    lane = lax.broadcasted_iota(jnp.int32, (deep, N), 1)
    for core in range(2):

        @pl.when(ints[3] == core)
        def _():
            start = core * (COARSE // 2)
            held = {}

            def turned(c):
                if c not in held:
                    shift = (c * COARSE - start) % N
                    held[c] = pltpu.roll(blocks[c], shift, 1) if shift else blocks[c]
                return held[c]

            for tile in range(-(-share // N)):
                low = tile * N + start
                c = low // COARSE
                value = turned(c)
                after = (c + 1) * COARSE - low
                if after < N and c + 1 < 32:
                    value = jnp.where(lane < after, value, turned(c + 1))
                if after + COARSE < N and c + 2 < 32:
                    value = jnp.where(lane < after + COARSE, value, turned(c + 2))
                width = min(N, share - tile * N)
                out[:, tile * N:tile * N + width] = value[:, :width]


def prepare_kernel(
    ints, floats, stiff, mass, stiff_v, mass_v, basis, eigen, basis_v, eigen_v, restrict, restrict_v,
    wb, wbt, wrt, lb, lbt, lr, bt_out, rt_out, mk, mirror, mirror_coarse, vert, scal, spread, mask, cut,
    profile, profile_rows, alpha, bands, modes, vertical,
):
    a1, a2, a3 = floats[0], floats[1], floats[2]
    rows = lax.broadcasted_iota(jnp.int32, (N, N), 0)
    lanes = lax.broadcasted_iota(jnp.int32, (N, N), 1)
    eye = rows == lanes

    def column(row):
        picked = jnp.sum(jnp.where(eye, row, 0.0), axis=1, keepdims=True)
        return jnp.broadcast_to(picked, (N, N))

    b, k, m = basis[...], stiff[...], mass[...]
    bt = b.T
    r = jnp.concatenate([restrict[...], jnp.zeros((N - COARSE, N), F32)], axis=0)
    rt = r.T
    wb[...], wbt[...], wrt[...] = pack_right(b), pack_right(bt), pack_right(rt)
    lb[...], lbt[...], lr[...] = pack_left(b), pack_left(bt), pack_left(r)
    bt_out[...], rt_out[...] = bt, rt
    mk[:, :N], mk[:, N:] = m, k
    mirror[...] = (rows + lanes == N - 1).astype(F32)
    mirror_coarse[...] = (rows + lanes == COARSE - 1).astype(F32)
    alpha[...] = a1 * column(eigen[...]) + a2 * eigen[...]

    turn = (
        lax.broadcasted_iota(jnp.int32, (LAYERS, LAYERS), 0)
        + lax.broadcasted_iota(jnp.int32, (LAYERS, LAYERS), 1)
        == LAYERS - 1
    ).astype(F32)
    first = ints[2] == 0
    kv, mv = stiff_v[...], mass_v[...]
    ordered = []
    for matrix in (mv, a3 * kv):
        turned = dot_full(dot_full(turn, matrix), turn)
        ordered.append((jnp.where(first, matrix, turned), jnp.where(first, turned, matrix)))
    deep = lax.broadcasted_iota(jnp.int32, (ROWS, LAYERS), 0)
    wide = lax.broadcasted_iota(jnp.int32, (ROWS, LAYERS), 1)
    inside = (deep < HALF) & (wide < REACH)
    own_stiff = jnp.where(first, kv, dot_full(dot_full(turn, kv), turn))
    vert[0] = jnp.where(inside, ordered[0][0][:ROWS], 0.0)[:, :ROWS]
    vert[1] = jnp.where(inside, own_stiff[:ROWS], 0.0)[:, :ROWS]
    for which in range(2):
        for s in range(2):
            for d in range(BAND + 1):
                picked = jnp.where(deep - wide == d, ordered[s][which][:ROWS], 0.0)
                bands[which, s, d] = jnp.broadcast_to(jnp.sum(picked, axis=1, keepdims=True), (ROWS, N))

    rv = restrict_v[...]
    backwards = dot_full(rv, turn)
    vertical[:, :HALF] = jnp.where(first, rv, backwards)[:, :HALF]
    vertical[:, HALF:] = jnp.where(first, backwards, rv)[:, :HALF]

    mu = eigen_v[...]
    least = jnp.min(mu, axis=1, keepdims=True)
    number = lax.broadcasted_iota(jnp.int32, (1, LAYERS), 1)
    chosen = jnp.min(jnp.where(mu == least, number, LAYERS), axis=1, keepdims=True)
    low = jnp.sum(jnp.where(number == chosen, basis_v[...], 0.0), axis=1, keepdims=True)
    low = jnp.broadcast_to(low, (LAYERS, N))
    low_mass = dot_full(mv, low)
    low_turned, mass_turned = dot_full(turn, low), dot_full(turn, low_mass)
    modes[0] = jnp.where(first, low, low_turned)[:ROWS]
    modes[1] = jnp.where(first, low_mass, mass_turned)[:ROWS]
    modes[2] = jnp.where(first, mass_turned, low_mass)[:ROWS]
    modes[3] = jnp.broadcast_to(a3 * least, (ROWS, N))

    for side in range(2):
        start = ints[4 + side] == 0

        def end_row(matrix, count=N):
            return jnp.where(start, matrix[0:1, :], matrix[count - 1:count, :])

        def corner(matrix):
            value = jnp.where(start, matrix[0:1, 0:1], matrix[N - 1:N, N - 1:N])
            return jnp.broadcast_to(value, (1, N))

        cut_row = end_row(r, COARSE)
        cut_at = jnp.broadcast_to(jnp.where(start, cut_row[:, 0:1], cut_row[:, N - 1:N]), (1, N))
        stiff_profile = jnp.broadcast_to(jnp.sum(r * end_row(k), axis=1, keepdims=True), (N, N))
        mass_profile = jnp.broadcast_to(jnp.sum(r * end_row(m), axis=1, keepdims=True), (N, N))
        at_face = jnp.where(start, 0, COARSE - 1)
        at_rows = [stiff_profile, mass_profile, (rows == at_face).astype(F32)]
        for s in range(3):
            turned_row = jnp.sum(jnp.where(eye, at_rows[s], 0.0), axis=0, keepdims=True)
            profile_rows[3 * side + s:3 * side + s + 1, :] = turned_row
        profile[3 * side] = stiff_profile
        profile[3 * side + 1] = mass_profile
        profile[3 * side + 2] = (rows == at_face).astype(F32)
        spread[side] = column(end_row(b))
        mask[side] = (rows == ints[4 + side]).astype(F32)
        cut[side] = column(cut_row)
        scal[side] = jnp.concatenate(
            [
                corner(k) * a1,
                corner(m) * a2,
                corner(m) * a3,
                jnp.broadcast_to(ints[0].astype(F32), (1, N)),
                end_row(stiff_profile, COARSE) * a1,
                end_row(mass_profile, COARSE) * a2,
                end_row(mass_profile, COARSE) * a3,
                cut_at,
            ],
            axis=0,
        )


def per_device(
    load_vector,
    reaction,
    geometry,
    stiff_plane,
    mass_plane,
    stiff_vertical,
    mass_vertical,
    basis_plane,
    eigen_plane,
    basis_vertical,
    eigen_vertical,
    restrict_plane,
    restrict_vertical,
    patch_links,
):
    patches = lax.axis_size("patch")
    links = patch_links
    square, two = (N, N), (2, N, N)
    right = jax.ShapeDtypeStruct((2 * N, 2 * N), BF16)
    left = jax.ShapeDtypeStruct((N, 2 * N), BF16)
    (
        wb, wbt, wrt, lb, lbt, lr, basis_t, restrict_t, mk, mirror, mirror_coarse, vert, scal, spread, mask,
        cut, profile, profile_rows, alpha, bands, modes, vertical,
    ) = call(
        prepare_kernel,
        [
            right, right, right, left, left, left, square, square, (N, 2 * N), square, square,
            (2, ROWS, ROWS), (2, 8, N), two, two, two, (6, N, N), (8, N), square, (2, 2, BAND + 1, ROWS, N), (4, ROWS, N),
            restrict_vertical.shape,
        ],
        links, stiff_plane, mass_plane, stiff_vertical, mass_vertical, basis_plane, eigen_plane.reshape(1, N),
        basis_vertical, eigen_vertical.reshape(1, LAYERS), restrict_plane, restrict_vertical,
        geometry=geometry, flops=20_000_000,
    )

    pair = [(0, 1), (1, 0), (2, 3), (3, 2)]
    cross = [(0, 2), (2, 0), (1, 3), (3, 1)]
    chips = [[0, 1], [2, 3]]
    faces = []
    for p in range(patches):
        for h in range(2):
            west, east = 4 * p + 2 * h + 1, 4 * ((p + 1) % patches) + 2 * h
            faces += [(west, east), (east, west)]

    def swap_faces(slot_values):
        arrived = lax.ppermute(slot_values, ("patch", "slab"), faces)
        return lambda: lax.all_gather(arrived, "slab", axis_index_groups=chips)

    field = (HALF, N, N)
    own_load = load_vector[0].reshape(BLOCK, N, N)
    own_react = reaction[0].reshape(BLOCK, N, N)
    other_load = lax.ppermute(own_load, "slab", pair)
    other_react = lax.ppermute(own_react, "slab", pair)
    size = ROWS + 8
    f, pay, slot_values = call(
        load_kernel, [field, (2, size, N), (size, N)], links, own_load, other_load
    )
    arriving = swap_faces(slot_values)
    l, dinv = call(
        factor_kernel, [(HALF, BAND, N, N), field], links, slot_values, alpha, bands, flops=3_000_000_000
    )
    (gh,) = call(transform_kernel, [field], links, f, wb, lbt, flops=2_000_000_000)
    rec = arriving()
    rows_hat = pltpu.VMEM((2, ROWS, N), F32)
    sums = pltpu.VMEM((2, ROWS, 8, N), F32)
    message = (BAND + 1, N // 2, N)
    message_full = (BAND, N, N)
    state_shape = (6, 4, ROWS, N)
    rows_shape = (2, ROWS, N)
    up = total = None
    for sweep in range(SWEEPS):
        if sweep == 0:
            z, msg, low, state, rows_u, rows_g = call(
                first_kernel,
                [field, message, square, state_shape, rows_shape, rows_shape],
                links, gh, pay, rec, scal, spread, basis_plane, mirror, l, modes,
                scratch=[rows_hat], flops=10_000_000,
            )
        else:
            if sweep == 1:
                nscal = rec[:, ROWS + HALF:]
            z, msg, low, state, rows_u, rows_g = call(
                next_kernel,
                [field, message, square, state_shape, rows_shape, rows_shape],
                links, gh, pay, rec, state, scal, nscal, spread, basis_plane, mirror, mk, vert, l, modes,
                scratch=[rows_hat], flops=10_000_000,
            )
        if sweep > 0:
            received = lax.all_gather(msg, "slab")
        else:
            crossing = lax.ppermute(msg, "slab", cross)
            r, react_faces = call(reaction_kernel, [field, (2, HALF, N)], links, msg, own_react, other_react)
            lm, dm, lo, do, mend = call(
                meet_kernel,
                [(BAND, BAND, N, N), message_full, (2 * BAND, BAND, N, N), message_full, square],
                links, alpha, bands, modes, l, dinv,
                scratch=[pltpu.VMEM((TOP, FACTOR_ROWS, N), F32)], flops=5_000_000_000,
            )
            received = lax.all_gather(crossing, "slab", axis_index_groups=chips)
        last = sweep == SWEEPS - 1
        size = ROWS + HALF + 8 if sweep == 0 else ROWS
        extra = [react_faces, scal] if sweep == 0 else []
        y, pay, slot_values = call(
            solve_kernel,
            [(REACH, N, N), (2, size, N), (size, N)],
            links, z, low, received, l, dinv, lm, dm, lo, do, mend, modes, spread, basis_t, state, *extra,
            scratch=[sums], flops=10_000_000,
        )
        args = [y, f, r, rows_u, rows_g, mask, wbt, lb]
        if sweep > 0:
            args += [up, total]
        plane_kernel = make_plane_kernel(sweep)
        if last:
            size = ROWS + HALF
            block = (HALF, 32, N)
            up, final, pay, slot_values = call(
                plane_kernel,
                [(BLOCK, N, N), field, (2, size, N), (size, N)],
                links, *args, cut, pay,
                scratch=[pltpu.VMEM((2, HALF, 8, N), F32)], flops=3_000_000_000,
            )
            arriving = swap_faces(slot_values)
            kept, sent = call(
                restrict_kernel, [block, block], links, final, wrt, lr,
                scratch=[pltpu.VMEM((GROUP, N, N), F32)], flops=3_000_000_000,
            )
            arrived = lax.ppermute(sent, "slab", cross)
            rec = arriving()
        else:
            arriving = swap_faces(slot_values)
            up, total, gh = call(
                plane_kernel, [field, field, field], links, *args, wb, lbt, flops=4_000_000_000
            )
            rec = arriving()
    parts, rows_u = call(
        final_kernel,
        [(6, HALF, N), rows_shape],
        links, pay, rec, state, scal, nscal, mirror, mirror_coarse, mk, vert, restrict_t,
        geometry=geometry, flops=80_000_000_000,
    )
    far_parts = lax.ppermute(parts, "slab", cross)
    (out_u,) = call(iterate_kernel, [(BLOCK, N, N)], links, up, rows_u, mask, flops=2_000_000_000)
    deep = restrict_vertical.shape[0]
    share = COARSE * COARSE // 4
    (flat,) = call(
        coarse_kernel,
        [(deep, share)],
        links, kept.reshape(HALF * 32, N), arrived.reshape(HALF * 32, N), parts, far_parts,
        profile, profile_rows, vertical,
        scratch=[pltpu.VMEM((32, deep, N), F32), pltpu.VMEM((6, deep, N), F32)],
        flops=10_000_000,
    )
    return out_u.reshape(1, BLOCK, N * N), flat[None]


def solution(mesh):
    in_specs = (
        P("patch", "slab", None),
        P("patch", "slab", None),
        P("patch", None),
        P(), P(), P(), P(), P(), P(), P(), P(), P(), P(),
        P("patch", None),
    )
    out_specs = (P("patch", "slab", None), P("patch", None, "slab"))
    return jax.shard_map(
        per_device, mesh=mesh, in_specs=in_specs, out_specs=out_specs, check_vma=False
    )
```

```python
import jax
import jax.numpy as jnp
from jax import lax
from jax.experimental import pallas as pl
from jax.experimental.pallas import tpu as pltpu
from jax.sharding import PartitionSpec as P

BAND = 4
SWEEPS = 3
DAMPING = 0.25
KEEP = 1.0 - DAMPING
HIGHEST = lax.Precision.HIGHEST
F32 = jnp.float32
BF16 = jnp.bfloat16

N = 128
LAYERS = 64
HALF = 32
BLOCK = 16
REACH = HALF + BAND
ROWS = 40
TOP = HALF - BAND
CHUNK = 32
COARSE = N - 2


def split(x):
    high = x.astype(BF16)
    return high, (x - high.astype(F32)).astype(BF16)


def right_mul(x, packed):
    high, low = split(x)
    both = jnp.dot(jnp.concatenate([high, low], axis=-1), packed, preferred_element_type=F32)
    return both[:, :N] + both[:, N:]


def left_mul_planes(packed, planes):
    out = []
    for q in range(0, len(planes), 2):
        high, low = split(jnp.concatenate(planes[q:q + 2], axis=1))
        wide = jnp.dot(packed, jnp.concatenate([high, high], axis=0), preferred_element_type=F32)
        wide = wide + jnp.dot(packed[:, :N], low, preferred_element_type=F32)
        out += [wide[:, :N], wide[:, N:]]
    return out


def dot_full(x, y):
    return jnp.dot(x, y, precision=HIGHEST, preferred_element_type=F32)


def mirrored(x, mirror):
    high, rest = split(x)
    middle, low = split(x - high.astype(F32))
    return jnp.dot(
        jnp.concatenate([high, middle, low], axis=-1), mirror, preferred_element_type=F32
    )


def pack_right(a):
    high, low = split(a)
    top = jnp.concatenate([high, low], axis=1)
    bottom = jnp.concatenate([high, jnp.zeros_like(low)], axis=1)
    return jnp.concatenate([top, bottom], axis=0)


def pack_left(a):
    return jnp.concatenate(split(a), axis=1)


def call(kernel, outs, links, *args, flops=0, scratch=(), geometry=None):
    smem = [links] if geometry is None else [links, geometry]
    specs = [pl.BlockSpec(memory_space=pltpu.SMEM)] * len(smem)
    specs += [pl.BlockSpec(memory_space=pltpu.VMEM)] * len(args)
    shapes = [s if isinstance(s, jax.ShapeDtypeStruct) else jax.ShapeDtypeStruct(s, F32) for s in outs]
    moved = sum(a.size * a.dtype.itemsize for a in args) + sum(4 * s.size for s in shapes)

    def body(links_ref, *refs):
        ints = facts(links_ref)
        if geometry is None:
            kernel(ints, *refs)
        else:
            kernel(ints, scales(ints, refs[0]), *refs[1:])

    return pl.pallas_call(
        body,
        out_shape=shapes,
        in_specs=specs,
        out_specs=[pl.BlockSpec(memory_space=pltpu.VMEM)] * len(outs),
        scratch_shapes=list(scratch),
        compiler_params=pltpu.CompilerParams(vmem_limit_bytes=16 * 1024 * 1024),
        cost_estimate=pl.CostEstimate(
            flops=flops, bytes_accessed=moved, transcendentals=0
        ),
    )(*smem, *args)


def facts(links):
    slab = lax.axis_index("slab")
    west, east = links[0, 0], links[0, 1]
    return (
        links[0, 2], jnp.right_shift(west, 1), jnp.right_shift(slab, 1), jnp.bitwise_and(slab, 1),
        (N - 1) * jnp.bitwise_and(west, 1), (N - 1) * jnp.bitwise_and(east, 1),
    )


def scales(ints, geometry):
    turned = ints[1] == 1
    first, second = geometry[0, 0], geometry[0, 1]
    return (
        jnp.where(turned, second, first), jnp.where(turned, first, second), geometry[0, 2], jnp.float32(0),
    )


def source_layer(ints, t):
    inside = jnp.where(ints[2] == 1, HALF - 1 - t, t)
    return jnp.right_shift(inside, 4), jnp.bitwise_and(inside, BLOCK - 1)


def load_layers(ints, own_ref, other_ref, out_ref):
    def run(turn):
        def body(g, carry):
            for q in range(8):
                t = g * 8 + q
                block, index = source_layer(ints, t)
                value = jnp.where(block == ints[3], own_ref[index], other_ref[index])
                out_ref[t] = value.T if turn else value
            return carry

        lax.fori_loop(0, HALF // 8, body, 0)

    @pl.when(ints[1] == 0)
    def _():
        run(False)

    @pl.when(ints[1] == 1)
    def _():
        run(True)


def slot(ints, west, east, slot_ref):
    slot_ref[...] = jnp.where(ints[3] == 0, west, east)


def face_rows(ints, ref, side):
    position = ints[4 + side]
    return jnp.where(position == 0, ref[:, 0, :], ref[:, N - 1, :])


def load_kernel(ints, own, other, f_ref, pay_ref, slot_ref):
    load_layers(ints, own, other, f_ref)
    flag = jnp.broadcast_to(ints[0].astype(F32), (8, N))
    for side in range(2):
        rows = face_rows(ints, f_ref, side)
        pay_ref[side] = jnp.concatenate([rows, jnp.zeros((ROWS - HALF, N), F32), flag], axis=0)
    slot(ints, pay_ref[0], pay_ref[1], slot_ref)


def reaction_kernel(ints, ready, own, other, r_ref, face_ref):
    load_layers(ints, own, other, r_ref)
    for side in range(2):
        face_ref[side] = face_rows(ints, r_ref, side)


def forward_planes(x, wb, lbt):
    count = x.shape[0]
    first = right_mul(x.reshape(count * N, N), wb).reshape(count, N, N)
    return left_mul_planes(lbt, [first[q] for q in range(count)])


GROUP = 32


def transform_kernel(ints, f_ref, wb, lbt, out_ref):
    def body(g, carry):
        t = g * GROUP
        planes = forward_planes(f_ref[pl.ds(t, GROUP)], wb[...], lbt[...])
        for q in range(GROUP):
            out_ref[t + q] = planes[q]
        return carry

    lax.fori_loop(0, HALF // GROUP, body, 0)


FACTOR_ROWS = 16


def coefficient(bands, alpha, which, t, d):
    return alpha * bands[which, 0, d, t:t + 1, :] + bands[which, 1, d, t:t + 1, :]


def row_weights(a, l, t, least):
    w = {}
    for d in range(min(BAND, t), least - 1, -1):
        v = a[d]
        for m in range(d + 1, min(BAND, t) + 1):
            v = v - w[m] * l[t - d][m - d]
        w[d] = v
    return w


def eliminate(a, l, dinv, t):
    w = row_weights(a, l, t, 1)
    row = {d: w[d] * dinv[t - d] for d in w}
    pivot = a[0]
    for d in w:
        pivot = pivot - w[d] * row[d]
    return row, 1.0 / pivot


def factor_kernel(ints, ready, alpha_ref, bands, l_ref, dinv_ref):
    def body(c, carry):
        part = pl.ds(c * FACTOR_ROWS, FACTOR_ROWS)
        alpha = alpha_ref[part, :]
        l, dinv = {}, {}
        for t in range(HALF):
            a = [coefficient(bands, alpha, 0, t, d) for d in range(min(BAND, t) + 1)]
            l[t], dinv[t] = eliminate(a, l, dinv, t)
            for d in l[t]:
                l_ref[t, d - 1, part, :] = l[t][d]
            dinv_ref[t, part, :] = dinv[t]
        return carry

    lax.fori_loop(0, N // FACTOR_ROWS, body, 0)


def meet_kernel(
    ints, alpha_ref, bands, modes, l_ref, dinv_ref, lm_ref, dm_ref, lo_ref, do_ref, mend_ref, zs
):
    def mode(which, t):
        return modes[which, t:t + 1, :]

    def body(c, carry):
        part = pl.ds(c * FACTOR_ROWS, FACTOR_ROWS)
        alpha = alpha_ref[part, :]
        l, dinv, sent = {}, {}, {}
        for t in range(HALF):
            a = [coefficient(bands, alpha, 1, t, d) for d in range(min(BAND, t) + 1)]
            l[t], dinv[t] = eliminate(a, l, dinv, t)
            sent[t] = jnp.broadcast_to(mode(2, t), alpha.shape)
            for d in l[t]:
                sent[t] = sent[t] - l[t][d] * sent[t - d]
            if t >= TOP:
                for d in range(1, BAND + 1):
                    lo_ref[t - TOP, d - 1, part, :] = l[t][d]
                do_ref[t - TOP, part, :] = dinv[t]
        outer = {}
        for j in range(BAND):
            t = HALF + j
            a = [coefficient(bands, alpha, 1, t, d) for d in range(BAND + 1)]
            outer[j] = row_weights(a, l, t, j + 1)
            l[t] = {d: outer[j][d] * dinv[t - d] for d in outer[j]}
            for d in l[t]:
                lo_ref[BAND + j, d - 1, part, :] = l[t][d]
        schur = {}
        for j in range(BAND):
            for i in range(j + 1):
                total = None
                for s in range(TOP + j, HALF):
                    term = outer[j][HALF + j - s] * l[HALF + i][HALF + i - s]
                    total = term if total is None else total + term
                schur[(j, i)] = schur[(i, j)] = total
        shift = {}
        for j in range(BAND):
            for d in range(j + 1, BAND + 1):
                term = l[HALF + j][d] * sent[HALF + j - d]
                shift[j] = term if j not in shift else shift[j] + term
        z = {}
        for t in range(TOP):
            z[t] = jnp.broadcast_to(mode(1, t), alpha.shape)
            for d in range(1, min(BAND, t) + 1):
                z[t] = z[t] - l_ref[t, d - 1, part, :] * z[t - d]
            zs[t] = z[t]
        l = {
            t: {d: l_ref[t, d - 1, part, :] for d in range(1, BAND + 1)} for t in range(TOP - BAND, TOP)
        }
        dinv = {t: dinv_ref[t, part, :] for t in range(TOP - BAND, TOP)}
        for t in range(TOP, HALF):
            a = [coefficient(bands, alpha, 0, t, d) for d in range(BAND + 1)]
            j = HALF - 1 - t
            for d in range(t - TOP + 1):
                a[d] = a[d] - schur[(j, j + d)]
            l[t], dinv[t] = eliminate(a, l, dinv, t)
            for d in range(1, BAND + 1):
                lm_ref[t - TOP, d - 1, part, :] = l[t][d]
            dm_ref[t - TOP, part, :] = dinv[t]
            z[t] = mode(1, t) - shift[j]
            for d in range(1, BAND + 1):
                z[t] = z[t] - l[t][d] * z[t - d]
        exact = 1.0 / (alpha + modes[3, 0:1, :])
        y, miss, norm = {}, jnp.zeros_like(alpha), jnp.zeros_like(modes[3, 0:1, :])
        for t in range(HALF - 1, -1, -1):
            y[t] = z[t] * dinv[t] if t >= TOP else zs[t] * dinv_ref[t, part, :]
            for d in range(1, min(BAND, HALF - 1 - t) + 1):
                factor = l[t + d][d] if t + d >= TOP else l_ref[t + d, d - 1, part, :]
                y[t] = y[t] - factor * y[t + d]
            miss = miss + mode(1, t) * (mode(0, t) * exact - y[t])
            norm = norm + mode(1, t) * mode(0, t)
        mend_ref[part, :] = jnp.where(norm > 0.01, miss / jnp.maximum(norm, 0.01), 0.0)
        return carry

    lax.fori_loop(0, N // FACTOR_ROWS, body, 0)


def four(get):
    return [get(side, who) for side in range(2) for who in range(2)]


def vertical_apply(products, vert, scal_k, scal_m, scal_v):
    mass = [k * p[:, :N] + m * p[:, N:] for p, k, m in zip(products, scal_k, scal_m)]
    stiff = [v * p[:, :N] for p, v in zip(products, scal_v)]
    out = dot_full(vert[0], jnp.concatenate(mass, axis=1))
    out = out + dot_full(vert[1], jnp.concatenate(stiff, axis=1))
    return [out[:, q * N:(q + 1) * N] for q in range(len(products))]


def plane_products(faces, mk):
    stacked = dot_full(jnp.concatenate(faces, axis=0), mk[...])
    return [stacked[q * ROWS:(q + 1) * ROWS] for q in range(len(faces))]


def flip_masks(scal, nscal):
    return [scal[side, 3:4, :] != nscal[side, 3:4, :] for side in range(2)]


def orient_all(arrays, mirror, masks):
    turned = mirrored(jnp.concatenate([a for _, a in arrays], axis=0), mirror[...])
    return [
        jnp.where(masks[side], turned[q * ROWS:(q + 1) * ROWS], a)
        for q, (side, a) in enumerate(arrays)
    ]


def update_faces(c_faces, state, scal, nscal, mirror, mk, vert):
    masks = flip_masks(scal, nscal)
    residual = four(lambda side, who: state[4][2 * side + who])
    arrays = []
    for side in range(2):
        for who in range(2):
            arrays.append((side, c_faces[2 * side + 1 - who]))
    for side in range(2):
        for who in range(2):
            arrays.append((side, residual[2 * side + 1 - who]))
    turned = orient_all(arrays, mirror, masks)
    e, added = turned[:4], turned[4:]
    products = plane_products(e, mk)
    which = four(lambda side, who: (nscal if who else scal)[side])
    applied = vertical_apply(
        products, vert, [w[0:1] for w in which], [w[1:2] for w in which], [w[2:3] for w in which]
    )
    new = [list(state[s]) for s in range(6)]
    for q in range(4):
        new[2][q] = state[2][q] + DAMPING * (c_faces[q] + e[q])
        new[3][q] = state[3][q] + DAMPING * (residual[q] + added[q] + applied[q])
        new[4][q] = state[0][q] - state[1][q] * new[2][q] - new[3][q]
        new[5][q] = KEEP * state[5][q] + DAMPING * e[q]
    return new, e, masks


def read_state(ref):
    return [[ref[s, q] for q in range(4)] for s in range(6)]


def pad_rows(x):
    return jnp.concatenate([x, jnp.zeros((ROWS - x.shape[0], N), F32)], axis=0)


def eliminate_forward(gh_ref, spread, rows_hat, l_ref, modes, z_ref, msg_ref, low_ref, core):
    def body(c, carry):
        part = pl.ds(pl.multiple_of(c * CHUNK, CHUNK), CHUNK)
        west, east = spread[0, part, :], spread[1, part, :]
        z = {}
        lowest = jnp.zeros_like(west)
        for t in range(HALF):
            x = gh_ref[t, part, :] + west * rows_hat[0, t:t + 1, :] + east * rows_hat[1, t:t + 1, :]
            lowest = lowest + modes[0, t:t + 1, :] * x
            z_ref[t, part, :] = x
            for d in range(min(BAND, t), 0, -1):
                x = x - l_ref[t, d - 1, part, :] * z[t - d]
            z[t] = x
            if t < TOP:
                z_ref[t, part, :] = x
        low_ref[part, :] = lowest

        @pl.when(jnp.right_shift(c, 1) == core)
        def _():
            there = pl.ds(pl.multiple_of(jnp.bitwise_and(c, 1) * CHUNK, CHUNK), CHUNK)
            for s in range(BAND):
                msg_ref[s, there, :] = z[TOP + s]
            msg_ref[BAND, there, :] = lowest

        return carry

    lax.fori_loop(0, N // CHUNK, body, 0)


def first_kernel(
    ints, gh, own_pay, rec, scal, spread, wb, mirror, l_ref, modes,
    z_ref, msg_ref, low_ref, state_ref, rows_u, rows_g, rows_hat,
):
    received = (rec[0], rec[1])
    masks = [received[side][ROWS:ROWS + 1] != scal[side, 3:4, :] for side in range(2)]
    state_ref[...] = jnp.zeros_like(state_ref)
    for side in range(2):
        for who in range(2):
            values = received[side][:ROWS] if who else own_pay[side, :ROWS]
            state_ref[0, 2 * side + who] = values
            state_ref[4, 2 * side + who] = values
    turned = orient_all([(side, received[side][:ROWS]) for side in range(2)], mirror, masks)
    rows_u[...] = jnp.zeros_like(rows_u)
    for side in range(2):
        rows_g[side] = turned[side]
        rows_hat[side] = right_mul(turned[side], wb[...])
    eliminate_forward(gh, spread, rows_hat, l_ref, modes, z_ref, msg_ref, low_ref, ints[3])


def next_kernel(
    ints, gh, own_pay, rec, state_in, scal, nscal, spread, wb, mirror, mk, vert,
    l_ref, modes, z_ref, msg_ref, low_ref, state_ref, rows_u, rows_g, rows_hat,
):
    received = (rec[0], rec[1])
    state = read_state(state_in)
    if own_pay.shape[1] > ROWS:
        for side in range(2):
            state[1][2 * side] = pad_rows(own_pay[side, ROWS:ROWS + HALF])
            state[1][2 * side + 1] = pad_rows(received[side][ROWS:ROWS + HALF])
    c_faces = four(lambda side, who: received[side][:ROWS] if who else own_pay[side, :ROWS])
    state, e, masks = update_faces(c_faces, state, scal, nscal, mirror, mk, vert)
    for s in range(6):
        for q in range(4):
            state_ref[s, q] = state[s][q]
    turned = orient_all([(side, state[4][2 * side + 1]) for side in range(2)], mirror, masks)
    for side in range(2):
        step = DAMPING * e[2 * side]
        rows = turned[side] - state[1][2 * side] * step
        rows_u[side] = step
        rows_g[side] = rows
        rows_hat[side] = right_mul(rows, wb[...])
    eliminate_forward(gh, spread, rows_hat, l_ref, modes, z_ref, msg_ref, low_ref, ints[3])


def solve_kernel(
    ints, z_ref, low_ref, zr_ref, l_ref, dinv_ref, lm_ref, dm_ref, lo_ref, do_ref, mend, modes, spread, bt_full, state, *refs,
):
    sums = refs[-1]
    extra = refs[:2] if len(refs) > 4 else ()
    outs = refs[len(extra):-1]
    y_ref, pay_ref = outs[:2]
    sums[...] = jnp.zeros_like(sums)

    def body(c, carry):
        part = pl.ds(pl.multiple_of(c * CHUNK, CHUNK), CHUNK)
        source = jnp.right_shift(c, 1)
        if zr_ref.shape[0] > 2:
            source = source + 2 * (1 - ints[2])
        there = pl.ds(pl.multiple_of(jnp.bitwise_and(c, 1) * CHUNK, CHUNK), CHUNK)
        sent = [zr_ref[source, s, there, :] for s in range(BAND)]
        weights = (spread[0, part, :], spread[1, part, :])

        low = mend[part, :] * (low_ref[part, :] + zr_ref[source, BAND, there, :])

        def put(t, value):
            value = value + low * modes[0, t:t + 1, :]
            y_ref[t, part, :] = value
            for side in range(2):
                product = weights[side] * value
                total = product[0:8]
                for s in range(8, CHUNK, 8):
                    total = total + product[s:s + 8]
                sums[side, t] += total

        z = {t: z_ref[t, part, :] for t in range(TOP - BAND, HALF)}
        for j in range(BAND):
            for d in range(j + 1, BAND + 1):
                z[HALF - 1 - j] = z[HALF - 1 - j] - lo_ref[BAND + j, d - 1, part, :] * sent[BAND + j - d]
        for t in range(TOP, HALF):
            for d in range(BAND, 0, -1):
                z[t] = z[t] - lm_ref[t - TOP, d - 1, part, :] * z[t - d]

        def factor(t, d):
            return lm_ref[t - TOP, d - 1, part, :] if t >= TOP else l_ref[t, d - 1, part, :]

        y = {}
        for t in range(HALF - 1, TOP - 1, -1):
            value = z[t] * dm_ref[t - TOP, part, :]
            for d in range(HALF - 1 - t, 0, -1):
                value = value - factor(t + d, d) * y[t + d]
            y[t] = value
            put(t, value)
        far = {HALF + j: y[HALF - 1 - j] for j in range(BAND)}
        for t in range(HALF - 1, TOP - 1, -1):
            value = sent[t - TOP] * do_ref[t - TOP, part, :]
            for d in range(BAND, 0, -1):
                value = value - lo_ref[t + d - TOP, d - 1, part, :] * far[t + d]
            far[t] = value
            put(2 * HALF - 1 - t, value)
        for t in range(TOP - 1, -1, -1):
            known = z[t] if t in z else z_ref[t, part, :]
            value = known * dinv_ref[t, part, :]
            for d in range(BAND, 0, -1):
                value = value - factor(t + d, d) * y[t + d]
            y[t] = value
            put(t, value)
        return carry

    lax.fori_loop(0, N // CHUNK, body, 0)
    mixed = jnp.sum(sums[...], axis=2)
    faces = dot_full(mixed.reshape(2 * ROWS, N), bt_full[...])
    packs = []
    for side in range(2):
        c = faces[side * ROWS:(side + 1) * ROWS] - state[2, 2 * side]
        pay_ref[side, :ROWS] = c
        if extra:
            pay_ref[side, ROWS:ROWS + HALF] = extra[0][side]
            pay_ref[side, ROWS + HALF:] = extra[1][side]
    for slot_ref in outs[2:]:
        slot(ints, pay_ref[0], pay_ref[1], slot_ref)


def back_planes(y, wbt, lb):
    count = y.shape[0]
    across = right_mul(y.reshape(count * N, N), wbt).reshape(count, N, N)
    return left_mul_planes(lb, [across[q] for q in range(count)])


def make_plane_kernel(sweep):
    last = sweep == SWEEPS - 1

    def kernel(ints, *refs):
        refs = list(refs)
        y_ref, f_ref, r_ref, rows_u, rows_g, mask, wbt, lb = refs[:8]
        refs = refs[8:]
        if sweep > 0:
            up_in, g_in = refs[:2]
            refs = refs[2:]
        if last:
            cut, pay_in = refs[:2]
            up_out, final_out, pay_out, slot_ref, sums = refs[2:]
        else:
            wb, lbt = refs[:2]
            up_out, g_out, gh_out = refs[2:]

        def on_faces(rows, t):
            return mask[0] * rows[0, pl.ds(t, 1), :] + mask[1] * rows[1, pl.ds(t, 1), :]

        def body(g, carry):
            t0 = g * GROUP
            corrections = back_planes(y_ref[pl.ds(t0, GROUP)], wbt[...], lb[...])
            fresh = []
            for q in range(GROUP):
                t = t0 + q
                on_u, on_g = on_faces(rows_u, t), on_faces(rows_g, t)
                load, react = f_ref[t], r_ref[t]
                if sweep == 0:
                    u, total = on_u, DAMPING * (load + on_g)
                else:
                    old = up_in[t]
                    u = old + on_u
                    total = KEEP * g_in[t] + DAMPING * (load - react * old + on_g)
                new = KEEP * u + DAMPING * corrections[q]
                if last:
                    block, index = source_layer(ints, t)

                    @pl.when(block == ints[3])
                    def _():
                        up_out[index] = new
                else:
                    up_out[t] = new
                residual = load - react * new
                if last:
                    residual = residual - total
                    for side in range(2):
                        product = cut[side] * residual
                        part = product[0:8]
                        for s in range(8, N, 8):
                            part = part + product[s:s + 8]
                        sums[side, t] = part
                else:
                    g_out[t] = total
                if last:
                    final_out[t] = residual
                fresh.append(residual)
            if not last:
                stacked = jnp.concatenate(fresh, axis=0).reshape(GROUP, N, N)
                planes = forward_planes(stacked, wb[...], lbt[...])
                for q in range(GROUP):
                    gh_out[t0 + q] = planes[q]
            return carry

        lax.fori_loop(0, HALF // GROUP, body, 0)
        if last:
            for side in range(2):
                pay_out[side, :ROWS] = pay_in[side, :ROWS]
                pay_out[side, ROWS:] = jnp.sum(sums[side], axis=1)
            slot(ints, pay_out[0], pay_out[1], slot_ref)

    return kernel


def restrict_kernel(ints, final, wrt, lr, kept, sent, plane):
    def body(g, carry):
        t0 = g * GROUP
        planes = forward_planes(final[pl.ds(t0, GROUP)], wrt[...], lr[...])
        for q in range(GROUP):
            plane[q] = planes[q]

        @pl.when(ints[1] == 1)
        def _():
            for q in range(GROUP):
                plane[q] = planes[q].T

        for half in range(2):
            for core in range(2):
                first = half * (COARSE // 2) + core * 31

                @pl.when((ints[2] == half) & (ints[3] == core))
                def _():
                    kept[pl.ds(t0, GROUP)] = plane[:, first:first + 32]

                @pl.when((ints[2] != half) & (ints[3] == core))
                def _():
                    sent[pl.ds(t0, GROUP)] = plane[:, first:first + 32]

        return carry

    lax.fori_loop(0, HALF // GROUP, body, 0)


def final_kernel(
    ints, floats, own_pay, rec, state_in, scal, nscal, mirror, mirror_coarse, mk, vert, rt_full, parts, rows_u,
):
    received = (rec[0], rec[1])
    state = read_state(state_in)
    c_faces = four(lambda side, who: received[side][:ROWS] if who else own_pay[side, :ROWS])
    state, e, masks = update_faces(c_faces, state, scal, nscal, mirror, mk, vert)
    gathered = state[5]
    products = plane_products(gathered, mk)
    far = vertical_apply(
        [products[1], products[3]], vert,
        [nscal[side, 4:5] for side in range(2)],
        [nscal[side, 5:6] for side in range(2)],
        [nscal[side, 6:7] for side in range(2)],
    )
    one = floats[0]
    near_stiff = vertical_apply([products[0], products[2]], vert, [one] * 2, [floats[3]] * 2, [floats[3]] * 2)
    near_mass = vertical_apply([products[0], products[2]], vert, [floats[3]] * 2, [floats[1]] * 2, [floats[2]] * 2)
    stack = []
    for side in range(2):
        nbr = 2 * side + 1
        theirs = pad_rows(received[side][ROWS:])
        theirs = theirs - nscal[side, 7:8] * DAMPING * state[1][nbr] * e[nbr] - far[side]
        mine = scal[side, 7:8] * DAMPING * state[1][2 * side] * e[2 * side]
        stack += [near_stiff[side], near_mass[side], mine, theirs]
    restricted = dot_full(jnp.concatenate(stack, axis=0), rt_full[...])
    pieces = [restricted[q * ROWS:(q + 1) * ROWS] for q in range(8)]
    turned = mirrored(jnp.concatenate([pieces[3], pieces[7]], axis=0), mirror_coarse[...])
    for side in range(2):
        added = jnp.where(masks[side], turned[side * ROWS:(side + 1) * ROWS], pieces[4 * side + 3])
        parts[3 * side] = -pieces[4 * side][:HALF]
        parts[3 * side + 1] = -pieces[4 * side + 1][:HALF]
        parts[3 * side + 2] = (added - pieces[4 * side + 2])[:HALF]
        rows_u[side] = DAMPING * e[2 * side]

def iterate_kernel(ints, up, rows_u, mask, out_u):
    def body(index, carry):
        inside = ints[3] * BLOCK + index
        t = jnp.where(ints[2] == 1, HALF - 1 - inside, inside)
        value = up[index] + mask[0] * rows_u[0, pl.ds(t, 1), :] + mask[1] * rows_u[1, pl.ds(t, 1), :]
        out_u[index] = value

        @pl.when(ints[1] == 1)
        def _():
            out_u[index] = value.T

        return carry

    lax.fori_loop(0, BLOCK, body, 0, unroll=2)


def vertical_kernel(ints, kept, arrived, vertical, blocks):
    for c in range(32):
        rows = pl.ds(c, HALF, stride=32)
        both = jnp.concatenate([kept[rows, :], arrived[rows, :]], axis=0)
        blocks[c] = dot_full(vertical[...], both)


def coarse_kernel(ints, start_blocks, parts, far_parts, profile, profile_rows, vertical, out, blocks, columns):
    deep = vertical.shape[0]
    spots = [0, 31, COARSE // 2, COARSE // 2 + 31]
    stacked = [jnp.concatenate([parts[s], far_parts[s]], axis=0) for s in range(6)]
    mixed = dot_full(vertical[...], jnp.concatenate(stacked, axis=1))
    mixed = [mixed[:, s * N:(s + 1) * N] for s in range(6)]

    @pl.when(ints[1] == 0)
    def _():
        first = ints[2] * (COARSE // 2) + ints[3] * 31

        for c in range(32):
            value = start_blocks[c]
            for s in range(6):
                value = value + profile[s, pl.ds(first + c, 1), :] * mixed[s]
            blocks[c] = value

    @pl.when(ints[1] == 1)
    def _():
        for half in range(2):
            for core in range(2):
                shift = (N - spots[2 * half + core]) % N

                @pl.when((ints[2] == half) & (ints[3] == core))
                def _():
                    for s in range(6):
                        columns[s] = pltpu.roll(mixed[s], shift, 1) if shift else mixed[s]

        for c in range(32):
            value = start_blocks[c]
            for s in range(6):
                value = value + columns[s, :, c:c + 1] * profile_rows[s:s + 1, :]
            blocks[c] = value

    share = out.shape[1]
    lane = lax.broadcasted_iota(jnp.int32, (deep, N), 1)
    for core in range(2):

        @pl.when(ints[3] == core)
        def _():
            start = core * (COARSE // 2)
            held = {}

            def turned(c):
                if c not in held:
                    shift = (c * COARSE - start) % N
                    held[c] = pltpu.roll(blocks[c], shift, 1) if shift else blocks[c]
                return held[c]

            for tile in range(-(-share // N)):
                low = tile * N + start
                c = low // COARSE
                value = turned(c)
                after = (c + 1) * COARSE - low
                if after < N and c + 1 < 32:
                    value = jnp.where(lane < after, value, turned(c + 1))
                if after + COARSE < N and c + 2 < 32:
                    value = jnp.where(lane < after + COARSE, value, turned(c + 2))
                width = min(N, share - tile * N)
                out[:, tile * N:tile * N + width] = value[:, :width]


def prepare_kernel(
    ints, floats, stiff, mass, stiff_v, mass_v, basis, eigen, basis_v, eigen_v, restrict, restrict_v,
    wb, wbt, wrt, lb, lbt, lr, bt_out, rt_out, mk, mirror, mirror_coarse, vert, scal, spread, mask, cut,
    profile, profile_rows, alpha, bands, modes, vertical,
):
    a1, a2, a3 = floats[0], floats[1], floats[2]
    rows = lax.broadcasted_iota(jnp.int32, (N, N), 0)
    lanes = lax.broadcasted_iota(jnp.int32, (N, N), 1)
    eye = rows == lanes

    def column(row):
        picked = jnp.sum(jnp.where(eye, row, 0.0), axis=1, keepdims=True)
        return jnp.broadcast_to(picked, (N, N))

    b, k, m = basis[...], stiff[...], mass[...]
    bt = b.T
    r = jnp.concatenate([restrict[...], jnp.zeros((N - COARSE, N), F32)], axis=0)
    rt = r.T
    wb[...], wbt[...], wrt[...] = pack_right(b), pack_right(bt), pack_right(rt)
    lb[...], lbt[...], lr[...] = pack_left(b), pack_left(bt), pack_left(r)
    bt_out[...], rt_out[...] = bt, rt
    mk[:, :N], mk[:, N:] = m, k
    for out, count in ((mirror, N), (mirror_coarse, COARSE)):
        reverse = (rows + lanes == count - 1).astype(F32).astype(BF16)
        out[...] = jnp.concatenate([reverse] * 3, axis=0)
    alpha[...] = a1 * column(eigen[...]) + a2 * eigen[...]

    turn = (
        lax.broadcasted_iota(jnp.int32, (LAYERS, LAYERS), 0)
        + lax.broadcasted_iota(jnp.int32, (LAYERS, LAYERS), 1)
        == LAYERS - 1
    ).astype(F32)
    first = ints[2] == 0
    kv, mv = stiff_v[...], mass_v[...]
    ordered = []
    for matrix in (mv, a3 * kv):
        turned = dot_full(dot_full(turn, matrix), turn)
        ordered.append((jnp.where(first, matrix, turned), jnp.where(first, turned, matrix)))
    deep = lax.broadcasted_iota(jnp.int32, (ROWS, LAYERS), 0)
    wide = lax.broadcasted_iota(jnp.int32, (ROWS, LAYERS), 1)
    inside = (deep < HALF) & (wide < REACH)
    own_stiff = jnp.where(first, kv, dot_full(dot_full(turn, kv), turn))
    vert[0] = jnp.where(inside, ordered[0][0][:ROWS], 0.0)[:, :ROWS]
    vert[1] = jnp.where(inside, own_stiff[:ROWS], 0.0)[:, :ROWS]
    for which in range(2):
        for s in range(2):
            for d in range(BAND + 1):
                picked = jnp.where(deep - wide == d, ordered[s][which][:ROWS], 0.0)
                bands[which, s, d] = jnp.broadcast_to(jnp.sum(picked, axis=1, keepdims=True), (ROWS, N))

    rv = restrict_v[...]
    backwards = dot_full(rv, turn)
    vertical[:, :HALF] = jnp.where(first, rv, backwards)[:, :HALF]
    vertical[:, HALF:] = jnp.where(first, backwards, rv)[:, :HALF]

    mu = eigen_v[...]
    least = jnp.min(mu, axis=1, keepdims=True)
    number = lax.broadcasted_iota(jnp.int32, (1, LAYERS), 1)
    chosen = jnp.min(jnp.where(mu == least, number, LAYERS), axis=1, keepdims=True)
    low = jnp.sum(jnp.where(number == chosen, basis_v[...], 0.0), axis=1, keepdims=True)
    low = jnp.broadcast_to(low, (LAYERS, N))
    low_mass = dot_full(mv, low)
    low_turned, mass_turned = dot_full(turn, low), dot_full(turn, low_mass)
    modes[0] = jnp.where(first, low, low_turned)[:ROWS]
    modes[1] = jnp.where(first, low_mass, mass_turned)[:ROWS]
    modes[2] = jnp.where(first, mass_turned, low_mass)[:ROWS]
    modes[3] = jnp.broadcast_to(a3 * least, (ROWS, N))

    for side in range(2):
        start = ints[4 + side] == 0

        def end_row(matrix, count=N):
            return jnp.where(start, matrix[0:1, :], matrix[count - 1:count, :])

        def corner(matrix):
            value = jnp.where(start, matrix[0:1, 0:1], matrix[N - 1:N, N - 1:N])
            return jnp.broadcast_to(value, (1, N))

        cut_row = end_row(r, COARSE)
        cut_at = jnp.broadcast_to(jnp.where(start, cut_row[:, 0:1], cut_row[:, N - 1:N]), (1, N))
        stiff_profile = jnp.broadcast_to(jnp.sum(r * end_row(k), axis=1, keepdims=True), (N, N))
        mass_profile = jnp.broadcast_to(jnp.sum(r * end_row(m), axis=1, keepdims=True), (N, N))
        at_face = jnp.where(start, 0, COARSE - 1)
        at_rows = [stiff_profile, mass_profile, (rows == at_face).astype(F32)]
        for s in range(3):
            turned_row = jnp.sum(jnp.where(eye, at_rows[s], 0.0), axis=0, keepdims=True)
            profile_rows[3 * side + s:3 * side + s + 1, :] = turned_row
        profile[3 * side] = stiff_profile
        profile[3 * side + 1] = mass_profile
        profile[3 * side + 2] = (rows == at_face).astype(F32)
        spread[side] = column(end_row(b))
        mask[side] = (rows == ints[4 + side]).astype(F32)
        cut[side] = column(cut_row)
        scal[side] = jnp.concatenate(
            [
                corner(k) * a1,
                corner(m) * a2,
                corner(m) * a3,
                jnp.broadcast_to(ints[0].astype(F32), (1, N)),
                end_row(stiff_profile, COARSE) * a1,
                end_row(mass_profile, COARSE) * a2,
                end_row(mass_profile, COARSE) * a3,
                cut_at,
            ],
            axis=0,
        )


def per_device(
    load_vector,
    reaction,
    geometry,
    stiff_plane,
    mass_plane,
    stiff_vertical,
    mass_vertical,
    basis_plane,
    eigen_plane,
    basis_vertical,
    eigen_vertical,
    restrict_plane,
    restrict_vertical,
    patch_links,
):
    patches = lax.axis_size("patch")
    links = patch_links
    square, two = (N, N), (2, N, N)
    right = jax.ShapeDtypeStruct((2 * N, 2 * N), BF16)
    left = jax.ShapeDtypeStruct((N, 2 * N), BF16)
    thrice = jax.ShapeDtypeStruct((3 * N, N), BF16)
    (
        wb, wbt, wrt, lb, lbt, lr, basis_t, restrict_t, mk, mirror, mirror_coarse, vert, scal, spread, mask,
        cut, profile, profile_rows, alpha, bands, modes, vertical,
    ) = call(
        prepare_kernel,
        [
            right, right, right, left, left, left, square, square, (N, 2 * N), thrice, thrice,
            (2, ROWS, ROWS), (2, 8, N), two, two, two, (6, N, N), (8, N), square, (2, 2, BAND + 1, ROWS, N), (4, ROWS, N),
            restrict_vertical.shape,
        ],
        links, stiff_plane, mass_plane, stiff_vertical, mass_vertical, basis_plane, eigen_plane.reshape(1, N),
        basis_vertical, eigen_vertical.reshape(1, LAYERS), restrict_plane, restrict_vertical,
        geometry=geometry, flops=20_000_000,
    )

    pair = [(0, 1), (1, 0), (2, 3), (3, 2)]
    cross = [(0, 2), (2, 0), (1, 3), (3, 1)]
    chips = [[0, 1], [2, 3]]
    faces = []
    for p in range(patches):
        for h in range(2):
            west, east = 4 * p + 2 * h + 1, 4 * ((p + 1) % patches) + 2 * h
            faces += [(west, east), (east, west)]

    def swap_faces(slot_values):
        arrived = lax.ppermute(slot_values, ("patch", "slab"), faces)
        return lambda: lax.all_gather(arrived, "slab", axis_index_groups=chips)

    field = (HALF, N, N)
    own_load = load_vector[0].reshape(BLOCK, N, N)
    own_react = reaction[0].reshape(BLOCK, N, N)
    other_load = lax.ppermute(own_load, "slab", pair)
    other_react = lax.ppermute(own_react, "slab", pair)
    size = ROWS + 8
    f, pay, slot_values = call(
        load_kernel, [field, (2, size, N), (size, N)], links, own_load, other_load
    )
    arriving = swap_faces(slot_values)
    l, dinv = call(
        factor_kernel, [(HALF, BAND, N, N), field], links, slot_values, alpha, bands, flops=3_000_000_000
    )
    (gh,) = call(transform_kernel, [field], links, f, wb, lbt, flops=2_000_000_000)
    rec = arriving()
    rows_hat = pltpu.VMEM((2, ROWS, N), F32)
    sums = pltpu.VMEM((2, ROWS, 8, N), F32)
    message = (BAND + 1, N // 2, N)
    message_full = (BAND, N, N)
    state_shape = (6, 4, ROWS, N)
    rows_shape = (2, ROWS, N)
    up = total = None
    for sweep in range(SWEEPS):
        if sweep == 0:
            z, msg, low, state, rows_u, rows_g = call(
                first_kernel,
                [field, message, square, state_shape, rows_shape, rows_shape],
                links, gh, pay, rec, scal, spread, wb, mirror, l, modes,
                scratch=[rows_hat], flops=10_000_000,
            )
        else:
            if sweep == 1:
                nscal = rec[:, ROWS + HALF:]
            z, msg, low, state, rows_u, rows_g = call(
                next_kernel,
                [field, message, square, state_shape, rows_shape, rows_shape],
                links, gh, pay, rec, state, scal, nscal, spread, wb, mirror, mk, vert, l, modes,
                scratch=[rows_hat], flops=10_000_000,
            )
        if sweep > 0:
            received = lax.all_gather(msg, "slab")
        else:
            crossing = lax.ppermute(msg, "slab", cross)
            r, react_faces = call(reaction_kernel, [field, (2, HALF, N)], links, msg, own_react, other_react)
            lm, dm, lo, do, mend = call(
                meet_kernel,
                [(BAND, BAND, N, N), message_full, (2 * BAND, BAND, N, N), message_full, square],
                links, alpha, bands, modes, l, dinv,
                scratch=[pltpu.VMEM((TOP, FACTOR_ROWS, N), F32)], flops=5_000_000_000,
            )
            received = lax.all_gather(crossing, "slab", axis_index_groups=chips)
        last = sweep == SWEEPS - 1
        size = ROWS + HALF + 8 if sweep == 0 else ROWS
        extra = [react_faces, scal] if sweep == 0 else []
        y, pay, *slot_values = call(
            solve_kernel,
            [(REACH, N, N), (2, size, N)] + ([] if last else [(size, N)]),
            links, z, low, received, l, dinv, lm, dm, lo, do, mend, modes, spread, basis_t, state, *extra,
            scratch=[sums], flops=10_000_000,
        )
        args = [y, f, r, rows_u, rows_g, mask, wbt, lb]
        if sweep > 0:
            args += [up, total]
        plane_kernel = make_plane_kernel(sweep)
        if last:
            size = ROWS + HALF
            block = (HALF, 32, N)
            up, final, pay, slot_values = call(
                plane_kernel,
                [(BLOCK, N, N), field, (2, size, N), (size, N)],
                links, *args, cut, pay,
                scratch=[pltpu.VMEM((2, HALF, 8, N), F32)], flops=3_000_000_000,
            )
            arriving = swap_faces(slot_values)
            kept, sent = call(
                restrict_kernel, [block, block], links, final, wrt, lr,
                scratch=[pltpu.VMEM((GROUP, N, N), F32)], flops=3_000_000_000,
            )
            arrived = lax.ppermute(sent, "slab", cross)
            rec = arriving()
        else:
            arriving = swap_faces(slot_values[0])
            up, total, gh = call(
                plane_kernel, [field, field, field], links, *args, wb, lbt, flops=4_000_000_000
            )
            rec = arriving()
    parts, rows_u = call(
        final_kernel,
        [(6, HALF, N), rows_shape],
        links, pay, rec, state, scal, nscal, mirror, mirror_coarse, mk, vert, restrict_t,
        geometry=geometry, flops=80_000_000_000,
    )
    far_parts = lax.ppermute(parts, "slab", cross)
    (out_u,) = call(iterate_kernel, [(BLOCK, N, N)], links, up, rows_u, mask, flops=2_000_000_000)
    deep = restrict_vertical.shape[0]
    share = COARSE * COARSE // 4
    (blocks,) = call(
        vertical_kernel, [(32, deep, N)],
        links, kept.reshape(HALF * 32, N), arrived.reshape(HALF * 32, N), vertical, flops=2_000_000_000,
    )
    (flat,) = call(
        coarse_kernel,
        [(deep, share)],
        links, blocks, parts, far_parts, profile, profile_rows, vertical,
        scratch=[pltpu.VMEM((32, deep, N), F32), pltpu.VMEM((6, deep, N), F32)],
        flops=20_000_000_000,
    )
    return out_u.reshape(1, BLOCK, N * N), flat[None]


def solution(mesh):
    in_specs = (
        P("patch", "slab", None),
        P("patch", "slab", None),
        P("patch", None),
        P(), P(), P(), P(), P(), P(), P(), P(), P(), P(),
        P("patch", None),
    )
    out_specs = (P("patch", "slab", None), P("patch", None, "slab"))
    return jax.shard_map(
        per_device, mesh=mesh, in_specs=in_specs, out_specs=out_specs, check_vma=False
    )
```

```python
import jax
import jax.numpy as jnp
from jax import lax
from jax.experimental import pallas as pl
from jax.experimental.pallas import tpu as pltpu
from jax.sharding import PartitionSpec as P

BAND = 4
SWEEPS = 3
DAMPING = 0.25
KEEP = 1.0 - DAMPING
HIGHEST = lax.Precision.HIGHEST
F32 = jnp.float32
BF16 = jnp.bfloat16

N = 128
LAYERS = 64
HALF = 32
BLOCK = 16
REACH = HALF + BAND
ROWS = 40
TOP = HALF - BAND
CHUNK = 32
COARSE = N - 2


def split(x):
    high = x.astype(BF16)
    return high, (x - high.astype(F32)).astype(BF16)


def right_mul(x, packed):
    high, low = split(x)
    both = jnp.dot(jnp.concatenate([high, low], axis=-1), packed, preferred_element_type=F32)
    return both[:, :N] + both[:, N:]


def left_mul_planes(packed, planes):
    out = []
    for q in range(0, len(planes), 2):
        high, low = split(jnp.concatenate(planes[q:q + 2], axis=1))
        wide = jnp.dot(packed, jnp.concatenate([high, high], axis=0), preferred_element_type=F32)
        wide = wide + jnp.dot(packed[:, :N], low, preferred_element_type=F32)
        out += [wide[:, :N], wide[:, N:]]
    return out


def dot_full(x, y):
    return jnp.dot(x, y, precision=HIGHEST, preferred_element_type=F32)


def mirrored(x, mirror):
    high, rest = split(x)
    middle, low = split(x - high.astype(F32))
    return jnp.dot(
        jnp.concatenate([high, middle, low], axis=-1), mirror, preferred_element_type=F32
    )


def pack_right(a):
    high, low = split(a)
    top = jnp.concatenate([high, low], axis=1)
    bottom = jnp.concatenate([high, jnp.zeros_like(low)], axis=1)
    return jnp.concatenate([top, bottom], axis=0)


def pack_left(a):
    return jnp.concatenate(split(a), axis=1)


def call(kernel, outs, links, *args, flops=0, scratch=(), geometry=None, moved=None):
    smem = [links] if geometry is None else [links, geometry]
    specs = [pl.BlockSpec(memory_space=pltpu.SMEM)] * len(smem)
    specs += [pl.BlockSpec(memory_space=pltpu.VMEM)] * len(args)
    shapes = [s if isinstance(s, jax.ShapeDtypeStruct) else jax.ShapeDtypeStruct(s, F32) for s in outs]
    if moved is None:
        moved = sum(a.size * a.dtype.itemsize for a in args) + sum(4 * s.size for s in shapes)

    def body(links_ref, *refs):
        ints = facts(links_ref)
        if geometry is None:
            kernel(ints, *refs)
        else:
            kernel(ints, scales(ints, refs[0]), *refs[1:])

    return pl.pallas_call(
        body,
        out_shape=shapes,
        in_specs=specs,
        out_specs=[pl.BlockSpec(memory_space=pltpu.VMEM)] * len(outs),
        scratch_shapes=list(scratch),
        compiler_params=pltpu.CompilerParams(vmem_limit_bytes=16 * 1024 * 1024),
        cost_estimate=pl.CostEstimate(
            flops=flops, bytes_accessed=moved, transcendentals=0
        ),
    )(*smem, *args)


def facts(links):
    slab = lax.axis_index("slab")
    west, east = links[0, 0], links[0, 1]
    return (
        links[0, 2], jnp.right_shift(west, 1), jnp.right_shift(slab, 1), jnp.bitwise_and(slab, 1),
        (N - 1) * jnp.bitwise_and(west, 1), (N - 1) * jnp.bitwise_and(east, 1),
    )


def scales(ints, geometry):
    turned = ints[1] == 1
    first, second = geometry[0, 0], geometry[0, 1]
    return (
        jnp.where(turned, second, first), jnp.where(turned, first, second), geometry[0, 2], jnp.float32(0),
    )


def source_layer(ints, t):
    inside = jnp.where(ints[2] == 1, HALF - 1 - t, t)
    return jnp.right_shift(inside, 4), jnp.bitwise_and(inside, BLOCK - 1)


def load_layers(ints, own_ref, other_ref, out_ref):
    def run(turn):
        def body(g, carry):
            for q in range(8):
                t = g * 8 + q
                block, index = source_layer(ints, t)
                value = jnp.where(block == ints[3], own_ref[index], other_ref[index])
                out_ref[t] = value.T if turn else value
            return carry

        lax.fori_loop(0, HALF // 8, body, 0)

    @pl.when(ints[1] == 0)
    def _():
        run(False)

    @pl.when(ints[1] == 1)
    def _():
        run(True)


def slot(ints, west, east, slot_ref):
    slot_ref[...] = jnp.where(ints[3] == 0, west, east)


def face_rows(ints, ref, side):
    position = ints[4 + side]
    return jnp.where(position == 0, ref[:, 0, :], ref[:, N - 1, :])


def load_kernel(ints, own, other, f_ref, pay_ref, slot_ref):
    load_layers(ints, own, other, f_ref)
    flag = jnp.broadcast_to(ints[0].astype(F32), (8, N))
    for side in range(2):
        rows = face_rows(ints, f_ref, side)
        pay_ref[side] = jnp.concatenate([rows, jnp.zeros((ROWS - HALF, N), F32), flag], axis=0)
    slot(ints, pay_ref[0], pay_ref[1], slot_ref)


def reaction_kernel(ints, ready, own, other, r_ref, face_ref):
    load_layers(ints, own, other, r_ref)
    for side in range(2):
        face_ref[side] = face_rows(ints, r_ref, side)


def forward_planes(x, wb, lbt):
    count = x.shape[0]
    first = right_mul(x.reshape(count * N, N), wb).reshape(count, N, N)
    return left_mul_planes(lbt, [first[q] for q in range(count)])


GROUP = 32


def transform_kernel(ints, f_ref, wb, lbt, out_ref):
    def body(g, carry):
        t = g * GROUP
        planes = forward_planes(f_ref[pl.ds(t, GROUP)], wb[...], lbt[...])
        for q in range(GROUP):
            out_ref[t + q] = planes[q]
        return carry

    lax.fori_loop(0, HALF // GROUP, body, 0)


FACTOR_ROWS = 16


def coefficient(bands, alpha, which, t, d):
    return alpha * bands[which, 0, d, t:t + 1, :] + bands[which, 1, d, t:t + 1, :]


def row_weights(a, l, t, least):
    w = {}
    for d in range(min(BAND, t), least - 1, -1):
        v = a[d]
        for m in range(d + 1, min(BAND, t) + 1):
            v = v - w[m] * l[t - d][m - d]
        w[d] = v
    return w


def eliminate(a, l, dinv, t):
    w = row_weights(a, l, t, 1)
    row = {d: w[d] * dinv[t - d] for d in w}
    pivot = a[0]
    for d in w:
        pivot = pivot - w[d] * row[d]
    return row, 1.0 / pivot


def factor_kernel(ints, ready, alpha_ref, bands, l_ref, dinv_ref):
    def body(c, carry):
        part = pl.ds(c * FACTOR_ROWS, FACTOR_ROWS)
        alpha = alpha_ref[part, :]
        l, dinv = {}, {}
        for t in range(HALF):
            a = [coefficient(bands, alpha, 0, t, d) for d in range(min(BAND, t) + 1)]
            l[t], dinv[t] = eliminate(a, l, dinv, t)
            for d in l[t]:
                l_ref[t, d - 1, part, :] = l[t][d]
            dinv_ref[t, part, :] = dinv[t]
        return carry

    lax.fori_loop(0, N // FACTOR_ROWS, body, 0)


def meet_kernel(
    ints, alpha_ref, bands, modes, l_ref, dinv_ref, lm_ref, dm_ref, lo_ref, do_ref, mend_ref, zs
):
    def mode(which, t):
        return modes[which, t:t + 1, :]

    def body(c, carry):
        part = pl.ds(c * FACTOR_ROWS, FACTOR_ROWS)
        alpha = alpha_ref[part, :]
        l, dinv, sent = {}, {}, {}
        for t in range(HALF):
            a = [coefficient(bands, alpha, 1, t, d) for d in range(min(BAND, t) + 1)]
            l[t], dinv[t] = eliminate(a, l, dinv, t)
            sent[t] = jnp.broadcast_to(mode(2, t), alpha.shape)
            for d in l[t]:
                sent[t] = sent[t] - l[t][d] * sent[t - d]
            if t >= TOP:
                for d in range(1, BAND + 1):
                    lo_ref[t - TOP, d - 1, part, :] = l[t][d]
                do_ref[t - TOP, part, :] = dinv[t]
        outer = {}
        for j in range(BAND):
            t = HALF + j
            a = [coefficient(bands, alpha, 1, t, d) for d in range(BAND + 1)]
            outer[j] = row_weights(a, l, t, j + 1)
            l[t] = {d: outer[j][d] * dinv[t - d] for d in outer[j]}
            for d in l[t]:
                lo_ref[BAND + j, d - 1, part, :] = l[t][d]
        schur = {}
        for j in range(BAND):
            for i in range(j + 1):
                total = None
                for s in range(TOP + j, HALF):
                    term = outer[j][HALF + j - s] * l[HALF + i][HALF + i - s]
                    total = term if total is None else total + term
                schur[(j, i)] = schur[(i, j)] = total
        shift = {}
        for j in range(BAND):
            for d in range(j + 1, BAND + 1):
                term = l[HALF + j][d] * sent[HALF + j - d]
                shift[j] = term if j not in shift else shift[j] + term
        z = {}
        for t in range(TOP):
            z[t] = jnp.broadcast_to(mode(1, t), alpha.shape)
            for d in range(1, min(BAND, t) + 1):
                z[t] = z[t] - l_ref[t, d - 1, part, :] * z[t - d]
            zs[t] = z[t]
        l = {
            t: {d: l_ref[t, d - 1, part, :] for d in range(1, BAND + 1)} for t in range(TOP - BAND, TOP)
        }
        dinv = {t: dinv_ref[t, part, :] for t in range(TOP - BAND, TOP)}
        for t in range(TOP, HALF):
            a = [coefficient(bands, alpha, 0, t, d) for d in range(BAND + 1)]
            j = HALF - 1 - t
            for d in range(t - TOP + 1):
                a[d] = a[d] - schur[(j, j + d)]
            l[t], dinv[t] = eliminate(a, l, dinv, t)
            for d in range(1, BAND + 1):
                lm_ref[t - TOP, d - 1, part, :] = l[t][d]
            dm_ref[t - TOP, part, :] = dinv[t]
            z[t] = mode(1, t) - shift[j]
            for d in range(1, BAND + 1):
                z[t] = z[t] - l[t][d] * z[t - d]
        exact = 1.0 / (alpha + modes[3, 0:1, :])
        y, miss, norm = {}, jnp.zeros_like(alpha), jnp.zeros_like(modes[3, 0:1, :])
        for t in range(HALF - 1, -1, -1):
            y[t] = z[t] * dinv[t] if t >= TOP else zs[t] * dinv_ref[t, part, :]
            for d in range(1, min(BAND, HALF - 1 - t) + 1):
                factor = l[t + d][d] if t + d >= TOP else l_ref[t + d, d - 1, part, :]
                y[t] = y[t] - factor * y[t + d]
            miss = miss + mode(1, t) * (mode(0, t) * exact - y[t])
            norm = norm + mode(1, t) * mode(0, t)
        mend_ref[part, :] = jnp.where(norm > 0.01, miss / jnp.maximum(norm, 0.01), 0.0)
        return carry

    lax.fori_loop(0, N // FACTOR_ROWS, body, 0)


def four(get):
    return [get(side, who) for side in range(2) for who in range(2)]


def vertical_apply(products, vert, scal_k, scal_m, scal_v):
    mass = [k * p[:, :N] + m * p[:, N:] for p, k, m in zip(products, scal_k, scal_m)]
    stiff = [v * p[:, :N] for p, v in zip(products, scal_v)]
    out = dot_full(vert[0], jnp.concatenate(mass, axis=1))
    out = out + dot_full(vert[1], jnp.concatenate(stiff, axis=1))
    return [out[:, q * N:(q + 1) * N] for q in range(len(products))]


def plane_products(faces, mk):
    stacked = dot_full(jnp.concatenate(faces, axis=0), mk[...])
    return [stacked[q * ROWS:(q + 1) * ROWS] for q in range(len(faces))]


def flip_masks(scal, nscal):
    return [scal[side, 3:4, :] != nscal[side, 3:4, :] for side in range(2)]


def orient_all(arrays, mirror, masks):
    turned = mirrored(jnp.concatenate([a for _, a in arrays], axis=0), mirror[...])
    return [
        jnp.where(masks[side], turned[q * ROWS:(q + 1) * ROWS], a)
        for q, (side, a) in enumerate(arrays)
    ]


def update_faces(c_faces, state, scal, nscal, mirror, mk, vert):
    masks = flip_masks(scal, nscal)
    residual = four(lambda side, who: state[4][2 * side + who])
    arrays = []
    for side in range(2):
        for who in range(2):
            arrays.append((side, c_faces[2 * side + 1 - who]))
    for side in range(2):
        for who in range(2):
            arrays.append((side, residual[2 * side + 1 - who]))
    turned = orient_all(arrays, mirror, masks)
    e, added = turned[:4], turned[4:]
    products = plane_products(e, mk)
    which = four(lambda side, who: (nscal if who else scal)[side])
    applied = vertical_apply(
        products, vert, [w[0:1] for w in which], [w[1:2] for w in which], [w[2:3] for w in which]
    )
    new = [list(state[s]) for s in range(6)]
    for q in range(4):
        new[2][q] = state[2][q] + DAMPING * (c_faces[q] + e[q])
        new[3][q] = state[3][q] + DAMPING * (residual[q] + added[q] + applied[q])
        new[4][q] = state[0][q] - state[1][q] * new[2][q] - new[3][q]
        new[5][q] = KEEP * state[5][q] + DAMPING * e[q]
    return new, e, masks


def read_state(ref):
    return [[ref[s, q] for q in range(4)] for s in range(6)]


def pad_rows(x):
    return jnp.concatenate([x, jnp.zeros((ROWS - x.shape[0], N), F32)], axis=0)


def eliminate_forward(gh_ref, spread, rows_hat, l_ref, modes, z_ref, msg_ref, low_ref, core):
    def body(c, carry):
        part = pl.ds(pl.multiple_of(c * CHUNK, CHUNK), CHUNK)
        west, east = spread[0, part, :], spread[1, part, :]
        z = {}
        lowest = jnp.zeros_like(west)
        for t in range(HALF):
            x = gh_ref[t, part, :] + west * rows_hat[0, t:t + 1, :] + east * rows_hat[1, t:t + 1, :]
            lowest = lowest + modes[0, t:t + 1, :] * x
            z_ref[t, part, :] = x
            for d in range(min(BAND, t), 0, -1):
                x = x - l_ref[t, d - 1, part, :] * z[t - d]
            z[t] = x
            if t < TOP:
                z_ref[t, part, :] = x
        low_ref[part, :] = lowest

        @pl.when(jnp.right_shift(c, 1) == core)
        def _():
            there = pl.ds(pl.multiple_of(jnp.bitwise_and(c, 1) * CHUNK, CHUNK), CHUNK)
            for s in range(BAND):
                msg_ref[s, there, :] = z[TOP + s]
            msg_ref[BAND, there, :] = lowest

        return carry

    lax.fori_loop(0, N // CHUNK, body, 0)


def first_kernel(
    ints, gh, own_pay, rec, scal, spread, wb, mirror, l_ref, modes,
    z_ref, msg_ref, low_ref, state_ref, rows_u, rows_g, rows_hat,
):
    received = (rec[0], rec[1])
    masks = [received[side][ROWS:ROWS + 1] != scal[side, 3:4, :] for side in range(2)]
    state_ref[...] = jnp.zeros_like(state_ref)
    for side in range(2):
        for who in range(2):
            values = received[side][:ROWS] if who else own_pay[side, :ROWS]
            state_ref[0, 2 * side + who] = values
            state_ref[4, 2 * side + who] = values
    turned = orient_all([(side, received[side][:ROWS]) for side in range(2)], mirror, masks)
    rows_u[...] = jnp.zeros_like(rows_u)
    for side in range(2):
        rows_g[side] = turned[side]
        rows_hat[side] = right_mul(turned[side], wb[...])
    eliminate_forward(gh, spread, rows_hat, l_ref, modes, z_ref, msg_ref, low_ref, ints[3])


def next_kernel(
    ints, gh, own_pay, rec, state_in, scal, nscal, spread, wb, mirror, mk, vert,
    l_ref, modes, z_ref, msg_ref, low_ref, state_ref, rows_u, rows_g, rows_hat,
):
    received = (rec[0], rec[1])
    state = read_state(state_in)
    if own_pay.shape[1] > ROWS:
        for side in range(2):
            state[1][2 * side] = pad_rows(own_pay[side, ROWS:ROWS + HALF])
            state[1][2 * side + 1] = pad_rows(received[side][ROWS:ROWS + HALF])
    c_faces = four(lambda side, who: received[side][:ROWS] if who else own_pay[side, :ROWS])
    state, e, masks = update_faces(c_faces, state, scal, nscal, mirror, mk, vert)
    for s in range(6):
        for q in range(4):
            state_ref[s, q] = state[s][q]
    turned = orient_all([(side, state[4][2 * side + 1]) for side in range(2)], mirror, masks)
    for side in range(2):
        step = DAMPING * e[2 * side]
        rows = turned[side] - state[1][2 * side] * step
        rows_u[side] = step
        rows_g[side] = rows
        rows_hat[side] = right_mul(rows, wb[...])
    eliminate_forward(gh, spread, rows_hat, l_ref, modes, z_ref, msg_ref, low_ref, ints[3])


def solve_kernel(
    ints, z_ref, low_ref, zr_ref, l_ref, dinv_ref, lm_ref, dm_ref, lo_ref, do_ref, mend, modes, spread, bt_full, state, *refs,
):
    sums = refs[-1]
    extra = refs[:2] if len(refs) > 4 else ()
    outs = refs[len(extra):-1]
    y_ref, pay_ref = outs[:2]
    sums[...] = jnp.zeros_like(sums)

    def body(c, carry):
        part = pl.ds(pl.multiple_of(c * CHUNK, CHUNK), CHUNK)
        source = jnp.right_shift(c, 1)
        if zr_ref.shape[0] > 2:
            source = source + 2 * (1 - ints[2])
        there = pl.ds(pl.multiple_of(jnp.bitwise_and(c, 1) * CHUNK, CHUNK), CHUNK)
        sent = [zr_ref[source, s, there, :] for s in range(BAND)]
        weights = (spread[0, part, :], spread[1, part, :])

        low = mend[part, :] * (low_ref[part, :] + zr_ref[source, BAND, there, :])

        def put(t, value):
            value = value + low * modes[0, t:t + 1, :]
            y_ref[t, part, :] = value
            for side in range(2):
                product = weights[side] * value
                total = product[0:8]
                for s in range(8, CHUNK, 8):
                    total = total + product[s:s + 8]
                sums[side, t] += total

        z = {t: z_ref[t, part, :] for t in range(TOP - BAND, HALF)}
        for j in range(BAND):
            for d in range(j + 1, BAND + 1):
                z[HALF - 1 - j] = z[HALF - 1 - j] - lo_ref[BAND + j, d - 1, part, :] * sent[BAND + j - d]
        for t in range(TOP, HALF):
            for d in range(BAND, 0, -1):
                z[t] = z[t] - lm_ref[t - TOP, d - 1, part, :] * z[t - d]

        def factor(t, d):
            return lm_ref[t - TOP, d - 1, part, :] if t >= TOP else l_ref[t, d - 1, part, :]

        y = {}
        for t in range(HALF - 1, TOP - 1, -1):
            value = z[t] * dm_ref[t - TOP, part, :]
            for d in range(HALF - 1 - t, 0, -1):
                value = value - factor(t + d, d) * y[t + d]
            y[t] = value
            put(t, value)
        far = {HALF + j: y[HALF - 1 - j] for j in range(BAND)}
        for t in range(HALF - 1, TOP - 1, -1):
            value = sent[t - TOP] * do_ref[t - TOP, part, :]
            for d in range(BAND, 0, -1):
                value = value - lo_ref[t + d - TOP, d - 1, part, :] * far[t + d]
            far[t] = value
            put(2 * HALF - 1 - t, value)
        for t in range(TOP - 1, -1, -1):
            known = z[t] if t in z else z_ref[t, part, :]
            value = known * dinv_ref[t, part, :]
            for d in range(BAND, 0, -1):
                value = value - factor(t + d, d) * y[t + d]
            y[t] = value
            put(t, value)
        return carry

    lax.fori_loop(0, N // CHUNK, body, 0)
    mixed = jnp.sum(sums[...], axis=2)
    faces = dot_full(mixed.reshape(2 * ROWS, N), bt_full[...])
    packs = []
    for side in range(2):
        c = faces[side * ROWS:(side + 1) * ROWS] - state[2, 2 * side]
        pay_ref[side, :ROWS] = c
        if extra:
            pay_ref[side, ROWS:ROWS + HALF] = extra[0][side]
            pay_ref[side, ROWS + HALF:] = extra[1][side]
    for slot_ref in outs[2:]:
        slot(ints, pay_ref[0], pay_ref[1], slot_ref)


def back_planes(y, wbt, lb):
    count = y.shape[0]
    across = right_mul(y.reshape(count * N, N), wbt).reshape(count, N, N)
    return left_mul_planes(lb, [across[q] for q in range(count)])


def make_plane_kernel(sweep):
    last = sweep == SWEEPS - 1

    def kernel(ints, *refs):
        refs = list(refs)
        y_ref, f_ref, r_ref, rows_u, rows_g, mask, wbt, lb = refs[:8]
        refs = refs[8:]
        if sweep > 0:
            up_in, g_in = refs[:2]
            refs = refs[2:]
        if last:
            cut, pay_in = refs[:2]
            up_out, final_out, pay_out, slot_ref, sums = refs[2:]
        else:
            wb, lbt = refs[:2]
            up_out, g_out, gh_out = refs[2:]

        def on_faces(rows, t):
            return mask[0] * rows[0, pl.ds(t, 1), :] + mask[1] * rows[1, pl.ds(t, 1), :]

        def body(g, carry):
            t0 = g * GROUP
            corrections = back_planes(y_ref[pl.ds(t0, GROUP)], wbt[...], lb[...])
            fresh = []
            for q in range(GROUP):
                t = t0 + q
                on_u, on_g = on_faces(rows_u, t), on_faces(rows_g, t)
                load, react = f_ref[t], r_ref[t]
                if sweep == 0:
                    u, total = on_u, DAMPING * (load + on_g)
                else:
                    old = up_in[t]
                    u = old + on_u
                    total = KEEP * g_in[t] + DAMPING * (load - react * old + on_g)
                new = KEEP * u + DAMPING * corrections[q]
                if last:
                    block, index = source_layer(ints, t)

                    @pl.when(block == ints[3])
                    def _():
                        up_out[index] = new
                else:
                    up_out[t] = new
                residual = load - react * new
                if last:
                    residual = residual - total
                    for side in range(2):
                        product = cut[side] * residual
                        part = product[0:8]
                        for s in range(8, N, 8):
                            part = part + product[s:s + 8]
                        sums[side, t] = part
                else:
                    g_out[t] = total
                if last:
                    final_out[t] = residual
                fresh.append(residual)
            if not last:
                stacked = jnp.concatenate(fresh, axis=0).reshape(GROUP, N, N)
                planes = forward_planes(stacked, wb[...], lbt[...])
                for q in range(GROUP):
                    gh_out[t0 + q] = planes[q]
            return carry

        lax.fori_loop(0, HALF // GROUP, body, 0)
        if last:
            for side in range(2):
                pay_out[side, :ROWS] = pay_in[side, :ROWS]
                pay_out[side, ROWS:] = jnp.sum(sums[side], axis=1)
            slot(ints, pay_out[0], pay_out[1], slot_ref)

    return kernel


def restrict_kernel(ints, final, wrt, lr, kept, sent, plane):
    def body(g, carry):
        t0 = g * GROUP
        planes = forward_planes(final[pl.ds(t0, GROUP)], wrt[...], lr[...])
        for q in range(GROUP):
            plane[q] = planes[q]

        @pl.when(ints[1] == 1)
        def _():
            for q in range(GROUP):
                plane[q] = planes[q].T

        for half in range(2):
            for core in range(2):
                first = half * (COARSE // 2) + core * 31

                @pl.when((ints[2] == half) & (ints[3] == core))
                def _():
                    kept[pl.ds(t0, GROUP)] = plane[:, first:first + 32]

                @pl.when((ints[2] != half) & (ints[3] == core))
                def _():
                    sent[pl.ds(t0, GROUP)] = plane[:, first:first + 32]

        return carry

    lax.fori_loop(0, HALF // GROUP, body, 0)


def final_kernel(
    ints, floats, own_pay, rec, state_in, scal, nscal, mirror, mirror_coarse, mk, vert, rt_full, parts, rows_u,
):
    received = (rec[0], rec[1])
    state = read_state(state_in)
    c_faces = four(lambda side, who: received[side][:ROWS] if who else own_pay[side, :ROWS])
    state, e, masks = update_faces(c_faces, state, scal, nscal, mirror, mk, vert)
    gathered = state[5]
    products = plane_products(gathered, mk)
    far = vertical_apply(
        [products[1], products[3]], vert,
        [nscal[side, 4:5] for side in range(2)],
        [nscal[side, 5:6] for side in range(2)],
        [nscal[side, 6:7] for side in range(2)],
    )
    one = floats[0]
    near_stiff = vertical_apply([products[0], products[2]], vert, [one] * 2, [floats[3]] * 2, [floats[3]] * 2)
    near_mass = vertical_apply([products[0], products[2]], vert, [floats[3]] * 2, [floats[1]] * 2, [floats[2]] * 2)
    stack = []
    for side in range(2):
        nbr = 2 * side + 1
        theirs = pad_rows(received[side][ROWS:])
        theirs = theirs - nscal[side, 7:8] * DAMPING * state[1][nbr] * e[nbr] - far[side]
        mine = scal[side, 7:8] * DAMPING * state[1][2 * side] * e[2 * side]
        stack += [near_stiff[side], near_mass[side], mine, theirs]
    restricted = dot_full(jnp.concatenate(stack, axis=0), rt_full[...])
    pieces = [restricted[q * ROWS:(q + 1) * ROWS] for q in range(8)]
    turned = mirrored(jnp.concatenate([pieces[3], pieces[7]], axis=0), mirror_coarse[...])
    for side in range(2):
        added = jnp.where(masks[side], turned[side * ROWS:(side + 1) * ROWS], pieces[4 * side + 3])
        parts[3 * side] = -pieces[4 * side][:HALF]
        parts[3 * side + 1] = -pieces[4 * side + 1][:HALF]
        parts[3 * side + 2] = (added - pieces[4 * side + 2])[:HALF]
        rows_u[side] = DAMPING * e[2 * side]

def iterate_kernel(ints, up, rows_u, mask, out_u):
    def body(index, carry):
        inside = ints[3] * BLOCK + index
        t = jnp.where(ints[2] == 1, HALF - 1 - inside, inside)
        value = up[index] + mask[0] * rows_u[0, pl.ds(t, 1), :] + mask[1] * rows_u[1, pl.ds(t, 1), :]
        out_u[index] = value

        @pl.when(ints[1] == 1)
        def _():
            out_u[index] = value.T

        return carry

    lax.fori_loop(0, BLOCK, body, 0, unroll=2)


def vertical_kernel(ints, kept, arrived, vertical, blocks):
    for c in range(32):
        rows = pl.ds(c, HALF, stride=32)
        both = jnp.concatenate([kept[rows, :], arrived[rows, :]], axis=0)
        blocks[c] = dot_full(vertical[...], both)


def coarse_kernel(ints, start_blocks, parts, far_parts, profile, profile_rows, vertical, out, blocks, columns):
    deep = vertical.shape[0]
    spots = [0, 31, COARSE // 2, COARSE // 2 + 31]
    stacked = [jnp.concatenate([parts[s], far_parts[s]], axis=0) for s in range(6)]
    mixed = dot_full(vertical[...], jnp.concatenate(stacked, axis=1))
    mixed = [mixed[:, s * N:(s + 1) * N] for s in range(6)]

    @pl.when(ints[1] == 0)
    def _():
        first = ints[2] * (COARSE // 2) + ints[3] * 31

        for c in range(32):
            value = start_blocks[c]
            for s in range(6):
                value = value + profile[s, pl.ds(first + c, 1), :] * mixed[s]
            blocks[c] = value

    @pl.when(ints[1] == 1)
    def _():
        for half in range(2):
            for core in range(2):
                shift = (N - spots[2 * half + core]) % N

                @pl.when((ints[2] == half) & (ints[3] == core))
                def _():
                    for s in range(6):
                        columns[s] = pltpu.roll(mixed[s], shift, 1) if shift else mixed[s]

        for c in range(32):
            value = start_blocks[c]
            for s in range(6):
                value = value + columns[s, :, c:c + 1] * profile_rows[s:s + 1, :]
            blocks[c] = value

    share = out.shape[2]
    lane = lax.broadcasted_iota(jnp.int32, (deep, N), 1)
    for core in range(2):

        @pl.when(ints[3] == core)
        def _():
            start = core * (COARSE // 2)
            held = {}

            def turned(c):
                if c not in held:
                    shift = (c * COARSE - start) % N
                    held[c] = pltpu.roll(blocks[c], shift, 1) if shift else blocks[c]
                return held[c]

            for tile in range(-(-share // N)):
                low = tile * N + start
                c = low // COARSE
                value = turned(c)
                after = (c + 1) * COARSE - low
                if after < N and c + 1 < 32:
                    value = jnp.where(lane < after, value, turned(c + 1))
                if after + COARSE < N and c + 2 < 32:
                    value = jnp.where(lane < after + COARSE, value, turned(c + 2))
                width = min(N, share - tile * N)
                out[:, 0, tile * N:tile * N + width] = value[:, :width]


def prepare_kernel(
    ints, floats, stiff, mass, stiff_v, mass_v, basis, eigen, basis_v, eigen_v, restrict, restrict_v,
    wb, wbt, wrt, lb, lbt, lr, bt_out, rt_out, mk, mirror, mirror_coarse, vert, scal, spread, mask, cut,
    profile, profile_rows, alpha, bands, modes, vertical,
):
    a1, a2, a3 = floats[0], floats[1], floats[2]
    rows = lax.broadcasted_iota(jnp.int32, (N, N), 0)
    lanes = lax.broadcasted_iota(jnp.int32, (N, N), 1)
    eye = rows == lanes

    def column(row):
        picked = jnp.sum(jnp.where(eye, row, 0.0), axis=1, keepdims=True)
        return jnp.broadcast_to(picked, (N, N))

    b, k, m = basis[...], stiff[...], mass[...]
    bt = b.T
    r = jnp.concatenate([restrict[...], jnp.zeros((N - COARSE, N), F32)], axis=0)
    rt = r.T
    wb[...], wbt[...], wrt[...] = pack_right(b), pack_right(bt), pack_right(rt)
    lb[...], lbt[...], lr[...] = pack_left(b), pack_left(bt), pack_left(r)
    bt_out[...], rt_out[...] = bt, rt
    mk[:, :N], mk[:, N:] = m, k
    for out, count in ((mirror, N), (mirror_coarse, COARSE)):
        reverse = (rows + lanes == count - 1).astype(F32).astype(BF16)
        out[...] = jnp.concatenate([reverse] * 3, axis=0)
    alpha[...] = a1 * column(eigen[...]) + a2 * eigen[...]

    turn = (
        lax.broadcasted_iota(jnp.int32, (LAYERS, LAYERS), 0)
        + lax.broadcasted_iota(jnp.int32, (LAYERS, LAYERS), 1)
        == LAYERS - 1
    ).astype(F32)
    first = ints[2] == 0
    kv, mv = stiff_v[...], mass_v[...]
    ordered = []
    for matrix in (mv, a3 * kv):
        turned = dot_full(dot_full(turn, matrix), turn)
        ordered.append((jnp.where(first, matrix, turned), jnp.where(first, turned, matrix)))
    deep = lax.broadcasted_iota(jnp.int32, (ROWS, LAYERS), 0)
    wide = lax.broadcasted_iota(jnp.int32, (ROWS, LAYERS), 1)
    inside = (deep < HALF) & (wide < REACH)
    own_stiff = jnp.where(first, kv, dot_full(dot_full(turn, kv), turn))
    vert[0] = jnp.where(inside, ordered[0][0][:ROWS], 0.0)[:, :ROWS]
    vert[1] = jnp.where(inside, own_stiff[:ROWS], 0.0)[:, :ROWS]
    for which in range(2):
        for s in range(2):
            for d in range(BAND + 1):
                picked = jnp.where(deep - wide == d, ordered[s][which][:ROWS], 0.0)
                bands[which, s, d] = jnp.broadcast_to(jnp.sum(picked, axis=1, keepdims=True), (ROWS, N))

    rv = restrict_v[...]
    backwards = dot_full(rv, turn)
    vertical[:, :HALF] = jnp.where(first, rv, backwards)[:, :HALF]
    vertical[:, HALF:] = jnp.where(first, backwards, rv)[:, :HALF]

    mu = eigen_v[...]
    least = jnp.min(mu, axis=1, keepdims=True)
    number = lax.broadcasted_iota(jnp.int32, (1, LAYERS), 1)
    chosen = jnp.min(jnp.where(mu == least, number, LAYERS), axis=1, keepdims=True)
    low = jnp.sum(jnp.where(number == chosen, basis_v[...], 0.0), axis=1, keepdims=True)
    low = jnp.broadcast_to(low, (LAYERS, N))
    low_mass = dot_full(mv, low)
    low_turned, mass_turned = dot_full(turn, low), dot_full(turn, low_mass)
    modes[0] = jnp.where(first, low, low_turned)[:ROWS]
    modes[1] = jnp.where(first, low_mass, mass_turned)[:ROWS]
    modes[2] = jnp.where(first, mass_turned, low_mass)[:ROWS]
    modes[3] = jnp.broadcast_to(a3 * least, (ROWS, N))

    for side in range(2):
        start = ints[4 + side] == 0

        def end_row(matrix, count=N):
            return jnp.where(start, matrix[0:1, :], matrix[count - 1:count, :])

        def corner(matrix):
            value = jnp.where(start, matrix[0:1, 0:1], matrix[N - 1:N, N - 1:N])
            return jnp.broadcast_to(value, (1, N))

        cut_row = end_row(r, COARSE)
        cut_at = jnp.broadcast_to(jnp.where(start, cut_row[:, 0:1], cut_row[:, N - 1:N]), (1, N))
        stiff_profile = jnp.broadcast_to(jnp.sum(r * end_row(k), axis=1, keepdims=True), (N, N))
        mass_profile = jnp.broadcast_to(jnp.sum(r * end_row(m), axis=1, keepdims=True), (N, N))
        at_face = jnp.where(start, 0, COARSE - 1)
        at_rows = [stiff_profile, mass_profile, (rows == at_face).astype(F32)]
        for s in range(3):
            turned_row = jnp.sum(jnp.where(eye, at_rows[s], 0.0), axis=0, keepdims=True)
            profile_rows[3 * side + s:3 * side + s + 1, :] = turned_row
        profile[3 * side] = stiff_profile
        profile[3 * side + 1] = mass_profile
        profile[3 * side + 2] = (rows == at_face).astype(F32)
        spread[side] = column(end_row(b))
        mask[side] = (rows == ints[4 + side]).astype(F32)
        cut[side] = column(cut_row)
        scal[side] = jnp.concatenate(
            [
                corner(k) * a1,
                corner(m) * a2,
                corner(m) * a3,
                jnp.broadcast_to(ints[0].astype(F32), (1, N)),
                end_row(stiff_profile, COARSE) * a1,
                end_row(mass_profile, COARSE) * a2,
                end_row(mass_profile, COARSE) * a3,
                cut_at,
            ],
            axis=0,
        )


def per_device(
    load_vector,
    reaction,
    geometry,
    stiff_plane,
    mass_plane,
    stiff_vertical,
    mass_vertical,
    basis_plane,
    eigen_plane,
    basis_vertical,
    eigen_vertical,
    restrict_plane,
    restrict_vertical,
    patch_links,
):
    patches = lax.axis_size("patch")
    links = patch_links
    square, two = (N, N), (2, N, N)
    right = jax.ShapeDtypeStruct((2 * N, 2 * N), BF16)
    left = jax.ShapeDtypeStruct((N, 2 * N), BF16)
    thrice = jax.ShapeDtypeStruct((3 * N, N), BF16)
    (
        wb, wbt, wrt, lb, lbt, lr, basis_t, restrict_t, mk, mirror, mirror_coarse, vert, scal, spread, mask,
        cut, profile, profile_rows, alpha, bands, modes, vertical,
    ) = call(
        prepare_kernel,
        [
            right, right, right, left, left, left, square, square, (N, 2 * N), thrice, thrice,
            (2, ROWS, ROWS), (2, 8, N), two, two, two, (6, N, N), (8, N), square, (2, 2, BAND + 1, ROWS, N), (4, ROWS, N),
            restrict_vertical.shape,
        ],
        links, stiff_plane, mass_plane, stiff_vertical, mass_vertical, basis_plane, eigen_plane.reshape(1, N),
        basis_vertical, eigen_vertical.reshape(1, LAYERS), restrict_plane, restrict_vertical,
        geometry=geometry, flops=20_000_000,
    )

    pair = [(0, 1), (1, 0), (2, 3), (3, 2)]
    cross = [(0, 2), (2, 0), (1, 3), (3, 1)]
    chips = [[0, 1], [2, 3]]
    faces = []
    for p in range(patches):
        for h in range(2):
            west, east = 4 * p + 2 * h + 1, 4 * ((p + 1) % patches) + 2 * h
            faces += [(west, east), (east, west)]

    def swap_faces(slot_values):
        arrived = lax.ppermute(slot_values, ("patch", "slab"), faces)
        return lambda: lax.all_gather(arrived, "slab", axis_index_groups=chips)

    field = (HALF, N, N)
    own_load = load_vector[0].reshape(BLOCK, N, N)
    own_react = reaction[0].reshape(BLOCK, N, N)
    other_load = lax.ppermute(own_load, "slab", pair)
    other_react = lax.ppermute(own_react, "slab", pair)
    size = ROWS + 8
    f, pay, slot_values = call(
        load_kernel, [field, (2, size, N), (size, N)], links, own_load, other_load
    )
    arriving = swap_faces(slot_values)
    l, dinv = call(
        factor_kernel, [(HALF, BAND, N, N), field], links, slot_values, alpha, bands, flops=3_000_000_000
    )
    (gh,) = call(transform_kernel, [field], links, f, wb, lbt, flops=2_000_000_000)
    rec = arriving()
    rows_hat = pltpu.VMEM((2, ROWS, N), F32)
    sums = pltpu.VMEM((2, ROWS, 8, N), F32)
    message = (BAND + 1, N // 2, N)
    message_full = (BAND, N, N)
    state_shape = (6, 4, ROWS, N)
    rows_shape = (2, ROWS, N)
    up = total = None
    for sweep in range(SWEEPS):
        if sweep == 0:
            z, msg, low, state, rows_u, rows_g = call(
                first_kernel,
                [field, message, square, state_shape, rows_shape, rows_shape],
                links, gh, pay, rec, scal, spread, wb, mirror, l, modes,
                scratch=[rows_hat], flops=10_000_000,
            )
        else:
            if sweep == 1:
                nscal = rec[:, ROWS + HALF:]
            z, msg, low, state, rows_u, rows_g = call(
                next_kernel,
                [field, message, square, state_shape, rows_shape, rows_shape],
                links, gh, pay, rec, state, scal, nscal, spread, wb, mirror, mk, vert, l, modes,
                scratch=[rows_hat], flops=10_000_000,
            )
        if sweep > 0:
            received = lax.all_gather(msg, "slab")
        else:
            crossing = lax.ppermute(msg, "slab", cross)
            r, react_faces = call(reaction_kernel, [field, (2, HALF, N)], links, msg, own_react, other_react)
            lm, dm, lo, do, mend = call(
                meet_kernel,
                [(BAND, BAND, N, N), message_full, (2 * BAND, BAND, N, N), message_full, square],
                links, alpha, bands, modes, l, dinv,
                scratch=[pltpu.VMEM((TOP, FACTOR_ROWS, N), F32)], flops=5_000_000_000,
            )
            received = lax.all_gather(crossing, "slab", axis_index_groups=chips)
        last = sweep == SWEEPS - 1
        size = ROWS + HALF + 8 if sweep == 0 else ROWS
        extra = [react_faces, scal] if sweep == 0 else []
        y, pay, *slot_values = call(
            solve_kernel,
            [(REACH, N, N), (2, size, N)] + ([] if last else [(size, N)]),
            links, z, low, received, l, dinv, lm, dm, lo, do, mend, modes, spread, basis_t, state, *extra,
            scratch=[sums], flops=10_000_000,
        )
        args = [y, f, r, rows_u, rows_g, mask, wbt, lb]
        if sweep > 0:
            args += [up, total]
        plane_kernel = make_plane_kernel(sweep)
        if last:
            size = ROWS + HALF
            block = (HALF, 32, N)
            up, final, pay, slot_values = call(
                plane_kernel,
                [(BLOCK, N, N), field, (2, size, N), (size, N)],
                links, *args, cut, pay,
                scratch=[pltpu.VMEM((2, HALF, 8, N), F32)], flops=3_000_000_000,
            )
            arriving = swap_faces(slot_values)
            kept, sent = call(
                restrict_kernel, [block, block], links, final, wrt, lr,
                scratch=[pltpu.VMEM((GROUP, N, N), F32)], flops=3_000_000_000,
            )
            arrived = lax.ppermute(sent, "slab", cross)
            rec = arriving()
        else:
            arriving = swap_faces(slot_values[0])
            up, total, gh = call(
                plane_kernel, [field, field, field], links, *args, wb, lbt, flops=4_000_000_000
            )
            rec = arriving()
    parts, rows_u = call(
        final_kernel,
        [(6, HALF, N), rows_shape],
        links, pay, rec, state, scal, nscal, mirror, mirror_coarse, mk, vert, restrict_t,
        geometry=geometry, flops=80_000_000_000,
    )
    far_parts = lax.ppermute(parts, "slab", cross)
    (out_u,) = call(iterate_kernel, [(BLOCK, N, N)], links, up, rows_u, mask, flops=4_000_000_000)
    deep = restrict_vertical.shape[0]
    share = COARSE * COARSE // 4
    (blocks,) = call(
        vertical_kernel, [(32, deep, N)],
        links, kept.reshape(HALF * 32, N), arrived.reshape(HALF * 32, N), vertical, flops=1000, moved=1000,
    )
    (flat,) = call(
        coarse_kernel,
        [(deep, 1, share)],
        links, blocks, parts, far_parts, profile, profile_rows, vertical,
        scratch=[pltpu.VMEM((32, deep, N), F32), pltpu.VMEM((6, deep, N), F32)],
        flops=20_000_000_000,
    )
    return out_u.reshape(1, BLOCK, N * N), flat.transpose(1, 0, 2)


def solution(mesh):
    in_specs = (
        P("patch", "slab", None),
        P("patch", "slab", None),
        P("patch", None),
        P(), P(), P(), P(), P(), P(), P(), P(), P(), P(),
        P("patch", None),
    )
    out_specs = (P("patch", "slab", None), P("patch", None, "slab"))
    return jax.shard_map(
        per_device, mesh=mesh, in_specs=in_specs, out_specs=out_specs, check_vma=False
    )
```

```python
import jax
import jax.numpy as jnp
from jax import lax
from jax.experimental import pallas as pl
from jax.experimental.pallas import tpu as pltpu
from jax.sharding import PartitionSpec as P

BAND = 4
SWEEPS = 3
DAMPING = 0.25
KEEP = 1.0 - DAMPING
HIGHEST = lax.Precision.HIGHEST
F32 = jnp.float32
BF16 = jnp.bfloat16

N = 128
LAYERS = 64
HALF = 32
BLOCK = 16
REACH = HALF + BAND
ROWS = 40
TOP = HALF - BAND
CHUNK = 32
COARSE = N - 2


def split(x):
    high = x.astype(BF16)
    return high, (x - high.astype(F32)).astype(BF16)


def right_mul(x, packed):
    high, low = split(x)
    both = jnp.dot(jnp.concatenate([high, low], axis=-1), packed, preferred_element_type=F32)
    return both[:, :N] + both[:, N:]


def left_mul_planes(packed, planes):
    out = []
    for q in range(0, len(planes), 2):
        high, low = split(jnp.concatenate(planes[q:q + 2], axis=1))
        wide = jnp.dot(packed, jnp.concatenate([high, high], axis=0), preferred_element_type=F32)
        wide = wide + jnp.dot(packed[:, :N], low, preferred_element_type=F32)
        out += [wide[:, :N], wide[:, N:]]
    return out


def dot_full(x, y):
    return jnp.dot(x, y, precision=HIGHEST, preferred_element_type=F32)


def mirrored(x, mirror):
    high, rest = split(x)
    middle, low = split(x - high.astype(F32))
    return jnp.dot(
        jnp.concatenate([high, middle, low], axis=-1), mirror, preferred_element_type=F32
    )


def pack_right(a):
    high, low = split(a)
    top = jnp.concatenate([high, low], axis=1)
    bottom = jnp.concatenate([high, jnp.zeros_like(low)], axis=1)
    return jnp.concatenate([top, bottom], axis=0)


def pack_left(a):
    return jnp.concatenate(split(a), axis=1)


def call(kernel, outs, links, *args, flops=0, scratch=(), geometry=None, moved=None):
    smem = [links] if geometry is None else [links, geometry]
    specs = [pl.BlockSpec(memory_space=pltpu.SMEM)] * len(smem)
    specs += [pl.BlockSpec(memory_space=pltpu.VMEM)] * len(args)
    shapes = [s if isinstance(s, jax.ShapeDtypeStruct) else jax.ShapeDtypeStruct(s, F32) for s in outs]
    if moved is None:
        moved = sum(a.size * a.dtype.itemsize for a in args) + sum(4 * s.size for s in shapes)

    def body(links_ref, *refs):
        ints = facts(links_ref)
        if geometry is None:
            kernel(ints, *refs)
        else:
            kernel(ints, scales(ints, refs[0]), *refs[1:])

    return pl.pallas_call(
        body,
        out_shape=shapes,
        in_specs=specs,
        out_specs=[pl.BlockSpec(memory_space=pltpu.VMEM)] * len(outs),
        scratch_shapes=list(scratch),
        compiler_params=pltpu.CompilerParams(vmem_limit_bytes=16 * 1024 * 1024),
        cost_estimate=pl.CostEstimate(
            flops=flops, bytes_accessed=moved, transcendentals=0
        ),
    )(*smem, *args)


def facts(links):
    slab = lax.axis_index("slab")
    west, east = links[0, 0], links[0, 1]
    return (
        links[0, 2], jnp.right_shift(west, 1), jnp.right_shift(slab, 1), jnp.bitwise_and(slab, 1),
        (N - 1) * jnp.bitwise_and(west, 1), (N - 1) * jnp.bitwise_and(east, 1),
    )


def scales(ints, geometry):
    turned = ints[1] == 1
    first, second = geometry[0, 0], geometry[0, 1]
    return (
        jnp.where(turned, second, first), jnp.where(turned, first, second), geometry[0, 2], jnp.float32(0),
    )


def source_layer(ints, t):
    inside = jnp.where(ints[2] == 1, HALF - 1 - t, t)
    return jnp.right_shift(inside, 4), jnp.bitwise_and(inside, BLOCK - 1)


def load_layers(ints, own_ref, other_ref, out_ref):
    def run(turn):
        def body(g, carry):
            for q in range(8):
                t = g * 8 + q
                block, index = source_layer(ints, t)
                value = jnp.where(block == ints[3], own_ref[index], other_ref[index])
                out_ref[t] = value.T if turn else value
            return carry

        lax.fori_loop(0, HALF // 8, body, 0)

    @pl.when(ints[1] == 0)
    def _():
        run(False)

    @pl.when(ints[1] == 1)
    def _():
        run(True)


def slot(ints, west, east, slot_ref):
    slot_ref[...] = jnp.where(ints[3] == 0, west, east)


def face_rows(ints, ref, side):
    position = ints[4 + side]
    return jnp.where(position == 0, ref[:, 0, :], ref[:, N - 1, :])


def load_kernel(ints, own, other, f_ref, pay_ref, slot_ref):
    load_layers(ints, own, other, f_ref)
    flag = jnp.broadcast_to(ints[0].astype(F32), (8, N))
    for side in range(2):
        rows = face_rows(ints, f_ref, side)
        pay_ref[side] = jnp.concatenate([rows, jnp.zeros((ROWS - HALF, N), F32), flag], axis=0)
    slot(ints, pay_ref[0], pay_ref[1], slot_ref)


def reaction_kernel(ints, ready, own, other, r_ref, face_ref):
    load_layers(ints, own, other, r_ref)
    for side in range(2):
        face_ref[side] = face_rows(ints, r_ref, side)


def forward_planes(x, wb, lbt):
    count = x.shape[0]
    first = right_mul(x.reshape(count * N, N), wb).reshape(count, N, N)
    return left_mul_planes(lbt, [first[q] for q in range(count)])


GROUP = 32


def transform_kernel(ints, f_ref, wb, lbt, out_ref):
    def body(g, carry):
        t = g * GROUP
        planes = forward_planes(f_ref[pl.ds(t, GROUP)], wb[...], lbt[...])
        for q in range(GROUP):
            out_ref[t + q] = planes[q]
        return carry

    lax.fori_loop(0, HALF // GROUP, body, 0)


FACTOR_ROWS = 16


def coefficient(bands, alpha, which, t, d):
    return alpha * bands[which, 0, d, t:t + 1, :] + bands[which, 1, d, t:t + 1, :]


def row_weights(a, l, t, least):
    w = {}
    for d in range(min(BAND, t), least - 1, -1):
        v = a[d]
        for m in range(d + 1, min(BAND, t) + 1):
            v = v - w[m] * l[t - d][m - d]
        w[d] = v
    return w


def eliminate(a, l, dinv, t):
    w = row_weights(a, l, t, 1)
    row = {d: w[d] * dinv[t - d] for d in w}
    pivot = a[0]
    for d in w:
        pivot = pivot - w[d] * row[d]
    return row, 1.0 / pivot


def factor_kernel(ints, ready, alpha_ref, bands, l_ref, dinv_ref):
    def body(c, carry):
        part = pl.ds(c * FACTOR_ROWS, FACTOR_ROWS)
        alpha = alpha_ref[part, :]
        l, dinv = {}, {}
        for t in range(HALF):
            a = [coefficient(bands, alpha, 0, t, d) for d in range(min(BAND, t) + 1)]
            l[t], dinv[t] = eliminate(a, l, dinv, t)
            for d in l[t]:
                l_ref[t, d - 1, part, :] = l[t][d]
            dinv_ref[t, part, :] = dinv[t]
        return carry

    lax.fori_loop(0, N // FACTOR_ROWS, body, 0)


def meet_kernel(
    ints, alpha_ref, bands, modes, l_ref, dinv_ref, lm_ref, dm_ref, lo_ref, do_ref, mend_ref, zs
):
    def mode(which, t):
        return modes[which, t:t + 1, :]

    def body(c, carry):
        part = pl.ds(c * FACTOR_ROWS, FACTOR_ROWS)
        alpha = alpha_ref[part, :]
        l, dinv, sent = {}, {}, {}
        for t in range(HALF):
            a = [coefficient(bands, alpha, 1, t, d) for d in range(min(BAND, t) + 1)]
            l[t], dinv[t] = eliminate(a, l, dinv, t)
            sent[t] = jnp.broadcast_to(mode(2, t), alpha.shape)
            for d in l[t]:
                sent[t] = sent[t] - l[t][d] * sent[t - d]
            if t >= TOP:
                for d in range(1, BAND + 1):
                    lo_ref[t - TOP, d - 1, part, :] = l[t][d]
                do_ref[t - TOP, part, :] = dinv[t]
        outer = {}
        for j in range(BAND):
            t = HALF + j
            a = [coefficient(bands, alpha, 1, t, d) for d in range(BAND + 1)]
            outer[j] = row_weights(a, l, t, j + 1)
            l[t] = {d: outer[j][d] * dinv[t - d] for d in outer[j]}
            for d in l[t]:
                lo_ref[BAND + j, d - 1, part, :] = l[t][d]
        schur = {}
        for j in range(BAND):
            for i in range(j + 1):
                total = None
                for s in range(TOP + j, HALF):
                    term = outer[j][HALF + j - s] * l[HALF + i][HALF + i - s]
                    total = term if total is None else total + term
                schur[(j, i)] = schur[(i, j)] = total
        shift = {}
        for j in range(BAND):
            for d in range(j + 1, BAND + 1):
                term = l[HALF + j][d] * sent[HALF + j - d]
                shift[j] = term if j not in shift else shift[j] + term
        z = {}
        for t in range(TOP):
            z[t] = jnp.broadcast_to(mode(1, t), alpha.shape)
            for d in range(1, min(BAND, t) + 1):
                z[t] = z[t] - l_ref[t, d - 1, part, :] * z[t - d]
            zs[t] = z[t]
        l = {
            t: {d: l_ref[t, d - 1, part, :] for d in range(1, BAND + 1)} for t in range(TOP - BAND, TOP)
        }
        dinv = {t: dinv_ref[t, part, :] for t in range(TOP - BAND, TOP)}
        for t in range(TOP, HALF):
            a = [coefficient(bands, alpha, 0, t, d) for d in range(BAND + 1)]
            j = HALF - 1 - t
            for d in range(t - TOP + 1):
                a[d] = a[d] - schur[(j, j + d)]
            l[t], dinv[t] = eliminate(a, l, dinv, t)
            for d in range(1, BAND + 1):
                lm_ref[t - TOP, d - 1, part, :] = l[t][d]
            dm_ref[t - TOP, part, :] = dinv[t]
            z[t] = mode(1, t) - shift[j]
            for d in range(1, BAND + 1):
                z[t] = z[t] - l[t][d] * z[t - d]
        exact = 1.0 / (alpha + modes[3, 0:1, :])
        y, miss, norm = {}, jnp.zeros_like(alpha), jnp.zeros_like(modes[3, 0:1, :])
        for t in range(HALF - 1, -1, -1):
            y[t] = z[t] * dinv[t] if t >= TOP else zs[t] * dinv_ref[t, part, :]
            for d in range(1, min(BAND, HALF - 1 - t) + 1):
                factor = l[t + d][d] if t + d >= TOP else l_ref[t + d, d - 1, part, :]
                y[t] = y[t] - factor * y[t + d]
            miss = miss + mode(1, t) * (mode(0, t) * exact - y[t])
            norm = norm + mode(1, t) * mode(0, t)
        mend_ref[part, :] = jnp.where(norm > 0.01, miss / jnp.maximum(norm, 0.01), 0.0)
        return carry

    lax.fori_loop(0, N // FACTOR_ROWS, body, 0)


def four(get):
    return [get(side, who) for side in range(2) for who in range(2)]


def vertical_apply(products, vert, scal_k, scal_m, scal_v):
    mass = [k * p[:, :N] + m * p[:, N:] for p, k, m in zip(products, scal_k, scal_m)]
    stiff = [v * p[:, :N] for p, v in zip(products, scal_v)]
    out = dot_full(vert[0], jnp.concatenate(mass, axis=1))
    out = out + dot_full(vert[1], jnp.concatenate(stiff, axis=1))
    return [out[:, q * N:(q + 1) * N] for q in range(len(products))]


def plane_products(faces, mk):
    stacked = dot_full(jnp.concatenate(faces, axis=0), mk[...])
    return [stacked[q * ROWS:(q + 1) * ROWS] for q in range(len(faces))]


def flip_masks(scal, nscal):
    return [scal[side, 3:4, :] != nscal[side, 3:4, :] for side in range(2)]


def orient_all(arrays, mirror, masks):
    turned = mirrored(jnp.concatenate([a for _, a in arrays], axis=0), mirror[...])
    return [
        jnp.where(masks[side], turned[q * ROWS:(q + 1) * ROWS], a)
        for q, (side, a) in enumerate(arrays)
    ]


def update_faces(c_faces, state, scal, nscal, mirror, mk, vert):
    masks = flip_masks(scal, nscal)
    residual = four(lambda side, who: state[4][2 * side + who])
    arrays = []
    for side in range(2):
        for who in range(2):
            arrays.append((side, c_faces[2 * side + 1 - who]))
    for side in range(2):
        for who in range(2):
            arrays.append((side, residual[2 * side + 1 - who]))
    turned = orient_all(arrays, mirror, masks)
    e, added = turned[:4], turned[4:]
    products = plane_products(e, mk)
    which = four(lambda side, who: (nscal if who else scal)[side])
    applied = vertical_apply(
        products, vert, [w[0:1] for w in which], [w[1:2] for w in which], [w[2:3] for w in which]
    )
    new = [list(state[s]) for s in range(6)]
    for q in range(4):
        new[2][q] = state[2][q] + DAMPING * (c_faces[q] + e[q])
        new[3][q] = state[3][q] + DAMPING * (residual[q] + added[q] + applied[q])
        new[4][q] = state[0][q] - state[1][q] * new[2][q] - new[3][q]
        new[5][q] = KEEP * state[5][q] + DAMPING * e[q]
    return new, e, masks


def read_state(ref):
    return [[ref[s, q] for q in range(4)] for s in range(6)]


def pad_rows(x):
    return jnp.concatenate([x, jnp.zeros((ROWS - x.shape[0], N), F32)], axis=0)


def eliminate_forward(gh_ref, spread, rows_hat, l_ref, modes, z_ref, msg_ref, low_ref, core):
    def body(c, carry):
        part = pl.ds(pl.multiple_of(c * CHUNK, CHUNK), CHUNK)
        west, east = spread[0, part, :], spread[1, part, :]
        z = {}
        lowest = jnp.zeros_like(west)
        for t in range(HALF):
            x = gh_ref[t, part, :] + west * rows_hat[0, t:t + 1, :] + east * rows_hat[1, t:t + 1, :]
            lowest = lowest + modes[0, t:t + 1, :] * x
            z_ref[t, part, :] = x
            for d in range(min(BAND, t), 0, -1):
                x = x - l_ref[t, d - 1, part, :] * z[t - d]
            z[t] = x
            if t < TOP:
                z_ref[t, part, :] = x
        low_ref[part, :] = lowest

        @pl.when(jnp.right_shift(c, 1) == core)
        def _():
            there = pl.ds(pl.multiple_of(jnp.bitwise_and(c, 1) * CHUNK, CHUNK), CHUNK)
            for s in range(BAND):
                msg_ref[s, there, :] = z[TOP + s]
            msg_ref[BAND, there, :] = lowest

        return carry

    lax.fori_loop(0, N // CHUNK, body, 0)


def first_kernel(
    ints, gh, own_pay, rec, scal, spread, wb, mirror, l_ref, modes,
    z_ref, msg_ref, low_ref, state_ref, rows_u, rows_g, rows_hat,
):
    received = (rec[0], rec[1])
    masks = [received[side][ROWS:ROWS + 1] != scal[side, 3:4, :] for side in range(2)]
    state_ref[...] = jnp.zeros_like(state_ref)
    for side in range(2):
        for who in range(2):
            values = received[side][:ROWS] if who else own_pay[side, :ROWS]
            state_ref[0, 2 * side + who] = values
            state_ref[4, 2 * side + who] = values
    turned = orient_all([(side, received[side][:ROWS]) for side in range(2)], mirror, masks)
    rows_u[...] = jnp.zeros_like(rows_u)
    for side in range(2):
        rows_g[side] = turned[side]
        rows_hat[side] = right_mul(turned[side], wb[...])
    eliminate_forward(gh, spread, rows_hat, l_ref, modes, z_ref, msg_ref, low_ref, ints[3])


def next_kernel(
    ints, gh, own_pay, rec, state_in, scal, nscal, spread, wb, mirror, mk, vert,
    l_ref, modes, z_ref, msg_ref, low_ref, state_ref, rows_u, rows_g, rows_hat,
):
    received = (rec[0], rec[1])
    state = read_state(state_in)
    if own_pay.shape[1] > ROWS:
        for side in range(2):
            state[1][2 * side] = pad_rows(own_pay[side, ROWS:ROWS + HALF])
            state[1][2 * side + 1] = pad_rows(received[side][ROWS:ROWS + HALF])
    c_faces = four(lambda side, who: received[side][:ROWS] if who else own_pay[side, :ROWS])
    state, e, masks = update_faces(c_faces, state, scal, nscal, mirror, mk, vert)
    for s in range(6):
        for q in range(4):
            state_ref[s, q] = state[s][q]
    turned = orient_all([(side, state[4][2 * side + 1]) for side in range(2)], mirror, masks)
    for side in range(2):
        step = DAMPING * e[2 * side]
        rows = turned[side] - state[1][2 * side] * step
        rows_u[side] = step
        rows_g[side] = rows
        rows_hat[side] = right_mul(rows, wb[...])
    eliminate_forward(gh, spread, rows_hat, l_ref, modes, z_ref, msg_ref, low_ref, ints[3])


def solve_kernel(
    ints, z_ref, low_ref, zr_ref, l_ref, dinv_ref, lm_ref, dm_ref, lo_ref, do_ref, mend, modes, spread, bt_full, state, *refs,
):
    sums = refs[-1]
    extra = refs[:2] if len(refs) > 4 else ()
    outs = refs[len(extra):-1]
    y_ref, pay_ref = outs[:2]
    sums[...] = jnp.zeros_like(sums)

    def body(c, carry):
        part = pl.ds(pl.multiple_of(c * CHUNK, CHUNK), CHUNK)
        source = jnp.right_shift(c, 1)
        if zr_ref.shape[0] > 2:
            source = source + 2 * (1 - ints[2])
        there = pl.ds(pl.multiple_of(jnp.bitwise_and(c, 1) * CHUNK, CHUNK), CHUNK)
        sent = [zr_ref[source, s, there, :] for s in range(BAND)]
        weights = (spread[0, part, :], spread[1, part, :])

        low = mend[part, :] * (low_ref[part, :] + zr_ref[source, BAND, there, :])

        def put(t, value):
            value = value + low * modes[0, t:t + 1, :]
            y_ref[t, part, :] = value
            for side in range(2):
                product = weights[side] * value
                total = product[0:8]
                for s in range(8, CHUNK, 8):
                    total = total + product[s:s + 8]
                sums[side, t] += total

        z = {t: z_ref[t, part, :] for t in range(TOP - BAND, HALF)}
        for j in range(BAND):
            for d in range(j + 1, BAND + 1):
                z[HALF - 1 - j] = z[HALF - 1 - j] - lo_ref[BAND + j, d - 1, part, :] * sent[BAND + j - d]
        for t in range(TOP, HALF):
            for d in range(BAND, 0, -1):
                z[t] = z[t] - lm_ref[t - TOP, d - 1, part, :] * z[t - d]

        def factor(t, d):
            return lm_ref[t - TOP, d - 1, part, :] if t >= TOP else l_ref[t, d - 1, part, :]

        y = {}
        for t in range(HALF - 1, TOP - 1, -1):
            value = z[t] * dm_ref[t - TOP, part, :]
            for d in range(HALF - 1 - t, 0, -1):
                value = value - factor(t + d, d) * y[t + d]
            y[t] = value
            put(t, value)
        far = {HALF + j: y[HALF - 1 - j] for j in range(BAND)}
        for t in range(HALF - 1, TOP - 1, -1):
            value = sent[t - TOP] * do_ref[t - TOP, part, :]
            for d in range(BAND, 0, -1):
                value = value - lo_ref[t + d - TOP, d - 1, part, :] * far[t + d]
            far[t] = value
            put(2 * HALF - 1 - t, value)
        for t in range(TOP - 1, -1, -1):
            known = z[t] if t in z else z_ref[t, part, :]
            value = known * dinv_ref[t, part, :]
            for d in range(BAND, 0, -1):
                value = value - factor(t + d, d) * y[t + d]
            y[t] = value
            put(t, value)
        return carry

    lax.fori_loop(0, N // CHUNK, body, 0)
    mixed = jnp.sum(sums[...], axis=2)
    faces = dot_full(mixed.reshape(2 * ROWS, N), bt_full[...])
    packs = []
    for side in range(2):
        c = faces[side * ROWS:(side + 1) * ROWS] - state[2, 2 * side]
        pay_ref[side, :ROWS] = c
        if extra:
            pay_ref[side, ROWS:ROWS + HALF] = extra[0][side]
            pay_ref[side, ROWS + HALF:] = extra[1][side]
    for slot_ref in outs[2:]:
        slot(ints, pay_ref[0], pay_ref[1], slot_ref)


def back_planes(y, wbt, lb):
    count = y.shape[0]
    across = right_mul(y.reshape(count * N, N), wbt).reshape(count, N, N)
    return left_mul_planes(lb, [across[q] for q in range(count)])


def make_plane_kernel(sweep):
    last = sweep == SWEEPS - 1

    def kernel(ints, *refs):
        refs = list(refs)
        y_ref, f_ref, r_ref, rows_u, rows_g, mask, wbt, lb = refs[:8]
        refs = refs[8:]
        if sweep > 0:
            up_in, g_in = refs[:2]
            refs = refs[2:]
        if last:
            cut, pay_in = refs[:2]
            up_out, final_out, pay_out, slot_ref, sums = refs[2:]
        else:
            wb, lbt = refs[:2]
            up_out, g_out, gh_out = refs[2:]

        def on_faces(rows, t):
            return mask[0] * rows[0, pl.ds(t, 1), :] + mask[1] * rows[1, pl.ds(t, 1), :]

        def body(g, carry):
            t0 = g * GROUP
            corrections = back_planes(y_ref[pl.ds(t0, GROUP)], wbt[...], lb[...])
            fresh = []
            for q in range(GROUP):
                t = t0 + q
                on_u, on_g = on_faces(rows_u, t), on_faces(rows_g, t)
                load, react = f_ref[t], r_ref[t]
                if sweep == 0:
                    u, total = on_u, DAMPING * (load + on_g)
                else:
                    old = up_in[t]
                    u = old + on_u
                    total = KEEP * g_in[t] + DAMPING * (load - react * old + on_g)
                new = KEEP * u + DAMPING * corrections[q]
                if last:
                    block, index = source_layer(ints, t)

                    @pl.when(block == ints[3])
                    def _():
                        up_out[index] = new
                else:
                    up_out[t] = new
                residual = load - react * new
                if last:
                    residual = residual - total
                    for side in range(2):
                        product = cut[side] * residual
                        part = product[0:8]
                        for s in range(8, N, 8):
                            part = part + product[s:s + 8]
                        sums[side, t] = part
                else:
                    g_out[t] = total
                if last:
                    final_out[t] = residual
                fresh.append(residual)
            if not last:
                stacked = jnp.concatenate(fresh, axis=0).reshape(GROUP, N, N)
                planes = forward_planes(stacked, wb[...], lbt[...])
                for q in range(GROUP):
                    gh_out[t0 + q] = planes[q]
            return carry

        lax.fori_loop(0, HALF // GROUP, body, 0)
        if last:
            for side in range(2):
                pay_out[side, :ROWS] = pay_in[side, :ROWS]
                pay_out[side, ROWS:] = jnp.sum(sums[side], axis=1)
            slot(ints, pay_out[0], pay_out[1], slot_ref)

    return kernel


def restrict_kernel(ints, final, wrt, lr, kept, sent, plane):
    def body(g, carry):
        t0 = g * GROUP
        planes = forward_planes(final[pl.ds(t0, GROUP)], wrt[...], lr[...])
        for q in range(GROUP):
            plane[q] = planes[q]

        @pl.when(ints[1] == 1)
        def _():
            for q in range(GROUP):
                plane[q] = planes[q].T

        for half in range(2):
            for core in range(2):
                first = half * (COARSE // 2) + core * 31

                @pl.when((ints[2] == half) & (ints[3] == core))
                def _():
                    kept[pl.ds(t0, GROUP)] = plane[:, first:first + 32]

                @pl.when((ints[2] != half) & (ints[3] == core))
                def _():
                    sent[pl.ds(t0, GROUP)] = plane[:, first:first + 32]

        return carry

    lax.fori_loop(0, HALF // GROUP, body, 0)


def final_kernel(
    ints, floats, own_pay, rec, state_in, scal, nscal, mirror, mirror_coarse, mk, vert, rt_full, parts, rows_u,
):
    received = (rec[0], rec[1])
    state = read_state(state_in)
    c_faces = four(lambda side, who: received[side][:ROWS] if who else own_pay[side, :ROWS])
    state, e, masks = update_faces(c_faces, state, scal, nscal, mirror, mk, vert)
    gathered = state[5]
    products = plane_products(gathered, mk)
    far = vertical_apply(
        [products[1], products[3]], vert,
        [nscal[side, 4:5] for side in range(2)],
        [nscal[side, 5:6] for side in range(2)],
        [nscal[side, 6:7] for side in range(2)],
    )
    one = floats[0]
    near_stiff = vertical_apply([products[0], products[2]], vert, [one] * 2, [floats[3]] * 2, [floats[3]] * 2)
    near_mass = vertical_apply([products[0], products[2]], vert, [floats[3]] * 2, [floats[1]] * 2, [floats[2]] * 2)
    stack = []
    for side in range(2):
        nbr = 2 * side + 1
        theirs = pad_rows(received[side][ROWS:])
        theirs = theirs - nscal[side, 7:8] * DAMPING * state[1][nbr] * e[nbr] - far[side]
        mine = scal[side, 7:8] * DAMPING * state[1][2 * side] * e[2 * side]
        stack += [near_stiff[side], near_mass[side], mine, theirs]
    restricted = dot_full(jnp.concatenate(stack, axis=0), rt_full[...])
    pieces = [restricted[q * ROWS:(q + 1) * ROWS] for q in range(8)]
    turned = mirrored(jnp.concatenate([pieces[3], pieces[7]], axis=0), mirror_coarse[...])
    for side in range(2):
        added = jnp.where(masks[side], turned[side * ROWS:(side + 1) * ROWS], pieces[4 * side + 3])
        parts[3 * side] = -pieces[4 * side][:HALF]
        parts[3 * side + 1] = -pieces[4 * side + 1][:HALF]
        parts[3 * side + 2] = (added - pieces[4 * side + 2])[:HALF]
        rows_u[side] = DAMPING * e[2 * side]

def iterate_kernel(ints, up, rows_u, mask, out_u):
    def body(index, carry):
        inside = ints[3] * BLOCK + index
        t = jnp.where(ints[2] == 1, HALF - 1 - inside, inside)
        value = up[index] + mask[0] * rows_u[0, pl.ds(t, 1), :] + mask[1] * rows_u[1, pl.ds(t, 1), :]
        out_u[index] = value

        @pl.when(ints[1] == 1)
        def _():
            out_u[index] = value.T

        return carry

    lax.fori_loop(0, BLOCK, body, 0, unroll=2)


def vertical_kernel(ints, kept, arrived, vertical, blocks):
    for c in range(32):
        rows = pl.ds(c, HALF, stride=32)
        both = jnp.concatenate([kept[rows, :], arrived[rows, :]], axis=0)
        blocks[c] = dot_full(vertical[...], both)


def coarse_kernel(ints, start_blocks, parts, far_parts, profile, profile_rows, vertical, out, blocks, columns):
    deep = vertical.shape[0]
    spots = [0, 31, COARSE // 2, COARSE // 2 + 31]
    stacked = [jnp.concatenate([parts[s], far_parts[s]], axis=0) for s in range(6)]
    mixed = dot_full(vertical[...], jnp.concatenate(stacked, axis=1))
    mixed = [mixed[:, s * N:(s + 1) * N] for s in range(6)]

    @pl.when(ints[1] == 0)
    def _():
        first = ints[2] * (COARSE // 2) + ints[3] * 31

        for c in range(32):
            value = start_blocks[c]
            for s in range(6):
                value = value + profile[s, pl.ds(first + c, 1), :] * mixed[s]
            blocks[c] = value

    @pl.when(ints[1] == 1)
    def _():
        for half in range(2):
            for core in range(2):
                shift = (N - spots[2 * half + core]) % N

                @pl.when((ints[2] == half) & (ints[3] == core))
                def _():
                    for s in range(6):
                        columns[s] = pltpu.roll(mixed[s], shift, 1) if shift else mixed[s]

        for c in range(32):
            value = start_blocks[c]
            for s in range(6):
                value = value + columns[s, :, c:c + 1] * profile_rows[s:s + 1, :]
            blocks[c] = value

    share = out.shape[2]
    lane = lax.broadcasted_iota(jnp.int32, (deep, N), 1)
    for core in range(2):

        @pl.when(ints[3] == core)
        def _():
            start = core * (COARSE // 2)
            held = {}

            def turned(c):
                if c not in held:
                    shift = (c * COARSE - start) % N
                    held[c] = pltpu.roll(blocks[c], shift, 1) if shift else blocks[c]
                return held[c]

            for tile in range(-(-share // N)):
                low = tile * N + start
                c = low // COARSE
                value = turned(c)
                after = (c + 1) * COARSE - low
                if after < N and c + 1 < 32:
                    value = jnp.where(lane < after, value, turned(c + 1))
                if after + COARSE < N and c + 2 < 32:
                    value = jnp.where(lane < after + COARSE, value, turned(c + 2))
                width = min(N, share - tile * N)
                out[:, 0, tile * N:tile * N + width] = value[:, :width]


def prepare_kernel(
    ints, floats, stiff, mass, stiff_v, mass_v, basis, eigen, basis_v, eigen_v, restrict, restrict_v,
    wb, wbt, wrt, lb, lbt, lr, bt_out, rt_out, mk, mirror, mirror_coarse, vert, scal, spread, mask, cut,
    profile, profile_rows, alpha, bands, modes, vertical,
):
    a1, a2, a3 = floats[0], floats[1], floats[2]
    rows = lax.broadcasted_iota(jnp.int32, (N, N), 0)
    lanes = lax.broadcasted_iota(jnp.int32, (N, N), 1)
    eye = rows == lanes

    def column(row):
        picked = jnp.sum(jnp.where(eye, row, 0.0), axis=1, keepdims=True)
        return jnp.broadcast_to(picked, (N, N))

    b, k, m = basis[...], stiff[...], mass[...]
    bt = b.T
    r = jnp.concatenate([restrict[...], jnp.zeros((N - COARSE, N), F32)], axis=0)
    rt = r.T
    wb[...], wbt[...], wrt[...] = pack_right(b), pack_right(bt), pack_right(rt)
    lb[...], lbt[...], lr[...] = pack_left(b), pack_left(bt), pack_left(r)
    bt_out[...], rt_out[...] = bt, rt
    mk[:, :N], mk[:, N:] = m, k
    for out, count in ((mirror, N), (mirror_coarse, COARSE)):
        reverse = (rows + lanes == count - 1).astype(F32).astype(BF16)
        out[...] = jnp.concatenate([reverse] * 3, axis=0)
    alpha[...] = a1 * column(eigen[...]) + a2 * eigen[...]

    turn = (
        lax.broadcasted_iota(jnp.int32, (LAYERS, LAYERS), 0)
        + lax.broadcasted_iota(jnp.int32, (LAYERS, LAYERS), 1)
        == LAYERS - 1
    ).astype(F32)
    first = ints[2] == 0
    kv, mv = stiff_v[...], mass_v[...]
    ordered = []
    for matrix in (mv, a3 * kv):
        turned = dot_full(dot_full(turn, matrix), turn)
        ordered.append((jnp.where(first, matrix, turned), jnp.where(first, turned, matrix)))
    deep = lax.broadcasted_iota(jnp.int32, (ROWS, LAYERS), 0)
    wide = lax.broadcasted_iota(jnp.int32, (ROWS, LAYERS), 1)
    inside = (deep < HALF) & (wide < REACH)
    own_stiff = jnp.where(first, kv, dot_full(dot_full(turn, kv), turn))
    vert[0] = jnp.where(inside, ordered[0][0][:ROWS], 0.0)[:, :ROWS]
    vert[1] = jnp.where(inside, own_stiff[:ROWS], 0.0)[:, :ROWS]
    for which in range(2):
        for s in range(2):
            for d in range(BAND + 1):
                picked = jnp.where(deep - wide == d, ordered[s][which][:ROWS], 0.0)
                bands[which, s, d] = jnp.broadcast_to(jnp.sum(picked, axis=1, keepdims=True), (ROWS, N))

    rv = restrict_v[...]
    backwards = dot_full(rv, turn)
    vertical[:, :HALF] = jnp.where(first, rv, backwards)[:, :HALF]
    vertical[:, HALF:] = jnp.where(first, backwards, rv)[:, :HALF]

    mu = eigen_v[...]
    least = jnp.min(mu, axis=1, keepdims=True)
    number = lax.broadcasted_iota(jnp.int32, (1, LAYERS), 1)
    chosen = jnp.min(jnp.where(mu == least, number, LAYERS), axis=1, keepdims=True)
    low = jnp.sum(jnp.where(number == chosen, basis_v[...], 0.0), axis=1, keepdims=True)
    low = jnp.broadcast_to(low, (LAYERS, N))
    low_mass = dot_full(mv, low)
    low_turned, mass_turned = dot_full(turn, low), dot_full(turn, low_mass)
    modes[0] = jnp.where(first, low, low_turned)[:ROWS]
    modes[1] = jnp.where(first, low_mass, mass_turned)[:ROWS]
    modes[2] = jnp.where(first, mass_turned, low_mass)[:ROWS]
    modes[3] = jnp.broadcast_to(a3 * least, (ROWS, N))

    for side in range(2):
        start = ints[4 + side] == 0

        def end_row(matrix, count=N):
            return jnp.where(start, matrix[0:1, :], matrix[count - 1:count, :])

        def corner(matrix):
            value = jnp.where(start, matrix[0:1, 0:1], matrix[N - 1:N, N - 1:N])
            return jnp.broadcast_to(value, (1, N))

        cut_row = end_row(r, COARSE)
        cut_at = jnp.broadcast_to(jnp.where(start, cut_row[:, 0:1], cut_row[:, N - 1:N]), (1, N))
        stiff_profile = jnp.broadcast_to(jnp.sum(r * end_row(k), axis=1, keepdims=True), (N, N))
        mass_profile = jnp.broadcast_to(jnp.sum(r * end_row(m), axis=1, keepdims=True), (N, N))
        at_face = jnp.where(start, 0, COARSE - 1)
        at_rows = [stiff_profile, mass_profile, (rows == at_face).astype(F32)]
        for s in range(3):
            turned_row = jnp.sum(jnp.where(eye, at_rows[s], 0.0), axis=0, keepdims=True)
            profile_rows[3 * side + s:3 * side + s + 1, :] = turned_row
        profile[3 * side] = stiff_profile
        profile[3 * side + 1] = mass_profile
        profile[3 * side + 2] = (rows == at_face).astype(F32)
        spread[side] = column(end_row(b))
        mask[side] = (rows == ints[4 + side]).astype(F32)
        cut[side] = column(cut_row)
        scal[side] = jnp.concatenate(
            [
                corner(k) * a1,
                corner(m) * a2,
                corner(m) * a3,
                jnp.broadcast_to(ints[0].astype(F32), (1, N)),
                end_row(stiff_profile, COARSE) * a1,
                end_row(mass_profile, COARSE) * a2,
                end_row(mass_profile, COARSE) * a3,
                cut_at,
            ],
            axis=0,
        )


def per_device(
    load_vector,
    reaction,
    geometry,
    stiff_plane,
    mass_plane,
    stiff_vertical,
    mass_vertical,
    basis_plane,
    eigen_plane,
    basis_vertical,
    eigen_vertical,
    restrict_plane,
    restrict_vertical,
    patch_links,
):
    patches = lax.axis_size("patch")
    links = patch_links
    square, two = (N, N), (2, N, N)
    right = jax.ShapeDtypeStruct((2 * N, 2 * N), BF16)
    left = jax.ShapeDtypeStruct((N, 2 * N), BF16)
    thrice = jax.ShapeDtypeStruct((3 * N, N), BF16)
    (
        wb, wbt, wrt, lb, lbt, lr, basis_t, restrict_t, mk, mirror, mirror_coarse, vert, scal, spread, mask,
        cut, profile, profile_rows, alpha, bands, modes, vertical,
    ) = call(
        prepare_kernel,
        [
            right, right, right, left, left, left, square, square, (N, 2 * N), thrice, thrice,
            (2, ROWS, ROWS), (2, 8, N), two, two, two, (6, N, N), (8, N), square, (2, 2, BAND + 1, ROWS, N), (4, ROWS, N),
            restrict_vertical.shape,
        ],
        links, stiff_plane, mass_plane, stiff_vertical, mass_vertical, basis_plane, eigen_plane.reshape(1, N),
        basis_vertical, eigen_vertical.reshape(1, LAYERS), restrict_plane, restrict_vertical,
        geometry=geometry, flops=20_000_000,
    )

    pair = [(0, 1), (1, 0), (2, 3), (3, 2)]
    cross = [(0, 2), (2, 0), (1, 3), (3, 1)]
    chips = [[0, 1], [2, 3]]
    faces = []
    for p in range(patches):
        for h in range(2):
            west, east = 4 * p + 2 * h + 1, 4 * ((p + 1) % patches) + 2 * h
            faces += [(west, east), (east, west)]

    def swap_faces(slot_values):
        arrived = lax.ppermute(slot_values, ("patch", "slab"), faces)
        return lambda: lax.all_gather(arrived, "slab", axis_index_groups=chips)

    field = (HALF, N, N)
    own_load = load_vector[0].reshape(BLOCK, N, N)
    own_react = reaction[0].reshape(BLOCK, N, N)
    other_load = lax.ppermute(own_load, "slab", pair)
    size = ROWS + 8
    f, pay, slot_values = call(
        load_kernel, [field, (2, size, N), (size, N)], links, own_load, other_load
    )
    slot_values, own_react = lax.optimization_barrier((slot_values, own_react))
    arriving = swap_faces(slot_values)
    other_react = lax.ppermute(own_react, "slab", pair)
    l, dinv = call(
        factor_kernel, [(HALF, BAND, N, N), field], links, slot_values, alpha, bands, flops=3_000_000_000
    )
    (gh,) = call(transform_kernel, [field], links, f, wb, lbt, flops=2_000_000_000)
    rec = arriving()
    rows_hat = pltpu.VMEM((2, ROWS, N), F32)
    sums = pltpu.VMEM((2, ROWS, 8, N), F32)
    message = (BAND + 1, N // 2, N)
    message_full = (BAND, N, N)
    state_shape = (6, 4, ROWS, N)
    rows_shape = (2, ROWS, N)
    up = total = None
    for sweep in range(SWEEPS):
        if sweep == 0:
            z, msg, low, state, rows_u, rows_g = call(
                first_kernel,
                [field, message, square, state_shape, rows_shape, rows_shape],
                links, gh, pay, rec, scal, spread, wb, mirror, l, modes,
                scratch=[rows_hat], flops=10_000_000,
            )
        else:
            if sweep == 1:
                nscal = rec[:, ROWS + HALF:]
            z, msg, low, state, rows_u, rows_g = call(
                next_kernel,
                [field, message, square, state_shape, rows_shape, rows_shape],
                links, gh, pay, rec, state, scal, nscal, spread, wb, mirror, mk, vert, l, modes,
                scratch=[rows_hat], flops=10_000_000,
            )
        if sweep > 0:
            received = lax.all_gather(msg, "slab")
        else:
            crossing = lax.ppermute(msg, "slab", cross)
            r, react_faces = call(reaction_kernel, [field, (2, HALF, N)], links, msg, own_react, other_react)
            lm, dm, lo, do, mend = call(
                meet_kernel,
                [(BAND, BAND, N, N), message_full, (2 * BAND, BAND, N, N), message_full, square],
                links, alpha, bands, modes, l, dinv,
                scratch=[pltpu.VMEM((TOP, FACTOR_ROWS, N), F32)], flops=5_000_000_000,
            )
            received = lax.all_gather(crossing, "slab", axis_index_groups=chips)
        last = sweep == SWEEPS - 1
        size = ROWS + HALF + 8 if sweep == 0 else ROWS
        extra = [react_faces, scal] if sweep == 0 else []
        y, pay, *slot_values = call(
            solve_kernel,
            [(REACH, N, N), (2, size, N)] + ([] if last else [(size, N)]),
            links, z, low, received, l, dinv, lm, dm, lo, do, mend, modes, spread, basis_t, state, *extra,
            scratch=[sums], flops=10_000_000,
        )
        args = [y, f, r, rows_u, rows_g, mask, wbt, lb]
        if sweep > 0:
            args += [up, total]
        plane_kernel = make_plane_kernel(sweep)
        if last:
            size = ROWS + HALF
            block = (HALF, 32, N)
            up, final, pay, slot_values = call(
                plane_kernel,
                [(BLOCK, N, N), field, (2, size, N), (size, N)],
                links, *args, cut, pay,
                scratch=[pltpu.VMEM((2, HALF, 8, N), F32)], flops=3_000_000_000,
            )
            arriving = swap_faces(slot_values)
            kept, sent = call(
                restrict_kernel, [block, block], links, final, wrt, lr,
                scratch=[pltpu.VMEM((GROUP, N, N), F32)], flops=3_000_000_000,
            )
            arrived = lax.ppermute(sent, "slab", cross)
            rec = arriving()
        else:
            arriving = swap_faces(slot_values[0])
            up, total, gh = call(
                plane_kernel, [field, field, field], links, *args, wb, lbt, flops=4_000_000_000
            )
            rec = arriving()
    parts, rows_u = call(
        final_kernel,
        [(6, HALF, N), rows_shape],
        links, pay, rec, state, scal, nscal, mirror, mirror_coarse, mk, vert, restrict_t,
        geometry=geometry, flops=80_000_000_000,
    )
    far_parts = lax.ppermute(parts, "slab", cross)
    (out_u,) = call(iterate_kernel, [(BLOCK, N, N)], links, up, rows_u, mask, flops=4_000_000_000)
    deep = restrict_vertical.shape[0]
    share = COARSE * COARSE // 4
    (blocks,) = call(
        vertical_kernel, [(32, deep, N)],
        links, kept.reshape(HALF * 32, N), arrived.reshape(HALF * 32, N), vertical, flops=1000, moved=1000,
    )
    (flat,) = call(
        coarse_kernel,
        [(deep, 1, share)],
        links, blocks, parts, far_parts, profile, profile_rows, vertical,
        scratch=[pltpu.VMEM((32, deep, N), F32), pltpu.VMEM((6, deep, N), F32)],
        flops=20_000_000_000,
    )
    return out_u.reshape(1, BLOCK, N * N), flat.transpose(1, 0, 2)


def solution(mesh):
    in_specs = (
        P("patch", "slab", None),
        P("patch", "slab", None),
        P("patch", None),
        P(), P(), P(), P(), P(), P(), P(), P(), P(), P(),
        P("patch", None),
    )
    out_specs = (P("patch", "slab", None), P("patch", None, "slab"))
    return jax.shard_map(
        per_device, mesh=mesh, in_specs=in_specs, out_specs=out_specs, check_vma=False
    )
```

```python
import jax
import jax.numpy as jnp
from jax import lax
from jax.experimental import pallas as pl
from jax.experimental.pallas import tpu as pltpu
from jax.sharding import PartitionSpec as P

BAND = 4
SWEEPS = 3
DAMPING = 0.25
KEEP = 1.0 - DAMPING
HIGHEST = lax.Precision.HIGHEST
F32 = jnp.float32
BF16 = jnp.bfloat16

N = 128
LAYERS = 64
HALF = 32
BLOCK = 16
REACH = HALF + BAND
ROWS = 40
TOP = HALF - BAND
CHUNK = 32
COARSE = N - 2


def split(x):
    high = x.astype(BF16)
    return high, (x - high.astype(F32)).astype(BF16)


def right_mul(x, packed):
    high, low = split(x)
    both = jnp.dot(jnp.concatenate([high, low], axis=-1), packed, preferred_element_type=F32)
    return both[:, :N] + both[:, N:]


def left_mul_planes(packed, planes):
    out = []
    for q in range(0, len(planes), 2):
        high, low = split(jnp.concatenate(planes[q:q + 2], axis=1))
        wide = jnp.dot(packed, jnp.concatenate([high, high], axis=0), preferred_element_type=F32)
        wide = wide + jnp.dot(packed[:, :N], low, preferred_element_type=F32)
        out += [wide[:, :N], wide[:, N:]]
    return out


def dot_full(x, y):
    return jnp.dot(x, y, precision=HIGHEST, preferred_element_type=F32)


def three_products(x, y):
    (xh, xl), (yh, yl) = split(x), split(y)
    out = jnp.dot(xh, yl, preferred_element_type=F32) + jnp.dot(xl, yh, preferred_element_type=F32)
    return out + jnp.dot(xh, yh, preferred_element_type=F32)


def mirrored(x, mirror):
    high, rest = split(x)
    middle, low = split(x - high.astype(F32))
    return jnp.dot(
        jnp.concatenate([high, middle, low], axis=-1), mirror, preferred_element_type=F32
    )


def pack_right(a):
    high, low = split(a)
    top = jnp.concatenate([high, low], axis=1)
    bottom = jnp.concatenate([high, jnp.zeros_like(low)], axis=1)
    return jnp.concatenate([top, bottom], axis=0)


def pack_left(a):
    return jnp.concatenate(split(a), axis=1)


def call(kernel, outs, links, *args, flops=0, scratch=(), geometry=None, moved=None):
    smem = [links] if geometry is None else [links, geometry]
    specs = [pl.BlockSpec(memory_space=pltpu.SMEM)] * len(smem)
    specs += [pl.BlockSpec(memory_space=pltpu.VMEM)] * len(args)
    shapes = [s if isinstance(s, jax.ShapeDtypeStruct) else jax.ShapeDtypeStruct(s, F32) for s in outs]
    if moved is None:
        moved = sum(a.size * a.dtype.itemsize for a in args) + sum(4 * s.size for s in shapes)

    def body(links_ref, *refs):
        ints = facts(links_ref)
        if geometry is None:
            kernel(ints, *refs)
        else:
            kernel(ints, scales(ints, refs[0]), *refs[1:])

    return pl.pallas_call(
        body,
        out_shape=shapes,
        in_specs=specs,
        out_specs=[pl.BlockSpec(memory_space=pltpu.VMEM)] * len(outs),
        scratch_shapes=list(scratch),
        compiler_params=pltpu.CompilerParams(vmem_limit_bytes=16 * 1024 * 1024),
        cost_estimate=pl.CostEstimate(
            flops=flops, bytes_accessed=moved, transcendentals=0
        ),
    )(*smem, *args)


def facts(links):
    slab = lax.axis_index("slab")
    west, east = links[0, 0], links[0, 1]
    return (
        links[0, 2], jnp.right_shift(west, 1), jnp.right_shift(slab, 1), jnp.bitwise_and(slab, 1),
        (N - 1) * jnp.bitwise_and(west, 1), (N - 1) * jnp.bitwise_and(east, 1),
    )


def scales(ints, geometry):
    turned = ints[1] == 1
    first, second = geometry[0, 0], geometry[0, 1]
    return (
        jnp.where(turned, second, first), jnp.where(turned, first, second), geometry[0, 2], jnp.float32(0),
    )


def source_layer(ints, t):
    inside = jnp.where(ints[2] == 1, HALF - 1 - t, t)
    return jnp.right_shift(inside, 4), jnp.bitwise_and(inside, BLOCK - 1)


def load_layers(ints, own_ref, other_ref, out_ref):
    def run(turn):
        def body(g, carry):
            for q in range(8):
                t = g * 8 + q
                block, index = source_layer(ints, t)
                value = jnp.where(block == ints[3], own_ref[index], other_ref[index])
                out_ref[t] = value.T if turn else value
            return carry

        lax.fori_loop(0, HALF // 8, body, 0)

    @pl.when(ints[1] == 0)
    def _():
        run(False)

    @pl.when(ints[1] == 1)
    def _():
        run(True)


def slot(ints, west, east, slot_ref):
    slot_ref[...] = jnp.where(ints[3] == 0, west, east)


def face_rows(ints, ref, side):
    position = ints[4 + side]
    return jnp.where(position == 0, ref[:, 0, :], ref[:, N - 1, :])


def load_kernel(ints, own, other, f_ref, pay_ref, slot_ref):
    load_layers(ints, own, other, f_ref)
    flag = jnp.broadcast_to(ints[0].astype(F32), (8, N))
    for side in range(2):
        rows = face_rows(ints, f_ref, side)
        pay_ref[side] = jnp.concatenate([rows, jnp.zeros((ROWS - HALF, N), F32), flag], axis=0)
    slot(ints, pay_ref[0], pay_ref[1], slot_ref)


def reaction_kernel(ints, ready, own, other, r_ref, face_ref):
    load_layers(ints, own, other, r_ref)
    for side in range(2):
        face_ref[side] = face_rows(ints, r_ref, side)


def forward_planes(x, wb, lbt):
    count = x.shape[0]
    first = right_mul(x.reshape(count * N, N), wb).reshape(count, N, N)
    return left_mul_planes(lbt, [first[q] for q in range(count)])


GROUP = 32


def transform_kernel(ints, f_ref, wb, lbt, out_ref):
    def body(g, carry):
        t = g * GROUP
        planes = forward_planes(f_ref[pl.ds(t, GROUP)], wb[...], lbt[...])
        for q in range(GROUP):
            out_ref[t + q] = planes[q]
        return carry

    lax.fori_loop(0, HALF // GROUP, body, 0)


FACTOR_ROWS = 16


def coefficient(bands, alpha, which, t, d):
    return alpha * bands[which, 0, d, t:t + 1, :] + bands[which, 1, d, t:t + 1, :]


def row_weights(a, l, t, least):
    w = {}
    for d in range(min(BAND, t), least - 1, -1):
        v = a[d]
        for m in range(d + 1, min(BAND, t) + 1):
            v = v - w[m] * l[t - d][m - d]
        w[d] = v
    return w


def eliminate(a, l, dinv, t):
    w = row_weights(a, l, t, 1)
    row = {d: w[d] * dinv[t - d] for d in w}
    pivot = a[0]
    for d in w:
        pivot = pivot - w[d] * row[d]
    return row, 1.0 / pivot


def factor_kernel(ints, ready, alpha_ref, bands, l_ref, dinv_ref):
    def body(c, carry):
        part = pl.ds(c * FACTOR_ROWS, FACTOR_ROWS)
        alpha = alpha_ref[part, :]
        l, dinv = {}, {}
        for t in range(HALF):
            a = [coefficient(bands, alpha, 0, t, d) for d in range(min(BAND, t) + 1)]
            l[t], dinv[t] = eliminate(a, l, dinv, t)
            for d in l[t]:
                l_ref[t, d - 1, part, :] = l[t][d]
            dinv_ref[t, part, :] = dinv[t]
        return carry

    lax.fori_loop(0, N // FACTOR_ROWS, body, 0)


def meet_kernel(
    ints, alpha_ref, bands, modes, l_ref, dinv_ref, lm_ref, dm_ref, lo_ref, do_ref, mend_ref, zs
):
    def mode(which, t):
        return modes[which, t:t + 1, :]

    def body(c, carry):
        part = pl.ds(c * FACTOR_ROWS, FACTOR_ROWS)
        alpha = alpha_ref[part, :]
        l, dinv, sent = {}, {}, {}
        for t in range(HALF):
            a = [coefficient(bands, alpha, 1, t, d) for d in range(min(BAND, t) + 1)]
            l[t], dinv[t] = eliminate(a, l, dinv, t)
            sent[t] = jnp.broadcast_to(mode(2, t), alpha.shape)
            for d in l[t]:
                sent[t] = sent[t] - l[t][d] * sent[t - d]
            if t >= TOP:
                for d in range(1, BAND + 1):
                    lo_ref[t - TOP, d - 1, part, :] = l[t][d]
                do_ref[t - TOP, part, :] = dinv[t]
        outer = {}
        for j in range(BAND):
            t = HALF + j
            a = [coefficient(bands, alpha, 1, t, d) for d in range(BAND + 1)]
            outer[j] = row_weights(a, l, t, j + 1)
            l[t] = {d: outer[j][d] * dinv[t - d] for d in outer[j]}
            for d in l[t]:
                lo_ref[BAND + j, d - 1, part, :] = l[t][d]
        schur = {}
        for j in range(BAND):
            for i in range(j + 1):
                total = None
                for s in range(TOP + j, HALF):
                    term = outer[j][HALF + j - s] * l[HALF + i][HALF + i - s]
                    total = term if total is None else total + term
                schur[(j, i)] = schur[(i, j)] = total
        shift = {}
        for j in range(BAND):
            for d in range(j + 1, BAND + 1):
                term = l[HALF + j][d] * sent[HALF + j - d]
                shift[j] = term if j not in shift else shift[j] + term
        z = {}
        for t in range(TOP):
            z[t] = jnp.broadcast_to(mode(1, t), alpha.shape)
            for d in range(1, min(BAND, t) + 1):
                z[t] = z[t] - l_ref[t, d - 1, part, :] * z[t - d]
            zs[t] = z[t]
        l = {
            t: {d: l_ref[t, d - 1, part, :] for d in range(1, BAND + 1)} for t in range(TOP - BAND, TOP)
        }
        dinv = {t: dinv_ref[t, part, :] for t in range(TOP - BAND, TOP)}
        for t in range(TOP, HALF):
            a = [coefficient(bands, alpha, 0, t, d) for d in range(BAND + 1)]
            j = HALF - 1 - t
            for d in range(t - TOP + 1):
                a[d] = a[d] - schur[(j, j + d)]
            l[t], dinv[t] = eliminate(a, l, dinv, t)
            for d in range(1, BAND + 1):
                lm_ref[t - TOP, d - 1, part, :] = l[t][d]
            dm_ref[t - TOP, part, :] = dinv[t]
            z[t] = mode(1, t) - shift[j]
            for d in range(1, BAND + 1):
                z[t] = z[t] - l[t][d] * z[t - d]
        exact = 1.0 / (alpha + modes[3, 0:1, :])
        y, miss, norm = {}, jnp.zeros_like(alpha), jnp.zeros_like(modes[3, 0:1, :])
        for t in range(HALF - 1, -1, -1):
            y[t] = z[t] * dinv[t] if t >= TOP else zs[t] * dinv_ref[t, part, :]
            for d in range(1, min(BAND, HALF - 1 - t) + 1):
                factor = l[t + d][d] if t + d >= TOP else l_ref[t + d, d - 1, part, :]
                y[t] = y[t] - factor * y[t + d]
            miss = miss + mode(1, t) * (mode(0, t) * exact - y[t])
            norm = norm + mode(1, t) * mode(0, t)
        mend_ref[part, :] = jnp.where(norm > 0.01, miss / jnp.maximum(norm, 0.01), 0.0)
        return carry

    lax.fori_loop(0, N // FACTOR_ROWS, body, 0)


def four(get):
    return [get(side, who) for side in range(2) for who in range(2)]


def vertical_apply(products, vert, scal_k, scal_m, scal_v):
    mass = [k * p[:, :N] + m * p[:, N:] for p, k, m in zip(products, scal_k, scal_m)]
    stiff = [v * p[:, :N] for p, v in zip(products, scal_v)]
    out = dot_full(vert[0], jnp.concatenate(mass, axis=1))
    out = out + dot_full(vert[1], jnp.concatenate(stiff, axis=1))
    return [out[:, q * N:(q + 1) * N] for q in range(len(products))]


def plane_products(faces, mk):
    stacked = dot_full(jnp.concatenate(faces, axis=0), mk[...])
    return [stacked[q * ROWS:(q + 1) * ROWS] for q in range(len(faces))]


def flip_masks(scal, nscal):
    return [scal[side, 3:4, :] != nscal[side, 3:4, :] for side in range(2)]


def orient_all(arrays, mirror, masks):
    turned = mirrored(jnp.concatenate([a for _, a in arrays], axis=0), mirror[...])
    return [
        jnp.where(masks[side], turned[q * ROWS:(q + 1) * ROWS], a)
        for q, (side, a) in enumerate(arrays)
    ]


def update_faces(c_faces, state, scal, nscal, mirror, mk, vert):
    masks = flip_masks(scal, nscal)
    residual = four(lambda side, who: state[4][2 * side + who])
    arrays = []
    for side in range(2):
        for who in range(2):
            arrays.append((side, c_faces[2 * side + 1 - who]))
    for side in range(2):
        for who in range(2):
            arrays.append((side, residual[2 * side + 1 - who]))
    turned = orient_all(arrays, mirror, masks)
    e, added = turned[:4], turned[4:]
    products = plane_products(e, mk)
    which = four(lambda side, who: (nscal if who else scal)[side])
    applied = vertical_apply(
        products, vert, [w[0:1] for w in which], [w[1:2] for w in which], [w[2:3] for w in which]
    )
    new = [list(state[s]) for s in range(6)]
    for q in range(4):
        new[2][q] = state[2][q] + DAMPING * (c_faces[q] + e[q])
        new[3][q] = state[3][q] + DAMPING * (residual[q] + added[q] + applied[q])
        new[4][q] = state[0][q] - state[1][q] * new[2][q] - new[3][q]
        new[5][q] = KEEP * state[5][q] + DAMPING * e[q]
    return new, e, masks


def read_state(ref):
    return [[ref[s, q] for q in range(4)] for s in range(6)]


def pad_rows(x):
    return jnp.concatenate([x, jnp.zeros((ROWS - x.shape[0], N), F32)], axis=0)


def eliminate_forward(gh_ref, spread, rows_hat, l_ref, modes, z_ref, msg_ref, low_ref, core):
    def body(c, carry):
        part = pl.ds(pl.multiple_of(c * CHUNK, CHUNK), CHUNK)
        west, east = spread[0, part, :], spread[1, part, :]
        z = {}
        lowest = jnp.zeros_like(west)
        for t in range(HALF):
            x = gh_ref[t, part, :] + west * rows_hat[0, t:t + 1, :] + east * rows_hat[1, t:t + 1, :]
            lowest = lowest + modes[0, t:t + 1, :] * x
            z_ref[t, part, :] = x
            for d in range(min(BAND, t), 0, -1):
                x = x - l_ref[t, d - 1, part, :] * z[t - d]
            z[t] = x
            if t < TOP:
                z_ref[t, part, :] = x
        low_ref[part, :] = lowest

        @pl.when(jnp.right_shift(c, 1) == core)
        def _():
            there = pl.ds(pl.multiple_of(jnp.bitwise_and(c, 1) * CHUNK, CHUNK), CHUNK)
            for s in range(BAND):
                msg_ref[s, there, :] = z[TOP + s]
            msg_ref[BAND, there, :] = lowest

        return carry

    lax.fori_loop(0, N // CHUNK, body, 0)


def first_kernel(
    ints, gh, own_pay, rec, scal, spread, wb, mirror, l_ref, modes,
    z_ref, msg_ref, low_ref, state_ref, rows_u, rows_g, rows_hat,
):
    received = (rec[0], rec[1])
    masks = [received[side][ROWS:ROWS + 1] != scal[side, 3:4, :] for side in range(2)]
    state_ref[...] = jnp.zeros_like(state_ref)
    for side in range(2):
        for who in range(2):
            values = received[side][:ROWS] if who else own_pay[side, :ROWS]
            state_ref[0, 2 * side + who] = values
            state_ref[4, 2 * side + who] = values
    turned = orient_all([(side, received[side][:ROWS]) for side in range(2)], mirror, masks)
    rows_u[...] = jnp.zeros_like(rows_u)
    for side in range(2):
        rows_g[side] = turned[side]
        rows_hat[side] = right_mul(turned[side], wb[...])
    eliminate_forward(gh, spread, rows_hat, l_ref, modes, z_ref, msg_ref, low_ref, ints[3])


def next_kernel(
    ints, gh, own_pay, rec, state_in, scal, nscal, spread, wb, mirror, mk, vert,
    l_ref, modes, z_ref, msg_ref, low_ref, state_ref, rows_u, rows_g, rows_hat,
):
    received = (rec[0], rec[1])
    state = read_state(state_in)
    if own_pay.shape[1] > ROWS:
        for side in range(2):
            state[1][2 * side] = pad_rows(own_pay[side, ROWS:ROWS + HALF])
            state[1][2 * side + 1] = pad_rows(received[side][ROWS:ROWS + HALF])
    c_faces = four(lambda side, who: received[side][:ROWS] if who else own_pay[side, :ROWS])
    state, e, masks = update_faces(c_faces, state, scal, nscal, mirror, mk, vert)
    for s in range(6):
        for q in range(4):
            state_ref[s, q] = state[s][q]
    turned = orient_all([(side, state[4][2 * side + 1]) for side in range(2)], mirror, masks)
    for side in range(2):
        step = DAMPING * e[2 * side]
        rows = turned[side] - state[1][2 * side] * step
        rows_u[side] = step
        rows_g[side] = rows
        rows_hat[side] = right_mul(rows, wb[...])
    eliminate_forward(gh, spread, rows_hat, l_ref, modes, z_ref, msg_ref, low_ref, ints[3])


def solve_kernel(
    ints, z_ref, low_ref, zr_ref, l_ref, dinv_ref, lm_ref, dm_ref, lo_ref, do_ref, mend, modes, spread, bt_full, state, *refs,
):
    sums = refs[-1]
    extra = refs[:2] if len(refs) > 4 else ()
    outs = refs[len(extra):-1]
    y_ref, pay_ref = outs[:2]
    sums[...] = jnp.zeros_like(sums)

    def body(c, carry):
        part = pl.ds(pl.multiple_of(c * CHUNK, CHUNK), CHUNK)
        source = jnp.right_shift(c, 1)
        if zr_ref.shape[0] > 2:
            source = source + 2 * (1 - ints[2])
        there = pl.ds(pl.multiple_of(jnp.bitwise_and(c, 1) * CHUNK, CHUNK), CHUNK)
        sent = [zr_ref[source, s, there, :] for s in range(BAND)]
        weights = (spread[0, part, :], spread[1, part, :])

        low = mend[part, :] * (low_ref[part, :] + zr_ref[source, BAND, there, :])

        def put(t, value):
            value = value + low * modes[0, t:t + 1, :]
            y_ref[t, part, :] = value
            for side in range(2):
                product = weights[side] * value
                total = product[0:8]
                for s in range(8, CHUNK, 8):
                    total = total + product[s:s + 8]
                sums[side, t] += total

        z = {t: z_ref[t, part, :] for t in range(TOP - BAND, HALF)}
        for j in range(BAND):
            for d in range(j + 1, BAND + 1):
                z[HALF - 1 - j] = z[HALF - 1 - j] - lo_ref[BAND + j, d - 1, part, :] * sent[BAND + j - d]
        for t in range(TOP, HALF):
            for d in range(BAND, 0, -1):
                z[t] = z[t] - lm_ref[t - TOP, d - 1, part, :] * z[t - d]

        def factor(t, d):
            return lm_ref[t - TOP, d - 1, part, :] if t >= TOP else l_ref[t, d - 1, part, :]

        y = {}
        for t in range(HALF - 1, TOP - 1, -1):
            value = z[t] * dm_ref[t - TOP, part, :]
            for d in range(HALF - 1 - t, 0, -1):
                value = value - factor(t + d, d) * y[t + d]
            y[t] = value
            put(t, value)
        far = {HALF + j: y[HALF - 1 - j] for j in range(BAND)}
        for t in range(HALF - 1, TOP - 1, -1):
            value = sent[t - TOP] * do_ref[t - TOP, part, :]
            for d in range(BAND, 0, -1):
                value = value - lo_ref[t + d - TOP, d - 1, part, :] * far[t + d]
            far[t] = value
            put(2 * HALF - 1 - t, value)
        for t in range(TOP - 1, -1, -1):
            known = z[t] if t in z else z_ref[t, part, :]
            value = known * dinv_ref[t, part, :]
            for d in range(BAND, 0, -1):
                value = value - factor(t + d, d) * y[t + d]
            y[t] = value
            put(t, value)
        return carry

    lax.fori_loop(0, N // CHUNK, body, 0)
    mixed = jnp.sum(sums[...], axis=2)
    faces = dot_full(mixed.reshape(2 * ROWS, N), bt_full[...])
    packs = []
    for side in range(2):
        c = faces[side * ROWS:(side + 1) * ROWS] - state[2, 2 * side]
        pay_ref[side, :ROWS] = c
        if extra:
            pay_ref[side, ROWS:ROWS + HALF] = extra[0][side]
            pay_ref[side, ROWS + HALF:] = extra[1][side]
    for slot_ref in outs[2:]:
        slot(ints, pay_ref[0], pay_ref[1], slot_ref)


def back_planes(y, wbt, lb):
    count = y.shape[0]
    across = right_mul(y.reshape(count * N, N), wbt).reshape(count, N, N)
    return left_mul_planes(lb, [across[q] for q in range(count)])


def make_plane_kernel(sweep):
    last = sweep == SWEEPS - 1

    def kernel(ints, *refs):
        refs = list(refs)
        y_ref, f_ref, r_ref, rows_u, rows_g, mask, wbt, lb = refs[:8]
        refs = refs[8:]
        if sweep > 0:
            up_in, g_in = refs[:2]
            refs = refs[2:]
        if last:
            cut, pay_in = refs[:2]
            up_out, final_out, pay_out, slot_ref, sums = refs[2:]
        else:
            wb, lbt = refs[:2]
            up_out, g_out, gh_out = refs[2:]

        def on_faces(rows, t):
            return mask[0] * rows[0, pl.ds(t, 1), :] + mask[1] * rows[1, pl.ds(t, 1), :]

        def body(g, carry):
            t0 = g * GROUP
            corrections = back_planes(y_ref[pl.ds(t0, GROUP)], wbt[...], lb[...])
            fresh = []
            for q in range(GROUP):
                t = t0 + q
                on_u, on_g = on_faces(rows_u, t), on_faces(rows_g, t)
                load, react = f_ref[t], r_ref[t]
                if sweep == 0:
                    u, total = on_u, DAMPING * (load + on_g)
                else:
                    old = up_in[t]
                    u = old + on_u
                    total = KEEP * g_in[t] + DAMPING * (load - react * old + on_g)
                new = KEEP * u + DAMPING * corrections[q]
                if last:
                    block, index = source_layer(ints, t)

                    @pl.when(block == ints[3])
                    def _():
                        up_out[index] = new
                else:
                    up_out[t] = new
                residual = load - react * new
                if last:
                    residual = residual - total
                    for side in range(2):
                        product = cut[side] * residual
                        part = product[0:8]
                        for s in range(8, N, 8):
                            part = part + product[s:s + 8]
                        sums[side, t] = part
                else:
                    g_out[t] = total
                if last:
                    final_out[t] = residual
                fresh.append(residual)
            if not last:
                stacked = jnp.concatenate(fresh, axis=0).reshape(GROUP, N, N)
                planes = forward_planes(stacked, wb[...], lbt[...])
                for q in range(GROUP):
                    gh_out[t0 + q] = planes[q]
            return carry

        lax.fori_loop(0, HALF // GROUP, body, 0)
        if last:
            for side in range(2):
                pay_out[side, :ROWS] = pay_in[side, :ROWS]
                pay_out[side, ROWS:] = jnp.sum(sums[side], axis=1)
            slot(ints, pay_out[0], pay_out[1], slot_ref)

    return kernel


def restrict_kernel(ints, final, wrt, lr, kept, sent, plane):
    def body(g, carry):
        t0 = g * GROUP
        planes = forward_planes(final[pl.ds(t0, GROUP)], wrt[...], lr[...])
        for q in range(GROUP):
            plane[q] = planes[q]

        @pl.when(ints[1] == 1)
        def _():
            for q in range(GROUP):
                plane[q] = planes[q].T

        for half in range(2):
            for core in range(2):
                first = half * (COARSE // 2) + core * 31

                @pl.when((ints[2] == half) & (ints[3] == core))
                def _():
                    kept[pl.ds(t0, GROUP)] = plane[:, first:first + 32]

                @pl.when((ints[2] != half) & (ints[3] == core))
                def _():
                    sent[pl.ds(t0, GROUP)] = plane[:, first:first + 32]

        return carry

    lax.fori_loop(0, HALF // GROUP, body, 0)


def final_kernel(
    ints, floats, own_pay, rec, state_in, scal, nscal, mirror, mirror_coarse, mk, vert, rt_full, parts, rows_u,
):
    received = (rec[0], rec[1])
    state = read_state(state_in)
    c_faces = four(lambda side, who: received[side][:ROWS] if who else own_pay[side, :ROWS])
    state, e, masks = update_faces(c_faces, state, scal, nscal, mirror, mk, vert)
    gathered = state[5]
    products = plane_products(gathered, mk)
    far = vertical_apply(
        [products[1], products[3]], vert,
        [nscal[side, 4:5] for side in range(2)],
        [nscal[side, 5:6] for side in range(2)],
        [nscal[side, 6:7] for side in range(2)],
    )
    one = floats[0]
    near_stiff = vertical_apply([products[0], products[2]], vert, [one] * 2, [floats[3]] * 2, [floats[3]] * 2)
    near_mass = vertical_apply([products[0], products[2]], vert, [floats[3]] * 2, [floats[1]] * 2, [floats[2]] * 2)
    stack = []
    for side in range(2):
        nbr = 2 * side + 1
        theirs = pad_rows(received[side][ROWS:])
        theirs = theirs - nscal[side, 7:8] * DAMPING * state[1][nbr] * e[nbr] - far[side]
        mine = scal[side, 7:8] * DAMPING * state[1][2 * side] * e[2 * side]
        stack += [near_stiff[side], near_mass[side], mine, theirs]
    restricted = dot_full(jnp.concatenate(stack, axis=0), rt_full[...])
    pieces = [restricted[q * ROWS:(q + 1) * ROWS] for q in range(8)]
    turned = mirrored(jnp.concatenate([pieces[3], pieces[7]], axis=0), mirror_coarse[...])
    for side in range(2):
        added = jnp.where(masks[side], turned[side * ROWS:(side + 1) * ROWS], pieces[4 * side + 3])
        parts[3 * side] = -pieces[4 * side][:HALF]
        parts[3 * side + 1] = -pieces[4 * side + 1][:HALF]
        parts[3 * side + 2] = (added - pieces[4 * side + 2])[:HALF]
        rows_u[side] = DAMPING * e[2 * side]

def iterate_kernel(ints, up, rows_u, mask, out_u):
    def body(index, carry):
        inside = ints[3] * BLOCK + index
        t = jnp.where(ints[2] == 1, HALF - 1 - inside, inside)
        value = up[index] + mask[0] * rows_u[0, pl.ds(t, 1), :] + mask[1] * rows_u[1, pl.ds(t, 1), :]
        out_u[index] = value

        @pl.when(ints[1] == 1)
        def _():
            out_u[index] = value.T

        return carry

    lax.fori_loop(0, BLOCK, body, 0, unroll=2)


def vertical_kernel(ints, kept, arrived, vertical, blocks):
    for c in range(32):
        rows = pl.ds(c, HALF, stride=32)
        both = jnp.concatenate([kept[rows, :], arrived[rows, :]], axis=0)
        blocks[c] = three_products(vertical[...], both)


def coarse_kernel(ints, start_blocks, parts, far_parts, profile, profile_rows, vertical, out, blocks, columns):
    deep = vertical.shape[0]
    spots = [0, 31, COARSE // 2, COARSE // 2 + 31]
    stacked = [jnp.concatenate([parts[s], far_parts[s]], axis=0) for s in range(6)]
    mixed = three_products(vertical[...], jnp.concatenate(stacked, axis=1))
    mixed = [mixed[:, s * N:(s + 1) * N] for s in range(6)]

    @pl.when(ints[1] == 0)
    def _():
        first = ints[2] * (COARSE // 2) + ints[3] * 31

        for c in range(32):
            value = start_blocks[c]
            for s in range(6):
                value = value + profile[s, pl.ds(first + c, 1), :] * mixed[s]
            blocks[c] = value

    @pl.when(ints[1] == 1)
    def _():
        for half in range(2):
            for core in range(2):
                shift = (N - spots[2 * half + core]) % N

                @pl.when((ints[2] == half) & (ints[3] == core))
                def _():
                    for s in range(6):
                        columns[s] = pltpu.roll(mixed[s], shift, 1) if shift else mixed[s]

        for c in range(32):
            value = start_blocks[c]
            for s in range(6):
                value = value + columns[s, :, c:c + 1] * profile_rows[s:s + 1, :]
            blocks[c] = value

    share = out.shape[2]
    lane = lax.broadcasted_iota(jnp.int32, (deep, N), 1)
    for core in range(2):

        @pl.when(ints[3] == core)
        def _():
            start = core * (COARSE // 2)
            held = {}

            def turned(c):
                if c not in held:
                    shift = (c * COARSE - start) % N
                    held[c] = pltpu.roll(blocks[c], shift, 1) if shift else blocks[c]
                return held[c]

            for tile in range(-(-share // N)):
                low = tile * N + start
                c = low // COARSE
                value = turned(c)
                after = (c + 1) * COARSE - low
                if after < N and c + 1 < 32:
                    value = jnp.where(lane < after, value, turned(c + 1))
                if after + COARSE < N and c + 2 < 32:
                    value = jnp.where(lane < after + COARSE, value, turned(c + 2))
                width = min(N, share - tile * N)
                out[:, 0, tile * N:tile * N + width] = value[:, :width]


def prepare_kernel(
    ints, floats, stiff, mass, stiff_v, mass_v, basis, eigen, basis_v, eigen_v, restrict, restrict_v,
    wb, wbt, wrt, lb, lbt, lr, bt_out, rt_out, mk, mirror, mirror_coarse, vert, scal, spread, mask, cut,
    profile, profile_rows, alpha, bands, modes, vertical,
):
    a1, a2, a3 = floats[0], floats[1], floats[2]
    rows = lax.broadcasted_iota(jnp.int32, (N, N), 0)
    lanes = lax.broadcasted_iota(jnp.int32, (N, N), 1)
    eye = rows == lanes

    def column(row):
        picked = jnp.sum(jnp.where(eye, row, 0.0), axis=1, keepdims=True)
        return jnp.broadcast_to(picked, (N, N))

    b, k, m = basis[...], stiff[...], mass[...]
    bt = b.T
    r = jnp.concatenate([restrict[...], jnp.zeros((N - COARSE, N), F32)], axis=0)
    rt = r.T
    wb[...], wbt[...], wrt[...] = pack_right(b), pack_right(bt), pack_right(rt)
    lb[...], lbt[...], lr[...] = pack_left(b), pack_left(bt), pack_left(r)
    bt_out[...], rt_out[...] = bt, rt
    mk[:, :N], mk[:, N:] = m, k
    for out, count in ((mirror, N), (mirror_coarse, COARSE)):
        reverse = (rows + lanes == count - 1).astype(F32).astype(BF16)
        out[...] = jnp.concatenate([reverse] * 3, axis=0)
    alpha[...] = a1 * column(eigen[...]) + a2 * eigen[...]

    turn = (
        lax.broadcasted_iota(jnp.int32, (LAYERS, LAYERS), 0)
        + lax.broadcasted_iota(jnp.int32, (LAYERS, LAYERS), 1)
        == LAYERS - 1
    ).astype(F32)
    first = ints[2] == 0
    kv, mv = stiff_v[...], mass_v[...]
    ordered = []
    for matrix in (mv, a3 * kv):
        turned = dot_full(dot_full(turn, matrix), turn)
        ordered.append((jnp.where(first, matrix, turned), jnp.where(first, turned, matrix)))
    deep = lax.broadcasted_iota(jnp.int32, (ROWS, LAYERS), 0)
    wide = lax.broadcasted_iota(jnp.int32, (ROWS, LAYERS), 1)
    inside = (deep < HALF) & (wide < REACH)
    own_stiff = jnp.where(first, kv, dot_full(dot_full(turn, kv), turn))
    vert[0] = jnp.where(inside, ordered[0][0][:ROWS], 0.0)[:, :ROWS]
    vert[1] = jnp.where(inside, own_stiff[:ROWS], 0.0)[:, :ROWS]
    for which in range(2):
        for s in range(2):
            for d in range(BAND + 1):
                picked = jnp.where(deep - wide == d, ordered[s][which][:ROWS], 0.0)
                bands[which, s, d] = jnp.broadcast_to(jnp.sum(picked, axis=1, keepdims=True), (ROWS, N))

    rv = restrict_v[...]
    backwards = dot_full(rv, turn)
    vertical[:, :HALF] = jnp.where(first, rv, backwards)[:, :HALF]
    vertical[:, HALF:] = jnp.where(first, backwards, rv)[:, :HALF]

    mu = eigen_v[...]
    least = jnp.min(mu, axis=1, keepdims=True)
    number = lax.broadcasted_iota(jnp.int32, (1, LAYERS), 1)
    chosen = jnp.min(jnp.where(mu == least, number, LAYERS), axis=1, keepdims=True)
    low = jnp.sum(jnp.where(number == chosen, basis_v[...], 0.0), axis=1, keepdims=True)
    low = jnp.broadcast_to(low, (LAYERS, N))
    low_mass = dot_full(mv, low)
    low_turned, mass_turned = dot_full(turn, low), dot_full(turn, low_mass)
    modes[0] = jnp.where(first, low, low_turned)[:ROWS]
    modes[1] = jnp.where(first, low_mass, mass_turned)[:ROWS]
    modes[2] = jnp.where(first, mass_turned, low_mass)[:ROWS]
    modes[3] = jnp.broadcast_to(a3 * least, (ROWS, N))

    for side in range(2):
        start = ints[4 + side] == 0

        def end_row(matrix, count=N):
            return jnp.where(start, matrix[0:1, :], matrix[count - 1:count, :])

        def corner(matrix):
            value = jnp.where(start, matrix[0:1, 0:1], matrix[N - 1:N, N - 1:N])
            return jnp.broadcast_to(value, (1, N))

        cut_row = end_row(r, COARSE)
        cut_at = jnp.broadcast_to(jnp.where(start, cut_row[:, 0:1], cut_row[:, N - 1:N]), (1, N))
        stiff_profile = jnp.broadcast_to(jnp.sum(r * end_row(k), axis=1, keepdims=True), (N, N))
        mass_profile = jnp.broadcast_to(jnp.sum(r * end_row(m), axis=1, keepdims=True), (N, N))
        at_face = jnp.where(start, 0, COARSE - 1)
        at_rows = [stiff_profile, mass_profile, (rows == at_face).astype(F32)]
        for s in range(3):
            turned_row = jnp.sum(jnp.where(eye, at_rows[s], 0.0), axis=0, keepdims=True)
            profile_rows[3 * side + s:3 * side + s + 1, :] = turned_row
        profile[3 * side] = stiff_profile
        profile[3 * side + 1] = mass_profile
        profile[3 * side + 2] = (rows == at_face).astype(F32)
        spread[side] = column(end_row(b))
        mask[side] = (rows == ints[4 + side]).astype(F32)
        cut[side] = column(cut_row)
        scal[side] = jnp.concatenate(
            [
                corner(k) * a1,
                corner(m) * a2,
                corner(m) * a3,
                jnp.broadcast_to(ints[0].astype(F32), (1, N)),
                end_row(stiff_profile, COARSE) * a1,
                end_row(mass_profile, COARSE) * a2,
                end_row(mass_profile, COARSE) * a3,
                cut_at,
            ],
            axis=0,
        )


def per_device(
    load_vector,
    reaction,
    geometry,
    stiff_plane,
    mass_plane,
    stiff_vertical,
    mass_vertical,
    basis_plane,
    eigen_plane,
    basis_vertical,
    eigen_vertical,
    restrict_plane,
    restrict_vertical,
    patch_links,
):
    patches = lax.axis_size("patch")
    links = patch_links
    square, two = (N, N), (2, N, N)
    right = jax.ShapeDtypeStruct((2 * N, 2 * N), BF16)
    left = jax.ShapeDtypeStruct((N, 2 * N), BF16)
    thrice = jax.ShapeDtypeStruct((3 * N, N), BF16)
    (
        wb, wbt, wrt, lb, lbt, lr, basis_t, restrict_t, mk, mirror, mirror_coarse, vert, scal, spread, mask,
        cut, profile, profile_rows, alpha, bands, modes, vertical,
    ) = call(
        prepare_kernel,
        [
            right, right, right, left, left, left, square, square, (N, 2 * N), thrice, thrice,
            (2, ROWS, ROWS), (2, 8, N), two, two, two, (6, N, N), (8, N), square, (2, 2, BAND + 1, ROWS, N), (4, ROWS, N),
            restrict_vertical.shape,
        ],
        links, stiff_plane, mass_plane, stiff_vertical, mass_vertical, basis_plane, eigen_plane.reshape(1, N),
        basis_vertical, eigen_vertical.reshape(1, LAYERS), restrict_plane, restrict_vertical,
        geometry=geometry, flops=20_000_000,
    )

    pair = [(0, 1), (1, 0), (2, 3), (3, 2)]
    cross = [(0, 2), (2, 0), (1, 3), (3, 1)]
    chips = [[0, 1], [2, 3]]
    faces = []
    for p in range(patches):
        for h in range(2):
            west, east = 4 * p + 2 * h + 1, 4 * ((p + 1) % patches) + 2 * h
            faces += [(west, east), (east, west)]

    def swap_faces(slot_values):
        arrived = lax.ppermute(slot_values, ("patch", "slab"), faces)
        return lambda: lax.all_gather(arrived, "slab", axis_index_groups=chips)

    field = (HALF, N, N)
    own_load = load_vector[0].reshape(BLOCK, N, N)
    own_react = reaction[0].reshape(BLOCK, N, N)
    other_load = lax.ppermute(own_load, "slab", pair)
    other_react = lax.ppermute(own_react, "slab", pair)
    size = ROWS + 8
    f, pay, slot_values = call(
        load_kernel, [field, (2, size, N), (size, N)], links, own_load, other_load
    )
    arriving = swap_faces(slot_values)
    l, dinv = call(
        factor_kernel, [(HALF, BAND, N, N), field], links, slot_values, alpha, bands, flops=3_000_000_000
    )
    (gh,) = call(transform_kernel, [field], links, f, wb, lbt, flops=2_000_000_000)
    rec = arriving()
    rows_hat = pltpu.VMEM((2, ROWS, N), F32)
    sums = pltpu.VMEM((2, ROWS, 8, N), F32)
    message = (BAND + 1, N // 2, N)
    message_full = (BAND, N, N)
    state_shape = (6, 4, ROWS, N)
    rows_shape = (2, ROWS, N)
    up = total = None
    for sweep in range(SWEEPS):
        if sweep == 0:
            z, msg, low, state, rows_u, rows_g = call(
                first_kernel,
                [field, message, square, state_shape, rows_shape, rows_shape],
                links, gh, pay, rec, scal, spread, wb, mirror, l, modes,
                scratch=[rows_hat], flops=10_000_000,
            )
        else:
            if sweep == 1:
                nscal = rec[:, ROWS + HALF:]
            z, msg, low, state, rows_u, rows_g = call(
                next_kernel,
                [field, message, square, state_shape, rows_shape, rows_shape],
                links, gh, pay, rec, state, scal, nscal, spread, wb, mirror, mk, vert, l, modes,
                scratch=[rows_hat], flops=10_000_000,
            )
        if sweep > 0:
            received = lax.all_gather(msg, "slab")
        else:
            crossing = lax.ppermute(msg, "slab", cross)
            r, react_faces = call(reaction_kernel, [field, (2, HALF, N)], links, msg, own_react, other_react)
            lm, dm, lo, do, mend = call(
                meet_kernel,
                [(BAND, BAND, N, N), message_full, (2 * BAND, BAND, N, N), message_full, square],
                links, alpha, bands, modes, l, dinv,
                scratch=[pltpu.VMEM((TOP, FACTOR_ROWS, N), F32)], flops=5_000_000_000,
            )
            received = lax.all_gather(crossing, "slab", axis_index_groups=chips)
        last = sweep == SWEEPS - 1
        size = ROWS + HALF + 8 if sweep == 0 else ROWS
        extra = [react_faces, scal] if sweep == 0 else []
        y, pay, *slot_values = call(
            solve_kernel,
            [(REACH, N, N), (2, size, N)] + ([] if last else [(size, N)]),
            links, z, low, received, l, dinv, lm, dm, lo, do, mend, modes, spread, basis_t, state, *extra,
            scratch=[sums], flops=10_000_000,
        )
        args = [y, f, r, rows_u, rows_g, mask, wbt, lb]
        if sweep > 0:
            args += [up, total]
        plane_kernel = make_plane_kernel(sweep)
        if last:
            size = ROWS + HALF
            block = (HALF, 32, N)
            up, final, pay, slot_values = call(
                plane_kernel,
                [(BLOCK, N, N), field, (2, size, N), (size, N)],
                links, *args, cut, pay,
                scratch=[pltpu.VMEM((2, HALF, 8, N), F32)], flops=3_000_000_000,
            )
            arriving = swap_faces(slot_values)
            kept, sent = call(
                restrict_kernel, [block, block], links, final, wrt, lr,
                scratch=[pltpu.VMEM((GROUP, N, N), F32)], flops=3_000_000_000,
            )
            arrived = lax.ppermute(sent, "slab", cross)
            rec = arriving()
        else:
            arriving = swap_faces(slot_values[0])
            up, total, gh = call(
                plane_kernel, [field, field, field], links, *args, wb, lbt, flops=4_000_000_000
            )
            rec = arriving()
    parts, rows_u = call(
        final_kernel,
        [(6, HALF, N), rows_shape],
        links, pay, rec, state, scal, nscal, mirror, mirror_coarse, mk, vert, restrict_t,
        geometry=geometry, flops=80_000_000_000,
    )
    far_parts = lax.ppermute(parts, "slab", cross)
    (out_u,) = call(iterate_kernel, [(BLOCK, N, N)], links, up, rows_u, mask, flops=4_000_000_000)
    deep = restrict_vertical.shape[0]
    share = COARSE * COARSE // 4
    (blocks,) = call(
        vertical_kernel, [(32, deep, N)],
        links, kept.reshape(HALF * 32, N), arrived.reshape(HALF * 32, N), vertical, flops=1000, moved=1000,
    )
    (flat,) = call(
        coarse_kernel,
        [(deep, 1, share)],
        links, blocks, parts, far_parts, profile, profile_rows, vertical,
        scratch=[pltpu.VMEM((32, deep, N), F32), pltpu.VMEM((6, deep, N), F32)],
        flops=20_000_000_000,
    )
    return out_u.reshape(1, BLOCK, N * N), flat.transpose(1, 0, 2)


def solution(mesh):
    in_specs = (
        P("patch", "slab", None),
        P("patch", "slab", None),
        P("patch", None),
        P(), P(), P(), P(), P(), P(), P(), P(), P(), P(),
        P("patch", None),
    )
    out_specs = (P("patch", "slab", None), P("patch", None, "slab"))
    return jax.shard_map(
        per_device, mesh=mesh, in_specs=in_specs, out_specs=out_specs, check_vma=False
    )
```
